32 devices in a mesh: ctx: 16 (over z, y, core), tp: 2 (over x).
Axes of the slice: x: 2, y: 2, z: 4, core: 2. Of those that a mesh axis runs over, the one named last changes fastest.
Arguments:
- hidden_in: bfloat16 [2, 3072, 5120], P(None, 'ctx', 'tp'), may hold values from -24 to 24
- w_q: bfloat16 [5120, 3072], P(None, 'tp'), may hold values from -0.078125 to 0.078125
- w_k: bfloat16 [5120, 3072], P(None, 'tp'), may hold values from -0.078125 to 0.078125
- w_v: bfloat16 [5120, 3072], P(None, 'tp'), may hold values from -0.078125 to 0.078125
- event_pos: int32 [2, 3072], P(None, 'ctx'), may hold values from 0 to 3071, as said below
Outputs:
- attention_out: bfloat16 [2, 3072, 3072], P(None, 'ctx', 'tp')
The draws below stay inside these ranges and needn't reach their ends.
Inputs may be any that keep to these rules, and one draw needn't show every extreme that they name: `event_pos`: for each sequence the rows d * 2 * 96 to d * 2 * 96 + 2 * 96 - 1 hold span c_d in order and then span 3072 / 96 - 1 - c_d in order, where span c covers positions c * 96 to c * 96 + 95 and c_d runs over a permutation, drawn for each sequence, of the first 16 spans; every position occurs once.
All inputs are finite; a program needn't handle non-finite values.
Results may differ from the reference program's by a relative error of at most 0.0075.
The reference program's roundings to bfloat16 on the way count: a program that leaves them out, or rounds other values in their place, can miss the bound.
Values may be sent and summed in bfloat16 or wider, within the bound.
No kernel may reach another device: no remote copies, remote signals or barrier semaphores. Data moves between devices by JAX's collectives and lax.ppermute only.
A program may use at most 192 MiB of HBM per device.

```python
import math
import jax
import jax.numpy as jnp
from jax import lax

D = 5120
HEADS = 24
HD = 128
SEQS = 2
CH = 96
LEN = 3072
FEATS = 3072


def draw_hidden_in(key, part):
    key_vals, key_scales = jax.random.split(key)
    values = jnp.clip(jax.random.normal(key_vals, (SEQS, LEN, D), jnp.float32), -4.0, 4.0)
    scales = jnp.exp(jax.random.uniform(key_scales, (SEQS, LEN, 1), jnp.float32, 0.0, math.log(3.0)))
    return (values * scales).astype(jnp.bfloat16)


def draw_event_pos(key, part):
    spans = LEN // (2 * CH)
    offsets = jnp.arange(CH, dtype=jnp.int32)
    sequences = []
    for seq_index in range(SEQS):
        order = jax.random.permutation(jax.random.fold_in(key, seq_index + 7), spans).astype(jnp.int32)
        lower = order[:, None] * CH + offsets[None, :]
        upper = (2 * spans - 1 - order)[:, None] * CH + offsets[None, :]
        sequences.append(jnp.concatenate([lower, upper], axis=1).reshape(LEN))
    return jnp.stack(sequences).astype(jnp.int32)


def block_levels(own_key, shape, pieces, smallest, largest):
    level = 1.0
    for dim, blocks in pieces:
        steps = jax.random.uniform(jax.random.fold_in(jax.random.fold_in(own_key, 6), dim), (blocks,), jnp.float32, smallest / len(pieces), largest / len(pieces))
        level = level * jnp.repeat(jnp.exp(steps), shape[dim] // blocks).reshape((-1,) + (1,) * (len(shape) - 1 - dim))
    return level


def gaussian(key, shape, width, most, cuts=(), kind=jnp.bfloat16):
    values = width * jax.random.normal(key, shape, jnp.float32)
    if cuts:
        values = values * block_levels(key, shape, cuts, -0.22, 0.18)
    return jnp.clip(values, -most, most).astype(kind)


def setup_inputs(seed: int = 0) -> dict:
    streams_of = jax.random.split(jax.random.key(seed), 6)
    hidden_in = draw_hidden_in(jax.random.fold_in(streams_of[5], 71), 0)
    w_q = gaussian(streams_of[1], (D, FEATS), D ** -0.5, 0.078125, ((1, 2),))
    w_k = gaussian(streams_of[2], (D, FEATS), D ** -0.5, 0.078125, ((1, 2),))
    w_v = gaussian(streams_of[3], (D, FEATS), D ** -0.5, 0.078125, ((1, 2),))
    event_pos = draw_event_pos(jax.random.fold_in(streams_of[5], 71), 0)
    return {"hidden_in": hidden_in, "w_q": w_q, "w_k": w_k, "w_v": w_v, "event_pos": event_pos}


def attend(pack):
    query_rows, key_rows, value_rows, positions = pack
    score_scale = 1.0 / math.sqrt(HD)
    scores = jnp.dot(query_rows, key_rows.T, preferred_element_type=jnp.float32) * score_scale
    visible = positions[None, :] <= positions[:, None]
    scores = jnp.where(visible, scores, -jnp.inf)
    row_max = lax.optimization_barrier(jnp.max(scores, axis=1, keepdims=True))
    weights = jnp.exp(scores - row_max)
    row_sum = lax.optimization_barrier(jnp.sum(weights, axis=1, keepdims=True))
    summed = jnp.dot(weights.astype(jnp.bfloat16), value_rows, preferred_element_type=jnp.float32)
    return (summed / row_sum).astype(jnp.bfloat16)

def reference(hidden_in, w_q, w_k, w_v, event_pos):
    flat_rows = hidden_in.reshape(SEQS * LEN, D)

    def project(matrix):
        result = jnp.dot(flat_rows, matrix, preferred_element_type=jnp.float32).astype(jnp.bfloat16)
        return result.reshape(SEQS, LEN, HEADS, HD).transpose(0, 2, 1, 3).reshape(SEQS * HEADS, LEN, HD)
    queries = project(w_q)
    keys = project(w_k)
    values = project(w_v)
    positions = jnp.broadcast_to(event_pos[:, None, :], (SEQS, HEADS, LEN)).reshape(SEQS * HEADS, LEN)
    result = lax.map(attend, (queries, keys, values, positions))
    return result.reshape(SEQS, HEADS, LEN, HD).transpose(0, 2, 1, 3).reshape(SEQS, LEN, HEADS * HD)
```

```python
import functools
import math

import jax
import jax.numpy as jnp
from jax import lax
from jax.experimental import pallas as pl
from jax.experimental.pallas import tpu as pltpu
from jax.sharding import PartitionSpec as P

HD = 128
LOG2_E = 1.4426950408889634
HIDDEN = -1e30


def exchange(value, axis, size, bit):
    return lax.ppermute(value, axis, [(i, i ^ bit) for i in range(size)])


def project_body(steps, parts, sequences, place, *refs):
    inputs = refs[: sequences * parts]
    weights = refs[sequences * parts : -2]
    out_ref, total = refs[-2:]
    step = pl.program_id(0)

    @pl.when(step == 0)
    def _():
        total[...] = jnp.zeros_like(total)

    for part in range(parts):

        @pl.when(step // steps == part)
        def _():
            for s in range(sequences):
                rows = inputs[s * parts + part]
                rows = rows[0] if len(rows.shape) == 3 else rows[...]
                for n, weight in enumerate(weights):
                    wide = weight.shape[1]
                    total[s, :, n * wide : (n + 1) * wide] += jnp.dot(
                        rows, weight[...], preferred_element_type=jnp.float32
                    )

    @pl.when(step == steps * parts - 1)
    def _():
        out_ref[...] = total[...].astype(out_ref.dtype)


def project(hidden_in, received, chosen, weights, tp_me, group, wide):
    rows, feats = hidden_in.shape[1:]
    parts = 1 + len(received[0])
    steps = max(1, feats // 1280)
    depth = feats // steps
    sequences = len(chosen)

    def share_map(part, i, place):
        return (0, jnp.clip(i - part * steps, 0, steps - 1))

    def own_map(s, i, place):
        return (s, 0, jnp.clip(i, 0, steps - 1))

    def weight_map(i, place):
        return ((place[0] ^ (i // steps)) * steps + i % steps, place[1])

    in_specs = []
    operands = []
    for s in chosen:
        in_specs.append(pl.BlockSpec((1, rows, depth), functools.partial(own_map, s)))
        operands.append(hidden_in)
        for part in range(1, parts):
            in_specs.append(pl.BlockSpec((rows, depth), functools.partial(share_map, part)))
            operands.append(received[s][part - 1])
    for weight in weights:
        in_specs.append(pl.BlockSpec((depth, wide), weight_map))
        operands.append(weight)
    columns = wide * len(weights)
    return pl.pallas_call(
        functools.partial(project_body, steps, parts, sequences),
        out_shape=jax.ShapeDtypeStruct((sequences, rows, columns), jnp.bfloat16),
        grid_spec=pltpu.PrefetchScalarGridSpec(
            num_scalar_prefetch=1,
            grid=(steps * parts,),
            in_specs=in_specs,
            out_specs=pl.BlockSpec((sequences, rows, columns), lambda i, place: (0, 0, 0)),
            scratch_shapes=[pltpu.VMEM((sequences, rows, columns), jnp.float32)],
        ),
        compiler_params=pltpu.CompilerParams(vmem_limit_bytes=32 * 2**20),
        cost_estimate=pl.CostEstimate(
            flops=2 * sequences * rows * feats * parts * columns,
            bytes_accessed=2 * feats * parts * (columns + sequences * rows),
            transcendentals=0,
        ),
    )(jnp.stack([tp_me, group]).astype(jnp.int32), *operands)


def attend_body(seq, ways, blocks, spans, tile, table, place, *refs):
    query_refs = refs[:ways]
    block_refs = refs[ways : ways + blocks]
    out_refs = refs[ways + blocks : 2 * ways + blocks]
    ordered, scores, highest, sums, total, offsets, sems = refs[2 * ways + blocks :]
    rows, width = out_refs[0].shape
    half = rows // 2
    heads = width // HD
    rest = blocks // ways
    me = place[0]

    def span_of(slot):
        return table[(me ^ slot) * 2 + seq]

    copies = []
    for slot in range(blocks):
        low = span_of(slot)
        for part, span in ((0, low), (1, spans - 1 - low)):
            copies.append(
                pltpu.make_async_copy(
                    block_refs[slot].at[0, pl.ds(part * half, half)],
                    ordered.at[pl.ds(pl.multiple_of(span * half, 16), half)],
                    sems.at[2 * slot + part],
                )
            )
    for copy in copies:
        copy.start()
    for copy in copies:
        copy.wait()

    per_tile = tile // half
    slope = LOG2_E / math.sqrt(HD)
    row = lax.broadcasted_iota(jnp.int32, (rows, tile), 0)
    lane = lax.broadcasted_iota(jnp.int32, (rows, tile), 1)

    def score_step(first, query_ref, t, carry):
        start = pl.multiple_of(t * tile, 128)
        visible = offsets[first:] >= start
        for h in range(heads):
            part = lax.dot_general(
                query_ref[0, first:, h * HD : (h + 1) * HD],
                ordered[pl.ds(start, tile), h * HD : (h + 1) * HD],
                (((1,), (1,)), ((), ())),
                preferred_element_type=jnp.float32,
            )
            part = jnp.where(visible, part, HIDDEN)
            scores[h, first:, pl.ds(start, tile)] = part
            top = highest[h, first:]
            for j in range(tile // 128):
                top = jnp.maximum(top, part[:, j * 128 : (j + 1) * 128])
            highest[h, first:] = top
        return carry

    def value_step(first, tops, t, carry):
        start = pl.multiple_of(t * tile, 128)
        for h in range(heads):
            part = scores[h, first:, pl.ds(start, tile)]
            weight = jnp.exp2((part - tops[h][first:]) * slope)
            added = sums[h, first:]
            for j in range(tile // 128):
                added = added + weight[:, j * 128 : (j + 1) * 128]
            sums[h, first:] = added
            total[h, first:] += jnp.dot(
                weight.astype(jnp.bfloat16),
                ordered[pl.ds(start, tile), width + h * HD : width + (h + 1) * HD],
                preferred_element_type=jnp.float32,
            )
        return carry

    for a in range(ways):
        low = span_of(a * rest)
        high = spans - 1 - low
        query_ref = query_refs[a]
        offsets[...] = jnp.where(row < half, low * half + row, high * half + row - half) - lane
        highest[...] = jnp.full_like(highest, HIDDEN)
        sums[...] = jnp.zeros_like(sums)
        total[...] = jnp.zeros_like(total)
        both = (low + per_tile) // per_tile
        upto = (high + per_tile) // per_tile
        lax.fori_loop(0, both, functools.partial(score_step, 0, query_ref), 0)
        lax.fori_loop(both, upto, functools.partial(score_step, half, query_ref), 0)
        tops = [jnp.max(highest[h], axis=1, keepdims=True) for h in range(heads)]
        lax.fori_loop(0, both, functools.partial(value_step, 0, tops), 0)
        lax.fori_loop(both, upto, functools.partial(value_step, half, tops), 0)
        for h in range(heads):
            denom = jnp.sum(sums[h], axis=1, keepdims=True)
            out_refs[a][:, h * HD : (h + 1) * HD] = (total[h] / denom).astype(jnp.bfloat16)


def attend(seq, queries, blocks, table, me):
    rows, width = queries[0].shape[1:]
    ways, count = len(queries), len(blocks)
    spans = 2 * count
    half = rows // 2
    length = count * rows
    tile = 4 * half
    heads = width // HD
    smem = pl.BlockSpec(memory_space=pltpu.SMEM)
    one = pl.BlockSpec((1, rows, width), lambda i: (seq, 0, 0))
    flops = ways * heads * (spans + 3) * half * half * HD * 4
    return pl.pallas_call(
        functools.partial(attend_body, seq, ways, count, spans, tile),
        out_shape=[jax.ShapeDtypeStruct((rows, width), jnp.bfloat16)] * ways,
        grid=(1,),
        in_specs=[smem, smem] + [one] * ways + [pl.BlockSpec(memory_space=pl.ANY)] * count,
        out_specs=[pl.BlockSpec((rows, width), lambda i: (0, 0))] * ways,
        scratch_shapes=[
            pltpu.VMEM((length, 2 * width), jnp.bfloat16),
            pltpu.VMEM((heads, rows, length), jnp.float32),
            pltpu.VMEM((heads, rows, 128), jnp.float32),
            pltpu.VMEM((heads, rows, 128), jnp.float32),
            pltpu.VMEM((heads, rows, HD), jnp.float32),
            pltpu.VMEM((rows, tile), jnp.int32),
            pltpu.SemaphoreType.DMA((2 * count,)),
        ],
        compiler_params=pltpu.CompilerParams(vmem_limit_bytes=48 * 2**20),
        cost_estimate=pl.CostEstimate(
            flops=flops,
            bytes_accessed=4 * length * width + 4 * ways * rows * width,
            transcendentals=flops // (4 * HD),
        ),
    )(table, me, *queries, *blocks)


def assemble_body(ways, sequences, place, *refs):
    out_ref = refs[-1]
    for a in range(ways):

        @pl.when(pl.program_id(0) == a)
        def _():
            for s in range(sequences):
                out_ref[s] = refs[s * ways + a][...]


def assemble(pieces, group):
    sequences, ways = len(pieces), len(pieces[0])
    rows, width = pieces[0][0].shape
    return pl.pallas_call(
        functools.partial(assemble_body, ways, sequences),
        out_shape=jax.ShapeDtypeStruct((sequences, rows, ways * width), jnp.bfloat16),
        grid_spec=pltpu.PrefetchScalarGridSpec(
            num_scalar_prefetch=1,
            grid=(ways,),
            in_specs=[pl.BlockSpec((rows, width), lambda a, place: (0, 0))] * (sequences * ways),
            out_specs=pl.BlockSpec((sequences, rows, width), lambda a, place: (0, 0, place[0] ^ a)),
        ),
        compiler_params=pltpu.CompilerParams(vmem_limit_bytes=32 * 2**20),
    )(group.reshape(1), *[piece for row in pieces for piece in row])


def on_device(ctx_size, tp_size, hidden_in, w_q, w_k, w_v, event_pos):
    sequences, rows, _ = hidden_in.shape
    features = w_q.shape[1]
    ways = math.gcd(features // HD, ctx_size)
    rest = ctx_size // ways
    width = features // ways
    ctx_me = lax.axis_index("ctx").astype(jnp.int32)
    tp_me = lax.axis_index("tp").astype(jnp.int32)
    group = ctx_me // rest

    table = lax.all_gather(event_pos[:, 0] // (rows // 2), "ctx", axis=0, tiled=True)
    received = []
    for s in range(sequences):
        shares = [hidden_in[s]]
        bit = 1
        while bit < tp_size:
            shares += [exchange(share, "tp", tp_size, bit) for share in shares]
            bit *= 2
        received.append(shares[1:])

    order = list(range(ways - 1, -1, -1))

    def swap_groups(made):
        return {
            a: (exchange(made[a], "ctx", ctx_size, a * rest) if a else made[a]) for a in made
        }

    blocks = []
    for s in range(sequences):
        made = {
            a: project(hidden_in, received, [s], [w_k, w_v], tp_me, group ^ a, width)
            for a in order
        }
        blocks.append(swap_groups(made))
    made = {
        a: project(hidden_in, received, list(range(sequences)), [w_q], tp_me, group ^ a, width)
        for a in order
    }
    queries = swap_groups(made)
    pieces = []
    for s in range(sequences):
        held = {a * rest: blocks[s][a] for a in range(ways)}
        bit = rest // 2
        while bit:
            held.update({i | bit: exchange(held[i], "ctx", ctx_size, bit) for i in list(held)})
            bit //= 2
        outs = attend(
            s,
            [queries[a] for a in range(ways)],
            [held[i] for i in range(ctx_size)],
            table,
            ctx_me.reshape(1),
        )
        back = swap_groups({a: outs[a] for a in order})
        pieces.append([back[a] for a in range(ways)])
    return assemble(pieces, group)


def solution(mesh):
    sizes = dict(mesh.shape)
    placed = (P(None, "ctx", "tp"), P(None, "tp"), P(None, "tp"), P(None, "tp"), P(None, "ctx"))
    return jax.shard_map(
        functools.partial(on_device, sizes["ctx"], sizes["tp"]),
        mesh=mesh,
        in_specs=placed,
        out_specs=P(None, "ctx", "tp"),
        check_vma=False,
    )
```

```python
import functools
import math

import jax
import jax.numpy as jnp
from jax import lax
from jax.experimental import pallas as pl
from jax.experimental.pallas import tpu as pltpu
from jax.sharding import PartitionSpec as P

HD = 128
LOG2_E = 1.4426950408889634
HIDDEN = -1e30
VMEM_LIMIT = 56 * 2**20


def exchange(value, axis, size, bit):
    return lax.ppermute(value, axis, [(i, i ^ bit) for i in range(size)])


def own_body(weights, *refs):
    hidden_ref = refs[0]
    sequences, rows, feats = hidden_ref.shape
    flat = hidden_ref[...].reshape(sequences * rows, feats)
    for weight_ref, out_ref in zip(refs[1 : 1 + weights], refs[1 + weights :]):
        result = jnp.dot(flat, weight_ref[...], preferred_element_type=jnp.float32)
        out_ref[0] = result.reshape(sequences, rows, -1)


def own_products(hidden_in, weights, place, ways):
    sequences, rows, feats = hidden_in.shape
    width = weights[0].shape[1] // ways

    def body(place, *refs):
        own_body(len(weights), *refs)

    return pl.pallas_call(
        body,
        out_shape=[jax.ShapeDtypeStruct((ways, sequences, rows, width), jnp.float32)] * len(weights),
        grid_spec=pltpu.PrefetchScalarGridSpec(
            num_scalar_prefetch=1,
            grid=(ways,),
            in_specs=[pl.BlockSpec((sequences, rows, feats), lambda g, place: (0, 0, 0))]
            + [pl.BlockSpec((feats, width), lambda g, place: (place[0], g))] * len(weights),
            out_specs=[pl.BlockSpec((1, sequences, rows, width), lambda g, place: (g, 0, 0, 0))]
            * len(weights),
        ),
        compiler_params=pltpu.CompilerParams(vmem_limit_bytes=VMEM_LIMIT),
        cost_estimate=pl.CostEstimate(
            flops=2 * sequences * rows * feats * width * ways * len(weights),
            bytes_accessed=2 * feats * width * ways * len(weights),
            transcendentals=0,
        ),
    )(place, hidden_in, *weights)


def rest_body(shares, weights, sequences, place, *refs):
    inputs = refs[: shares * sequences]
    weight_refs = refs[shares * sequences : shares * sequences + weights]
    start_refs = refs[shares * sequences + weights : shares * sequences + 2 * weights]
    out_ref = refs[shares * sequences + 2 * weights]
    totals = refs[shares * sequences + 2 * weights + 1 :]
    rows, width = out_ref.shape[2:]
    width //= weights
    step = pl.program_id(1)
    for share in range(shares):

        @pl.when(step == share)
        def _():
            flat = [inputs[s * shares + share][...] for s in range(sequences)]
            flat = flat[0] if sequences == 1 else jnp.concatenate(flat, axis=0)
            for n in range(weights):
                before = start_refs[n][0].reshape(sequences * rows, width) if share == 0 else totals[n][...]
                after = before + jnp.dot(flat, weight_refs[n][...], preferred_element_type=jnp.float32)
                if share < shares - 1:
                    totals[n][...] = after
                else:
                    after = after.astype(out_ref.dtype).reshape(sequences, rows, width)
                    out_ref[0, :, :, n * width : (n + 1) * width] = after


def rest_products(received, chosen, weights, starts, place, ways):
    shares = len(received[0])
    rows, feats = received[0][0].shape
    width = weights[0].shape[1] // ways
    sequences = len(chosen)
    first = chosen[0]
    in_specs = [pl.BlockSpec((rows, feats), lambda g, p, place: (0, 0))] * (shares * sequences)
    in_specs += [pl.BlockSpec((feats, width), lambda g, p, place: (place[0] ^ (p + 1), g))] * len(weights)
    in_specs += [
        pl.BlockSpec((1, sequences, rows, width), lambda g, p, place: (g, first // sequences, 0, 0))
    ] * len(weights)
    columns = width * len(weights)
    return pl.pallas_call(
        functools.partial(rest_body, shares, len(weights), sequences),
        out_shape=jax.ShapeDtypeStruct((ways, sequences, rows, columns), jnp.bfloat16),
        grid_spec=pltpu.PrefetchScalarGridSpec(
            num_scalar_prefetch=1,
            grid=(ways, shares),
            in_specs=in_specs,
            out_specs=pl.BlockSpec((1, sequences, rows, columns), lambda g, p, place: (g, 0, 0, 0)),
            scratch_shapes=[pltpu.VMEM((sequences * rows, width), jnp.float32)] * len(weights),
        ),
        compiler_params=pltpu.CompilerParams(vmem_limit_bytes=VMEM_LIMIT),
        cost_estimate=pl.CostEstimate(
            flops=2 * sequences * rows * feats * shares * columns * ways,
            bytes_accessed=2 * feats * shares * columns * ways,
            transcendentals=0,
        ),
    )(place, *[share for s in chosen for share in received[s]], *weights, *starts)


def attend_body(seq, ways, blocks, spans, tile, table, place, *refs):
    query_ref, blocks_ref, out_ref = refs[:3]
    ordered, scores, highest, sums, total, offsets, sems = refs[3:]
    rows, width = out_ref.shape[1:]
    half = rows // 2
    heads = width // HD
    rest = blocks // ways
    me = place[0]

    def span_of(device):
        return table[me ^ device, seq]

    copies = []
    for slot in range(blocks):
        low = span_of(slot % ways * rest + slot // ways)
        for part, span in ((0, low), (1, spans - 1 - low)):
            copies.append(
                pltpu.make_async_copy(
                    blocks_ref.at[slot, pl.ds(part * half, half)],
                    ordered.at[pl.ds(pl.multiple_of(span * half, 16), half)],
                    sems.at[2 * slot + part],
                )
            )
    for copy in copies:
        copy.start()
    for copy in copies:
        copy.wait()

    per_tile = tile // half
    slope = LOG2_E / math.sqrt(HD)
    row = lax.broadcasted_iota(jnp.int32, (rows, tile), 0)
    lane = lax.broadcasted_iota(jnp.int32, (rows, tile), 1)

    def score_step(first, a, t, carry):
        start = pl.multiple_of(t * tile, 128)
        visible = offsets[first:] >= start
        for h in range(heads):
            part = lax.dot_general(
                query_ref[a, 0, first:, h * HD : (h + 1) * HD],
                ordered[pl.ds(start, tile), h * HD : (h + 1) * HD],
                (((1,), (1,)), ((), ())),
                preferred_element_type=jnp.float32,
            )
            part = jnp.where(visible, part, HIDDEN)
            scores[h, first:, pl.ds(start, tile)] = part
            top = highest[h, first:]
            for j in range(tile // 128):
                top = jnp.maximum(top, part[:, j * 128 : (j + 1) * 128])
            highest[h, first:] = top
        return carry

    def value_step(first, tops, t, carry):
        start = pl.multiple_of(t * tile, 128)
        for h in range(heads):
            part = scores[h, first:, pl.ds(start, tile)]
            weight = jnp.exp2((part - tops[h][first:]) * slope)
            added = sums[h, first:]
            for j in range(tile // 128):
                added = added + weight[:, j * 128 : (j + 1) * 128]
            sums[h, first:] = added
            total[h, first:] += jnp.dot(
                weight.astype(jnp.bfloat16),
                ordered[pl.ds(start, tile), width + h * HD : width + (h + 1) * HD],
                preferred_element_type=jnp.float32,
            )
        return carry

    for a in range(ways):
        low = span_of(a * rest + me % rest)
        high = spans - 1 - low
        offsets[...] = jnp.where(row < half, low * half + row, high * half + row - half) - lane
        highest[...] = jnp.full_like(highest, HIDDEN)
        sums[...] = jnp.zeros_like(sums)
        total[...] = jnp.zeros_like(total)
        both = (low + per_tile) // per_tile
        upto = (high + per_tile) // per_tile
        lax.fori_loop(0, both, functools.partial(score_step, 0, a), 0)
        lax.fori_loop(both, upto, functools.partial(score_step, half, a), 0)
        tops = [jnp.max(highest[h], axis=1, keepdims=True) for h in range(heads)]
        lax.fori_loop(0, both, functools.partial(value_step, 0, tops), 0)
        lax.fori_loop(both, upto, functools.partial(value_step, half, tops), 0)
        for h in range(heads):
            denom = jnp.sum(sums[h], axis=1, keepdims=True)
            out_ref[a, :, h * HD : (h + 1) * HD] = (total[h] / denom).astype(jnp.bfloat16)


def attend(seq, queries, blocks, table, me):
    ways, _, rows, width = queries.shape
    count = blocks.shape[0]
    spans = 2 * count
    half = rows // 2
    length = count * rows
    tile = 4 * half
    heads = width // HD
    smem = pl.BlockSpec(memory_space=pltpu.SMEM)
    flops = ways * heads * (spans + 3) * half * half * HD * 4
    return pl.pallas_call(
        functools.partial(attend_body, seq, ways, count, spans, tile),
        out_shape=jax.ShapeDtypeStruct((ways, rows, width), jnp.bfloat16),
        grid=(1,),
        in_specs=[
            smem,
            smem,
            pl.BlockSpec((ways, 1, rows, width), lambda i: (0, seq, 0, 0)),
            pl.BlockSpec(memory_space=pl.ANY),
        ],
        out_specs=pl.BlockSpec((ways, rows, width), lambda i: (0, 0, 0)),
        scratch_shapes=[
            pltpu.VMEM((length, 2 * width), jnp.bfloat16),
            pltpu.VMEM((heads, rows, length), jnp.float32),
            pltpu.VMEM((heads, rows, 128), jnp.float32),
            pltpu.VMEM((heads, rows, 128), jnp.float32),
            pltpu.VMEM((heads, rows, HD), jnp.float32),
            pltpu.VMEM((rows, tile), jnp.int32),
            pltpu.SemaphoreType.DMA((2 * count,)),
        ],
        compiler_params=pltpu.CompilerParams(vmem_limit_bytes=VMEM_LIMIT),
        cost_estimate=pl.CostEstimate(
            flops=flops,
            bytes_accessed=4 * length * width + 4 * ways * rows * width,
            transcendentals=flops // (4 * HD),
        ),
    )(table, me, queries, blocks)


def assemble_body(*refs):
    out_ref = refs[-1]
    for s, ref in enumerate(refs[:-1]):
        out_ref[s] = ref[0]


def assemble(pieces):
    ways, rows, width = pieces[0].shape
    sequences = len(pieces)
    return pl.pallas_call(
        assemble_body,
        out_shape=jax.ShapeDtypeStruct((sequences, rows, ways * width), jnp.bfloat16),
        grid=(ways,),
        in_specs=[pl.BlockSpec((1, rows, width), lambda g: (g, 0, 0))] * sequences,
        out_specs=pl.BlockSpec((sequences, rows, width), lambda g: (0, 0, g)),
        compiler_params=pltpu.CompilerParams(vmem_limit_bytes=VMEM_LIMIT),
    )(*pieces)


def on_device(ctx_size, tp_size, hidden_in, w_q, w_k, w_v, event_pos):
    sequences, rows, _ = hidden_in.shape
    features = w_q.shape[1]
    ways = math.gcd(features // HD, ctx_size)
    rest = ctx_size // ways
    ctx_me = lax.axis_index("ctx").astype(jnp.int32)
    tp_me = lax.axis_index("tp").astype(jnp.int32)
    across = [[a * rest + j for a in range(ways)] for j in range(rest)]
    along = [[a * rest + j for j in range(rest)] for a in range(ways)]

    received = []
    for s in range(sequences):
        shares = [hidden_in[s]]
        bit = 1
        while bit < tp_size:
            shares += [exchange(share, "tp", tp_size, bit) for share in shares]
            bit *= 2
        received.append(shares[1:])

    table = event_pos[None, :, 0] // (rows // 2)
    bit = 1
    while bit < ctx_size:
        table = jnp.concatenate([table, exchange(table, "ctx", ctx_size, bit)], axis=0)
        bit *= 2

    def swap_groups(value):
        if ways == 1:
            return value
        return lax.all_to_all(value, "ctx", 0, 0, axis_index_groups=across, tiled=True)

    place = tp_me.reshape(1)
    start_k, start_v, start_q = own_products(hidden_in, [w_k, w_v, w_q], place, ways)
    place = jnp.concatenate([place, table.reshape(-1)])
    blocks = []
    for s in range(sequences):
        made = rest_products(received, [s], [w_k, w_v], [start_k, start_v], place, ways)
        blocks.append(swap_groups(made.reshape(ways, rows, -1)))
    made = rest_products(received, list(range(sequences)), [w_q], [start_q], place, ways)
    queries = swap_groups(made)
    pieces = []
    for s in range(sequences):
        gathered = lax.all_gather(blocks[s], "ctx", axis=0, axis_index_groups=along, tiled=True)
        outs = attend(s, queries, gathered, table, ctx_me.reshape(1))
        pieces.append(swap_groups(outs))
    return assemble(pieces)


def solution(mesh):
    sizes = dict(mesh.shape)
    placed = (P(None, "ctx", "tp"), P(None, "tp"), P(None, "tp"), P(None, "tp"), P(None, "ctx"))
    return jax.shard_map(
        functools.partial(on_device, sizes["ctx"], sizes["tp"]),
        mesh=mesh,
        in_specs=placed,
        out_specs=P(None, "ctx", "tp"),
        check_vma=False,
    )
```

```python
import functools
import math

import jax
import jax.numpy as jnp
from jax import lax
from jax.experimental import pallas as pl
from jax.experimental.pallas import tpu as pltpu
from jax.sharding import PartitionSpec as P

HD = 128
LOG2_E = 1.4426950408889634
HIDDEN = -1e30
VMEM_LIMIT = 56 * 2**20


def exchange(value, axis, size, bit):
    return lax.ppermute(value, axis, [(i, i ^ bit) for i in range(size)])


def own_body(weights, place, mine_ref, other_ref, *refs):
    flat_ref = refs[-1]
    rows = other_ref.shape[0]

    @pl.when(pl.program_id(0) == 0)
    def _():
        flat_ref[:rows] = mine_ref[0]
        flat_ref[rows:] = other_ref[...]

    for weight_ref, out_ref in zip(refs[:weights], refs[weights:-1]):
        result = jnp.dot(flat_ref[...], weight_ref[...], preferred_element_type=jnp.float32)
        out_ref[0] = result.reshape(2, rows, -1)


def own_products(hidden_in, other, weights, place, ways):
    rows, feats = other.shape
    width = weights[0].shape[1] // ways
    return pl.pallas_call(
        functools.partial(own_body, len(weights)),
        out_shape=[jax.ShapeDtypeStruct((ways, 2, rows, width), jnp.float32)] * len(weights),
        grid_spec=pltpu.PrefetchScalarGridSpec(
            num_scalar_prefetch=1,
            grid=(ways,),
            in_specs=[
                pl.BlockSpec((1, rows, feats), lambda g, place: (place[2], 0, 0)),
                pl.BlockSpec((rows, feats), lambda g, place: (0, 0)),
            ]
            + [pl.BlockSpec((feats, width), lambda g, place: (place[0], place[1] ^ g))] * len(weights),
            out_specs=[pl.BlockSpec((1, 2, rows, width), lambda g, place: (g, 0, 0, 0))] * len(weights),
            scratch_shapes=[pltpu.VMEM((2 * rows, feats), jnp.bfloat16)],
        ),
        compiler_params=pltpu.CompilerParams(vmem_limit_bytes=VMEM_LIMIT),
        cost_estimate=pl.CostEstimate(
            flops=4 * rows * feats * width * ways * len(weights),
            bytes_accessed=2 * feats * width * ways * len(weights),
            transcendentals=0,
        ),
    )(place, hidden_in, other, *weights)


def rest_body(shares, steps, weights, chunks, place, *refs):
    inputs = refs[: shares * chunks]
    weight_refs = refs[shares * chunks : shares * chunks + weights]
    start_refs = refs[shares * chunks + weights : shares * chunks + 2 * weights]
    out_refs = refs[shares * chunks + 2 * weights : shares * chunks + 2 * weights + chunks]
    totals = refs[shares * chunks + 2 * weights + chunks :]
    rows = out_refs[0].shape[0]
    width = out_refs[0].shape[1] // weights
    step = pl.program_id(0)

    @pl.when(step == 0)
    def _():
        for total, start in zip(totals, start_refs):
            total[...] = start[...].reshape(chunks * rows, width)

    for share in range(shares):

        @pl.when(step // steps == share)
        def _():
            flat = [inputs[c * shares + share][...] for c in range(chunks)]
            flat = flat[0] if chunks == 1 else jnp.concatenate(flat, axis=0)
            for total, weight in zip(totals, weight_refs):
                total[...] += jnp.dot(flat, weight[...], preferred_element_type=jnp.float32)

    @pl.when(step == shares * steps - 1)
    def _():
        for n, total in enumerate(totals):
            for c, out_ref in enumerate(out_refs):
                out_ref[:, n * width : (n + 1) * width] = total[c * rows : (c + 1) * rows].astype(
                    out_ref.dtype
                )


def rest_products(received, chosen, weights, starts, place, a, ways):
    shares = len(received[0])
    rows, feats = received[0][0].shape
    width = weights[0].shape[1] // ways
    chunks = len(chosen)
    steps = max(1, feats // 640)
    depth = feats // steps

    def share_map(share, i, place):
        return (0, jnp.clip(i - share * steps, 0, steps - 1))

    in_specs = []
    operands = []
    for c in chosen:
        for share in range(shares):
            in_specs.append(pl.BlockSpec((rows, depth), functools.partial(share_map, share)))
            operands.append(received[c][share])
    in_specs += [
        pl.BlockSpec(
            (depth, width),
            lambda i, place: ((place[0] ^ (i // steps + 1)) * steps + i % steps, place[1] ^ a),
        )
    ] * len(weights)
    in_specs += [
        pl.BlockSpec((1, chunks, rows, width), lambda i, place: (a, chosen[0] // chunks, 0, 0))
    ] * len(weights)
    columns = width * len(weights)
    return pl.pallas_call(
        functools.partial(rest_body, shares, steps, len(weights), chunks),
        out_shape=[jax.ShapeDtypeStruct((rows, columns), jnp.bfloat16)] * chunks,
        grid_spec=pltpu.PrefetchScalarGridSpec(
            num_scalar_prefetch=1,
            grid=(shares * steps,),
            in_specs=in_specs,
            out_specs=[pl.BlockSpec((rows, columns), lambda i, place: (0, 0))] * chunks,
            scratch_shapes=[pltpu.VMEM((chunks * rows, width), jnp.float32)] * len(weights),
        ),
        compiler_params=pltpu.CompilerParams(vmem_limit_bytes=VMEM_LIMIT),
        cost_estimate=pl.CostEstimate(
            flops=2 * chunks * rows * feats * shares * columns,
            bytes_accessed=2 * feats * shares * columns,
            transcendentals=0,
        ),
    )(place, *operands, *weights, *starts)


def attend_body(block, ways, offsets, spans, tile, table, place, *refs):
    count = len(offsets)
    query_refs = refs[:ways]
    block_refs = refs[ways : ways + count]
    out_refs = refs[ways + count : 2 * ways + count]
    ordered, asked, scores, highest, sums, total, position, sems = refs[2 * ways + count :]
    rows, width = out_refs[0].shape
    half = rows // 2
    heads = width // HD
    rest = count // ways
    seq = place[2]

    copies = []
    for slot, offset in enumerate(offsets):
        low = table[offset, seq]
        for part, span in ((0, low), (1, spans - 1 - low)):
            copies.append(
                pltpu.make_async_copy(
                    block_refs[slot].at[pl.ds(part * half, half)],
                    ordered.at[pl.ds(pl.multiple_of(span * half, 16), half)],
                    sems.at[2 * slot + part],
                )
            )
    for copy in copies:
        copy.start()

    from_lane = lax.broadcasted_iota(jnp.int32, (half, 128), 0) - lax.broadcasted_iota(
        jnp.int32, (half, 128), 1
    )
    for a in range(ways):
        low = table[a * rest + block, seq]
        here = slice(a * half, (a + 1) * half)
        for part, span in ((0, low), (1, spans - 1 - low)):
            asked[part, here] = query_refs[a][part * half : (part + 1) * half]
            position[part, here] = from_lane + span * half
    highest[...] = jnp.full_like(highest, HIDDEN)
    sums[...] = jnp.zeros_like(sums)
    total[...] = jnp.zeros_like(total)
    for copy in copies:
        copy.wait()

    slope = LOG2_E / math.sqrt(HD)
    middle = spans * half // 2
    for part in range(2):
        starts = range(0, middle * (part + 1), tile)
        for start in starts:
            for h in range(heads):
                found = lax.dot_general(
                    asked[part, :, h * HD : (h + 1) * HD],
                    ordered[start : start + tile, h * HD : (h + 1) * HD],
                    (((1,), (1,)), ((), ())),
                    preferred_element_type=jnp.float32,
                )
                top = highest[h]
                for j in range(tile // 128):
                    piece = found[:, j * 128 : (j + 1) * 128]
                    if start >= middle * part:
                        piece = jnp.where(position[part] >= start + j * 128, piece, HIDDEN)
                    scores[h, :, start + j * 128 : start + (j + 1) * 128] = piece
                    top = jnp.maximum(top, piece)
                highest[h] = top
        for h in range(heads):
            highest[h] = jnp.broadcast_to(
                jnp.max(highest[h], axis=1, keepdims=True), highest.shape[1:]
            )
        for start in starts:
            for h in range(heads):
                top = highest[h]
                added = sums[h]
                weights = []
                for j in range(tile // 128):
                    piece = scores[h, :, start + j * 128 : start + (j + 1) * 128]
                    piece = jnp.exp2((piece - top) * slope)
                    added = added + piece
                    weights.append(piece.astype(jnp.bfloat16))
                sums[h] = added
                total[h] += jnp.dot(
                    jnp.concatenate(weights, axis=1),
                    ordered[start : start + tile, width + h * HD : width + (h + 1) * HD],
                    preferred_element_type=jnp.float32,
                )
        for h in range(heads):
            result = total[h] / jnp.sum(sums[h], axis=1, keepdims=True)
            for a in range(ways):
                out_refs[a][part * half : (part + 1) * half, h * HD : (h + 1) * HD] = result[
                    a * half : (a + 1) * half
                ].astype(jnp.bfloat16)
        if part == 0:
            highest[...] = jnp.full_like(highest, HIDDEN)
            sums[...] = jnp.zeros_like(sums)
            total[...] = jnp.zeros_like(total)


def attend(block, queries, blocks, table, place):
    rows, width = queries[0].shape
    ways, count = len(queries), len(blocks)
    offsets = sorted(blocks)
    spans = 2 * count
    half = rows // 2
    length = count * rows
    tile = 8 * half
    heads = width // HD
    many = ways * half
    smem = pl.BlockSpec(memory_space=pltpu.SMEM)
    flops = 6 * many * heads * length * HD
    return pl.pallas_call(
        functools.partial(attend_body, block, ways, offsets, spans, tile),
        out_shape=[jax.ShapeDtypeStruct((rows, width), jnp.bfloat16)] * ways,
        grid=(1,),
        in_specs=[smem, smem]
        + [pl.BlockSpec((rows, width), lambda i: (0, 0))] * ways
        + [pl.BlockSpec(memory_space=pl.ANY)] * count,
        out_specs=[pl.BlockSpec((rows, width), lambda i: (0, 0))] * ways,
        scratch_shapes=[
            pltpu.VMEM((length, 2 * width), jnp.bfloat16),
            pltpu.VMEM((2, many, width), jnp.bfloat16),
            pltpu.VMEM((heads, many, length), jnp.float32),
            pltpu.VMEM((heads, many, 128), jnp.float32),
            pltpu.VMEM((heads, many, 128), jnp.float32),
            pltpu.VMEM((heads, many, HD), jnp.float32),
            pltpu.VMEM((2, many, 128), jnp.int32),
            pltpu.SemaphoreType.DMA((2 * count,)),
        ],
        compiler_params=pltpu.CompilerParams(vmem_limit_bytes=VMEM_LIMIT),
        cost_estimate=pl.CostEstimate(
            flops=flops,
            bytes_accessed=4 * length * width + 4 * ways * rows * width,
            transcendentals=flops // (4 * HD),
        ),
    )(table, place, *queries, *[blocks[i] for i in offsets])


def assemble_body(slots, place, *refs):
    for n in range(slots):

        @pl.when(pl.program_id(0) == n)
        def _():
            refs[-1][0] = refs[n][...]


def assemble(pieces, place):
    ways, sequences = len(pieces), len(pieces[0])
    rows, width = pieces[0][0].shape
    return pl.pallas_call(
        functools.partial(assemble_body, ways * sequences),
        out_shape=jax.ShapeDtypeStruct((sequences, rows, ways * width), jnp.bfloat16),
        grid_spec=pltpu.PrefetchScalarGridSpec(
            num_scalar_prefetch=1,
            grid=(ways * sequences,),
            in_specs=[pl.BlockSpec((rows, width), lambda n, place: (0, 0))] * (ways * sequences),
            out_specs=pl.BlockSpec(
                (1, rows, width),
                lambda n, place: (place[2] ^ (n % sequences), 0, place[1] ^ (n // sequences)),
            ),
        ),
        compiler_params=pltpu.CompilerParams(vmem_limit_bytes=VMEM_LIMIT),
    )(place, *[piece for row in pieces for piece in row])


def on_device(ctx_size, tp_size, hidden_in, w_q, w_k, w_v, event_pos):
    _, rows, _ = hidden_in.shape
    features = w_q.shape[1]
    ways = math.gcd(features // HD, ctx_size // 2)
    rest = ctx_size // ways
    ctx_me = lax.axis_index("ctx").astype(jnp.int32)
    tp_me = lax.axis_index("tp").astype(jnp.int32)
    core = ctx_me % 2
    place = jnp.stack([tp_me, ctx_me // rest, core, ctx_me])
    away = list(range(ways - 1, -1, -1))

    def over_ctx(value, offset):
        return exchange(value, "ctx", ctx_size, offset) if offset else value

    def other_shares(own):
        shares = [own]
        bit = 1
        while bit < tp_size:
            shares += [exchange(share, "tp", tp_size, bit) for share in shares]
            bit *= 2
        return shares[1:]

    mine = lax.dynamic_index_in_dim(hidden_in, core, 0, keepdims=False)
    other = over_ctx(lax.dynamic_index_in_dim(hidden_in, 1 - core, 0, keepdims=False), 1)
    received = [other_shares(mine), other_shares(other)]

    table = event_pos[None, :, 0] // (rows // 2)
    bit = 1
    while bit < ctx_size:
        table = jnp.concatenate([table, over_ctx(table, bit)], axis=0)
        bit *= 2

    start_k, start_v, start_q = own_products(hidden_in, other, [w_k, w_v, w_q], place, ways)
    place_later = jnp.concatenate([place, table.reshape(-1)])

    blocks = {}
    for b in range(2):
        for a in away:
            (made,) = rest_products(received, [b], [w_k, w_v], [start_k, start_v], place_later, a, ways)
            blocks[a * rest + b] = over_ctx(made, a * rest)
    bit = rest // 2
    while bit > 1:
        for i in list(blocks):
            blocks[i ^ bit] = over_ctx(blocks[i], bit)
        bit //= 2
    queries = [[None] * ways, [None] * ways]
    for a in away:
        made = rest_products(received, [0, 1], [w_q], [start_q], place_later, a, ways)
        for b in range(2):
            queries[b][a] = over_ctx(made[b], a * rest)
    pieces = [[None] * 2 for _ in range(ways)]
    for b in range(2):
        outs = attend(b, queries[b], blocks, table, place)
        for a in away:
            pieces[a][b] = over_ctx(outs[a], a * rest + b)
    return assemble(pieces, place)


def solution(mesh):
    sizes = dict(mesh.shape)
    placed = (P(None, "ctx", "tp"), P(None, "tp"), P(None, "tp"), P(None, "tp"), P(None, "ctx"))
    return jax.shard_map(
        functools.partial(on_device, sizes["ctx"], sizes["tp"]),
        mesh=mesh,
        in_specs=placed,
        out_specs=P(None, "ctx", "tp"),
        check_vma=False,
    )
```

```python
import functools
import math

import jax
import jax.numpy as jnp
from jax import lax
from jax.experimental import pallas as pl
from jax.experimental.pallas import tpu as pltpu
from jax.sharding import PartitionSpec as P

HD = 128
LOG2_E = 1.4426950408889634
HIDDEN = -1e30
VMEM_LIMIT = 56 * 2**20
PAD = 8


def exchange(value, axis, size, bit):
    return lax.ppermute(value, axis, [(i, i ^ bit) for i in range(size)])


def own_body(weights, place, mine_ref, other_ref, *refs):
    rows = other_ref.shape[0]
    flat = jnp.concatenate([mine_ref[0], other_ref[...]], axis=0)
    step = pl.program_id(0)
    for weight_ref, out_ref in zip(refs[:weights], refs[weights:]):
        result = jnp.dot(flat, weight_ref[...], preferred_element_type=jnp.float32)
        result = result.reshape(2, rows, -1)

        @pl.when(step == 0)
        def _():
            out_ref[...] = result

        @pl.when(step > 0)
        def _():
            out_ref[...] += result


def own_products(hidden_in, other, weights, place):
    rows, feats = other.shape
    features = weights[0].shape[1]
    steps = max(1, feats // 512)
    depth = feats // steps
    return pl.pallas_call(
        functools.partial(own_body, len(weights)),
        out_shape=[jax.ShapeDtypeStruct((2, rows, features), jnp.float32)] * len(weights),
        grid_spec=pltpu.PrefetchScalarGridSpec(
            num_scalar_prefetch=1,
            grid=(steps,),
            in_specs=[
                pl.BlockSpec((1, rows, depth), lambda i, place: (place[2], 0, i)),
                pl.BlockSpec((rows, depth), lambda i, place: (0, i)),
            ]
            + [pl.BlockSpec((depth, features), lambda i, place: (place[0] * steps + i, 0))] * len(weights),
            out_specs=[pl.BlockSpec((2, rows, features), lambda i, place: (0, 0, 0))] * len(weights),
        ),
        compiler_params=pltpu.CompilerParams(vmem_limit_bytes=VMEM_LIMIT),
        cost_estimate=pl.CostEstimate(
            flops=4 * rows * feats * features * len(weights),
            bytes_accessed=2 * feats * features * len(weights),
            transcendentals=0,
        ),
    )(place, hidden_in, other, *weights)


def rest_body(shares, steps, weights, chosen, ways, place, *refs):
    chunks = len(chosen)
    inputs = refs[: shares * chunks]
    weight_refs = refs[shares * chunks : shares * chunks + weights]
    refs = refs[shares * chunks + weights :]
    start_refs, out_refs, refs = refs[:weights], refs[weights : weights + chunks * ways], refs[weights + chunks * ways :]
    totals, earlier, sems = refs[:weights], refs[weights : 2 * weights], refs[2 * weights]
    rows = out_refs[0].shape[0]
    width = out_refs[0].shape[1] // weights
    step = pl.program_id(0)
    copies = [
        pltpu.make_async_copy(start_refs[n].at[pl.ds(chosen[0], chunks)], earlier[n], sems.at[n])
        for n in range(weights)
    ]

    @pl.when(step == 0)
    def _():
        for copy in copies:
            copy.start()

    for share in range(shares):

        @pl.when(step // steps == share)
        def _():
            flat = [inputs[c * shares + share][...] for c in range(chunks)]
            flat = flat[0] if chunks == 1 else jnp.concatenate(flat, axis=0)
            for total, weight in zip(totals, weight_refs):
                result = jnp.dot(flat, weight[...], preferred_element_type=jnp.float32)
                result = result.reshape(chunks, rows, -1)

                @pl.when(step == 0)
                def _():
                    total[...] = result

                @pl.when(step > 0)
                def _():
                    total[...] += result

    @pl.when(step == shares * steps - 1)
    def _():
        for copy in copies:
            copy.wait()
        for a in range(ways):
            columns = pl.ds(pl.multiple_of((place[1] ^ a) * width, HD), width)
            for n in range(weights):
                for c in range(chunks):
                    done = totals[n][c, :, columns] + earlier[n][c, :, columns]
                    out_refs[c * ways + a][:, n * width : (n + 1) * width] = done.astype(jnp.bfloat16)


def rest_products(received, chosen, weights, starts, place, ways):
    shares = len(received[0])
    rows, feats = received[0][0].shape
    features = weights[0].shape[1]
    width = features // ways
    chunks = len(chosen)
    steps = max(1, feats // 512)
    depth = feats // steps

    def share_map(share, i, place):
        return (0, jnp.clip(i - share * steps, 0, steps - 1))

    in_specs = []
    operands = []
    for c in chosen:
        for share in range(shares):
            in_specs.append(pl.BlockSpec((rows, depth), functools.partial(share_map, share)))
            operands.append(received[c][share])
    in_specs += [
        pl.BlockSpec(
            (depth, features),
            lambda i, place: ((place[0] ^ (i // steps + 1)) * steps + i % steps, 0),
        )
    ] * len(weights)
    in_specs += [pl.BlockSpec(memory_space=pl.ANY)] * len(weights)
    columns = width * len(weights)
    outs = pl.pallas_call(
        functools.partial(rest_body, shares, steps, len(weights), chosen, ways),
        out_shape=[jax.ShapeDtypeStruct((rows, columns), jnp.bfloat16)] * (chunks * ways),
        grid_spec=pltpu.PrefetchScalarGridSpec(
            num_scalar_prefetch=1,
            grid=(shares * steps,),
            in_specs=in_specs,
            out_specs=[pl.BlockSpec((rows, columns), lambda i, place: (0, 0))] * (chunks * ways),
            scratch_shapes=[pltpu.VMEM((chunks, rows, features), jnp.float32)] * (2 * len(weights))
            + [pltpu.SemaphoreType.DMA((len(weights),))],
        ),
        compiler_params=pltpu.CompilerParams(vmem_limit_bytes=VMEM_LIMIT),
        cost_estimate=pl.CostEstimate(
            flops=2 * chunks * rows * feats * shares * features * len(weights),
            bytes_accessed=2 * feats * shares * features * len(weights),
            transcendentals=0,
        ),
    )(place, *operands, *weights, *starts)
    return [outs[c * ways : (c + 1) * ways] for c in range(chunks)]


def attend_body(block, ways, offsets, spans, tile, table, place, *refs):
    count = len(offsets)
    query_refs = refs[:ways]
    block_refs = refs[ways : ways + count]
    out_refs = refs[ways + count : 2 * ways + count]
    ordered, asked, scores, highest, sums, total, position, sems = refs[2 * ways + count :]
    rows, width = out_refs[0].shape
    half = rows // 2
    heads = width // HD
    rest = count // ways
    seq = place[2]

    copies = []
    for slot, offset in enumerate(offsets):
        low = table[place[3] ^ offset, seq]
        for part, span in ((0, low), (1, spans - 1 - low)):
            copies.append(
                pltpu.make_async_copy(
                    block_refs[slot].at[pl.ds(part * half, half)],
                    ordered.at[pl.ds(pl.multiple_of(span * half, 16), half)],
                    sems.at[2 * slot + part],
                )
            )
    for copy in copies:
        copy.start()

    from_lane = lax.broadcasted_iota(jnp.int32, (half, 128), 0) - lax.broadcasted_iota(
        jnp.int32, (half, 128), 1
    )
    for a in range(ways):
        low = table[place[3] ^ (a * rest + block), seq]
        here = slice(a * half, (a + 1) * half)
        for part, span in ((0, low), (1, spans - 1 - low)):
            asked[part, here] = query_refs[a][part * half : (part + 1) * half]
            position[part, here] = from_lane + span * half
    highest[...] = jnp.full_like(highest, HIDDEN)
    sums[...] = jnp.zeros_like(sums)
    total[...] = jnp.zeros_like(total)
    for copy in copies:
        copy.wait()

    slope = LOG2_E / math.sqrt(HD)
    middle = spans * half // 2
    for part in range(2):
        starts = range(0, middle * (part + 1), tile)
        for start in starts:
            for h in range(heads):
                found = lax.dot_general(
                    asked[part, :, h * HD : (h + 1) * HD],
                    ordered[start : start + tile, h * HD : (h + 1) * HD],
                    (((1,), (1,)), ((), ())),
                    preferred_element_type=jnp.float32,
                )
                top = highest[h]
                for j in range(tile // 128):
                    piece = found[:, j * 128 : (j + 1) * 128]
                    if start >= middle * part:
                        piece = jnp.where(position[part] >= start + j * 128, piece, HIDDEN)
                    scores[h, :, start + j * 128 : start + (j + 1) * 128] = piece
                    top = jnp.maximum(top, piece)
                highest[h] = top
        for h in range(heads):
            highest[h] = jnp.broadcast_to(
                jnp.max(highest[h], axis=1, keepdims=True), highest.shape[1:]
            )
        for start in starts:
            for h in range(heads):
                top = highest[h]
                added = sums[h]
                weights = []
                for j in range(tile // 128):
                    piece = scores[h, :, start + j * 128 : start + (j + 1) * 128]
                    piece = jnp.exp2((piece - top) * slope)
                    added = added + piece
                    weights.append(piece.astype(jnp.bfloat16))
                sums[h] = added
                total[h] += jnp.dot(
                    jnp.concatenate(weights, axis=1),
                    ordered[start : start + tile, width + h * HD : width + (h + 1) * HD],
                    preferred_element_type=jnp.float32,
                )
        for h in range(heads):
            result = total[h] / jnp.sum(sums[h], axis=1, keepdims=True)
            for a in range(ways):
                out_refs[a][part * half : (part + 1) * half, h * HD : (h + 1) * HD] = result[
                    a * half : (a + 1) * half
                ].astype(jnp.bfloat16)
        if part == 0:
            highest[...] = jnp.full_like(highest, HIDDEN)
            sums[...] = jnp.zeros_like(sums)
            total[...] = jnp.zeros_like(total)


def attend(block, queries, blocks, table, place):
    rows, width = queries[0].shape
    ways, count = len(queries), len(blocks)
    offsets = sorted(blocks)
    spans = 2 * count
    half = rows // 2
    length = count * rows
    tile = 8 * half
    heads = width // HD
    many = ways * half
    smem = pl.BlockSpec(memory_space=pltpu.SMEM)
    flops = 6 * many * heads * length * HD
    return pl.pallas_call(
        functools.partial(attend_body, block, ways, offsets, spans, tile),
        out_shape=[jax.ShapeDtypeStruct((rows, width), jnp.bfloat16)] * ways,
        grid=(1,),
        in_specs=[smem, smem]
        + [pl.BlockSpec((rows, width), lambda i: (0, 0))] * ways
        + [pl.BlockSpec(memory_space=pl.ANY)] * count,
        out_specs=[pl.BlockSpec((rows, width), lambda i: (0, 0))] * ways,
        scratch_shapes=[
            pltpu.VMEM((length, 2 * width), jnp.bfloat16),
            pltpu.VMEM((2, many, width), jnp.bfloat16),
            pltpu.VMEM((heads, many, length), jnp.float32),
            pltpu.VMEM((heads, many, 128), jnp.float32),
            pltpu.VMEM((heads, many, 128), jnp.float32),
            pltpu.VMEM((heads, many, HD), jnp.float32),
            pltpu.VMEM((2, many, 128), jnp.int32),
            pltpu.SemaphoreType.DMA((2 * count,)),
        ],
        compiler_params=pltpu.CompilerParams(vmem_limit_bytes=VMEM_LIMIT),
        cost_estimate=pl.CostEstimate(
            flops=flops,
            bytes_accessed=4 * length * width + 4 * ways * rows * width,
            transcendentals=flops // (4 * HD),
        ),
    )(table, place, *queries, *[blocks[i] for i in offsets])


def assemble_body(ways, sequences, place, *refs):
    out_ref, sems = refs[-2:]
    width = refs[0].shape[1]
    copies = []
    for a in range(ways):
        for b in range(sequences):
            n = a * sequences + b
            columns = pl.ds(pl.multiple_of((place[1] ^ a) * width, HD), width)
            copies.append(
                pltpu.make_async_copy(refs[n], out_ref.at[place[2] ^ b, :, columns], sems.at[n])
            )
    for copy in copies:
        copy.start()
    for copy in copies:
        copy.wait()


def assemble(pieces, place):
    ways, sequences = len(pieces), len(pieces[0])
    rows, width = pieces[0][0].shape
    return pl.pallas_call(
        functools.partial(assemble_body, ways, sequences),
        out_shape=jax.ShapeDtypeStruct((sequences, rows, ways * width), jnp.bfloat16),
        in_specs=[pl.BlockSpec(memory_space=pltpu.SMEM)]
        + [pl.BlockSpec(memory_space=pl.ANY)] * (ways * sequences),
        out_specs=pl.BlockSpec(memory_space=pl.ANY),
        scratch_shapes=[pltpu.SemaphoreType.DMA((ways * sequences,))],
    )(place, *[piece for row in pieces for piece in row])


def on_device(ctx_size, tp_size, hidden_in, w_q, w_k, w_v, event_pos):
    _, rows, _ = hidden_in.shape
    features = w_q.shape[1]
    ways = math.gcd(features // HD, ctx_size // 2)
    rest = ctx_size // ways
    ctx_me = lax.axis_index("ctx").astype(jnp.int32)
    tp_me = lax.axis_index("tp").astype(jnp.int32)
    core = ctx_me % 2
    place = jnp.stack([tp_me, ctx_me // rest, core, ctx_me])
    away = list(range(ways - 1, -1, -1))

    def over_ctx(value, offset):
        return exchange(value, "ctx", ctx_size, offset) if offset else value

    def other_shares(own):
        shares = [own]
        bit = 1
        while bit < tp_size:
            shares += [exchange(share, "tp", tp_size, bit) for share in shares]
            bit *= 2
        return shares[1:]

    mine = lax.dynamic_index_in_dim(hidden_in, core, 0, keepdims=False)
    other = over_ctx(lax.dynamic_index_in_dim(hidden_in, 1 - core, 0, keepdims=False), 1)
    received = [other_shares(mine), other_shares(other)]

    firsts = jnp.broadcast_to((event_pos[:, 0] // (rows // 2))[None, :, None, None], (1, 2, PAD, 128))
    firsts = lax.optimization_barrier(lax.all_gather(lax.optimization_barrier(firsts), "ctx", axis=0, tiled=True))
    table = firsts[:, :, 0, 0]

    start_k, start_v, start_q = own_products(hidden_in, other, [w_k, w_v, w_q], place)

    blocks = {}
    for b in range(2):
        (made,) = rest_products(received, [b], [w_k, w_v], [start_k, start_v], place, ways)
        for a in away:
            blocks[a * rest + b] = over_ctx(made[a], a * rest)
    bit = rest // 2
    while bit > 1:
        for i in list(blocks):
            blocks[i ^ bit] = over_ctx(blocks[i], bit)
        bit //= 2
    queries = [[None] * ways, [None] * ways]
    made = rest_products(received, [0, 1], [w_q], [start_q], place, ways)
    for b in range(2):
        for a in away:
            queries[b][a] = over_ctx(made[b][a], a * rest)
    pieces = [[None] * 2 for _ in range(ways)]
    for b in range(2):
        outs = attend(b, queries[b], blocks, table, place)
        for a in away:
            pieces[a][b] = over_ctx(outs[a], a * rest + b)
    return assemble(pieces, place)


def solution(mesh):
    sizes = dict(mesh.shape)
    placed = (P(None, "ctx", "tp"), P(None, "tp"), P(None, "tp"), P(None, "tp"), P(None, "ctx"))
    return jax.shard_map(
        functools.partial(on_device, sizes["ctx"], sizes["tp"]),
        mesh=mesh,
        in_specs=placed,
        out_specs=P(None, "ctx", "tp"),
        check_vma=False,
    )
```

```python
import functools
import math

import jax
import jax.numpy as jnp
from jax import lax
from jax.experimental import pallas as pl
from jax.experimental.pallas import tpu as pltpu
from jax.sharding import PartitionSpec as P

HD = 128
LOG2_E = 1.4426950408889634
HIDDEN = -1e30
VMEM_LIMIT = 56 * 2**20


def exchange(value, axis, size, bit):
    return lax.ppermute(value, axis, [(i, i ^ bit) for i in range(size)])


def own_body(weights, place, mine_ref, other_ref, *refs):
    flat_ref = refs[-1]
    rows = other_ref.shape[0]

    @pl.when(pl.program_id(0) == 0)
    def _():
        flat_ref[:rows] = mine_ref[0]
        flat_ref[rows:] = other_ref[...]

    for weight_ref, out_ref in zip(refs[:weights], refs[weights:-1]):
        result = jnp.dot(flat_ref[...], weight_ref[...], preferred_element_type=jnp.float32)
        out_ref[...] = result.reshape(2, rows, -1)


def own_products(hidden_in, other, weights, place, ways):
    rows, feats = other.shape
    features = weights[0].shape[1]
    width = features // ways
    return pl.pallas_call(
        functools.partial(own_body, len(weights)),
        out_shape=[jax.ShapeDtypeStruct((2, rows, features), jnp.float32)] * len(weights),
        grid_spec=pltpu.PrefetchScalarGridSpec(
            num_scalar_prefetch=1,
            grid=(ways,),
            in_specs=[
                pl.BlockSpec((1, rows, feats), lambda g, place: (place[2], 0, 0)),
                pl.BlockSpec((rows, feats), lambda g, place: (0, 0)),
            ]
            + [pl.BlockSpec((feats, width), lambda g, place: (place[0], g))] * len(weights),
            out_specs=[pl.BlockSpec((2, rows, width), lambda g, place: (0, 0, g))] * len(weights),
            scratch_shapes=[pltpu.VMEM((2 * rows, feats), jnp.bfloat16)],
        ),
        compiler_params=pltpu.CompilerParams(vmem_limit_bytes=VMEM_LIMIT),
        cost_estimate=pl.CostEstimate(
            flops=4 * rows * feats * features * len(weights),
            bytes_accessed=2 * feats * features * len(weights),
            transcendentals=0,
        ),
    )(place, hidden_in, other, *weights)


def rest_body(shares, weights, chunks, away, place, *refs):
    inputs = refs[: shares * chunks]
    refs = refs[shares * chunks :]
    weight_refs, refs = refs[: weights * shares], refs[weights * shares :]
    start_refs, refs = refs[:weights], refs[weights:]
    out_refs, flats = refs[: chunks * len(away)], refs[chunks * len(away) :]
    rows, width = out_refs[0].shape
    width //= weights
    step = pl.program_id(0)
    if chunks > 1:

        @pl.when(step == 0)
        def _():
            for share in range(shares):
                for c in range(chunks):
                    flats[share][c * rows : (c + 1) * rows] = inputs[c * shares + share][...]

    else:
        flats = inputs
    made = []
    for n in range(weights):
        total = start_refs[n][...].reshape(chunks * rows, width)
        for share in range(shares):
            total += jnp.dot(
                flats[share][...], weight_refs[n * shares + share][...], preferred_element_type=jnp.float32
            )
        made.append(total.astype(jnp.bfloat16))
    for index in range(len(away)):

        @pl.when(step == index)
        def _():
            for c in range(chunks):
                for n in range(weights):
                    out_refs[c * len(away) + index][:, n * width : (n + 1) * width] = made[n][
                        c * rows : (c + 1) * rows
                    ]


def rest_products(received, chosen, weights, starts, place, ways, away):
    shares = len(received[0])
    rows, feats = received[0][0].shape
    width = weights[0].shape[1] // ways
    chunks = len(chosen)
    top = away[0]

    def weight_map(share, i, place):
        return (place[0] ^ (share + 1), place[1] ^ (top - i))

    in_specs = [pl.BlockSpec((rows, feats), lambda i, place: (0, 0))] * (shares * chunks)
    for _ in weights:
        for share in range(shares):
            in_specs.append(pl.BlockSpec((feats, width), functools.partial(weight_map, share)))
    in_specs += [
        pl.BlockSpec((chunks, rows, width), lambda i, place: (chosen[0] // chunks, 0, place[1] ^ (top - i)))
    ] * len(weights)
    columns = width * len(weights)
    scratch = [pltpu.VMEM((chunks * rows, feats), jnp.bfloat16)] * (shares if chunks > 1 else 0)
    outs = pl.pallas_call(
        functools.partial(rest_body, shares, len(weights), chunks, away),
        out_shape=[jax.ShapeDtypeStruct((rows, columns), jnp.bfloat16)] * (chunks * len(away)),
        grid_spec=pltpu.PrefetchScalarGridSpec(
            num_scalar_prefetch=1,
            grid=(len(away),),
            in_specs=in_specs,
            out_specs=[pl.BlockSpec((rows, columns), lambda i, place: (0, 0))] * (chunks * len(away)),
            scratch_shapes=scratch,
        ),
        compiler_params=pltpu.CompilerParams(vmem_limit_bytes=VMEM_LIMIT),
        cost_estimate=pl.CostEstimate(
            flops=2 * chunks * rows * feats * shares * columns * len(away),
            bytes_accessed=2 * feats * shares * columns * len(away),
            transcendentals=0,
        ),
    )(
        place,
        *[share for c in chosen for share in received[c]],
        *[weight for weight in weights for _ in range(shares)],
        *starts,
    )
    return [dict(zip(away, outs[c * len(away) : (c + 1) * len(away)])) for c in range(chunks)]


def attend_body(block, ways, offsets, spans, tile, table, place, *refs):
    count = len(offsets)
    query_refs = refs[:ways]
    block_refs = refs[ways : ways + count]
    out_refs = refs[ways + count : 2 * ways + count]
    ordered, asked, scores, highest, sums, total, position, sems = refs[2 * ways + count :]
    rows, width = out_refs[0].shape
    half = rows // 2
    heads = width // HD
    rest = count // ways
    seq = place[2]

    copies = []
    for slot, offset in enumerate(offsets):
        low = table[place[3] ^ offset, seq]
        for part, span in ((0, low), (1, spans - 1 - low)):
            copies.append(
                pltpu.make_async_copy(
                    block_refs[slot].at[pl.ds(part * half, half)],
                    ordered.at[pl.ds(pl.multiple_of(span * half, 16), half)],
                    sems.at[2 * slot + part],
                )
            )
    for copy in copies:
        copy.start()

    from_lane = lax.broadcasted_iota(jnp.int32, (half, 128), 0) - lax.broadcasted_iota(
        jnp.int32, (half, 128), 1
    )
    for a in range(ways):
        low = table[place[3] ^ (a * rest + block), seq]
        here = slice(a * half, (a + 1) * half)
        for part, span in ((0, low), (1, spans - 1 - low)):
            asked[part, here] = query_refs[a][part * half : (part + 1) * half]
            position[part, here] = from_lane + span * half
    highest[...] = jnp.full_like(highest, HIDDEN)
    sums[...] = jnp.zeros_like(sums)
    total[...] = jnp.zeros_like(total)
    for copy in copies:
        copy.wait()

    slope = LOG2_E / math.sqrt(HD)
    middle = spans * half // 2
    for part in range(2):
        starts = range(0, middle * (part + 1), tile)
        for start in starts:
            for h in range(heads):
                found = lax.dot_general(
                    asked[part, :, h * HD : (h + 1) * HD],
                    ordered[start : start + tile, h * HD : (h + 1) * HD],
                    (((1,), (1,)), ((), ())),
                    preferred_element_type=jnp.float32,
                )
                top = highest[h]
                for j in range(tile // 128):
                    piece = found[:, j * 128 : (j + 1) * 128]
                    if start >= middle * part:
                        piece = jnp.where(position[part] >= start + j * 128, piece, HIDDEN)
                    scores[h, :, start + j * 128 : start + (j + 1) * 128] = piece
                    top = jnp.maximum(top, piece)
                highest[h] = top
        for h in range(heads):
            highest[h] = jnp.broadcast_to(
                jnp.max(highest[h], axis=1, keepdims=True), highest.shape[1:]
            )
        for start in starts:
            for h in range(heads):
                top = highest[h]
                added = sums[h]
                weights = []
                for j in range(tile // 128):
                    piece = scores[h, :, start + j * 128 : start + (j + 1) * 128]
                    piece = jnp.exp2((piece - top) * slope)
                    added = added + piece
                    weights.append(piece.astype(jnp.bfloat16))
                sums[h] = added
                total[h] += jnp.dot(
                    jnp.concatenate(weights, axis=1),
                    ordered[start : start + tile, width + h * HD : width + (h + 1) * HD],
                    preferred_element_type=jnp.float32,
                )
        for h in range(heads):
            result = total[h] / jnp.sum(sums[h], axis=1, keepdims=True)
            for a in range(ways):
                out_refs[a][part * half : (part + 1) * half, h * HD : (h + 1) * HD] = result[
                    a * half : (a + 1) * half
                ].astype(jnp.bfloat16)
        if part == 0:
            highest[...] = jnp.full_like(highest, HIDDEN)
            sums[...] = jnp.zeros_like(sums)
            total[...] = jnp.zeros_like(total)


def attend(block, queries, blocks, table, place):
    rows, width = queries[0].shape
    ways, count = len(queries), len(blocks)
    offsets = sorted(blocks)
    spans = 2 * count
    half = rows // 2
    length = count * rows
    tile = 8 * half
    heads = width // HD
    many = ways * half
    smem = pl.BlockSpec(memory_space=pltpu.SMEM)
    flops = 6 * many * heads * length * HD
    return pl.pallas_call(
        functools.partial(attend_body, block, ways, offsets, spans, tile),
        out_shape=[jax.ShapeDtypeStruct((rows, width), jnp.bfloat16)] * ways,
        grid=(1,),
        in_specs=[smem, smem]
        + [pl.BlockSpec((rows, width), lambda i: (0, 0))] * ways
        + [pl.BlockSpec(memory_space=pl.ANY)] * count,
        out_specs=[pl.BlockSpec((rows, width), lambda i: (0, 0))] * ways,
        scratch_shapes=[
            pltpu.VMEM((length, 2 * width), jnp.bfloat16),
            pltpu.VMEM((2, many, width), jnp.bfloat16),
            pltpu.VMEM((heads, many, length), jnp.float32),
            pltpu.VMEM((heads, many, 128), jnp.float32),
            pltpu.VMEM((heads, many, 128), jnp.float32),
            pltpu.VMEM((heads, many, HD), jnp.float32),
            pltpu.VMEM((2, many, 128), jnp.int32),
            pltpu.SemaphoreType.DMA((2 * count,)),
        ],
        compiler_params=pltpu.CompilerParams(vmem_limit_bytes=VMEM_LIMIT),
        cost_estimate=pl.CostEstimate(
            flops=flops,
            bytes_accessed=4 * length * width + 4 * ways * rows * width,
            transcendentals=flops // (4 * HD),
        ),
    )(table, place, *queries, *[blocks[i] for i in offsets])


def assemble_body(ways, sequences, place, *refs):
    out_ref = refs[-1]
    for a in range(ways):

        @pl.when(pl.program_id(0) == a)
        def _():
            for b in range(sequences):
                out_ref[place[2] ^ b] = refs[a * sequences + b][...]


def assemble(pieces, place):
    ways, sequences = len(pieces), len(pieces[0])
    rows, width = pieces[0][0].shape
    return pl.pallas_call(
        functools.partial(assemble_body, ways, sequences),
        out_shape=jax.ShapeDtypeStruct((sequences, rows, ways * width), jnp.bfloat16),
        grid_spec=pltpu.PrefetchScalarGridSpec(
            num_scalar_prefetch=1,
            grid=(ways,),
            in_specs=[pl.BlockSpec((rows, width), lambda a, place: (0, 0))] * (ways * sequences),
            out_specs=pl.BlockSpec((sequences, rows, width), lambda a, place: (0, 0, place[1] ^ a)),
        ),
        compiler_params=pltpu.CompilerParams(vmem_limit_bytes=VMEM_LIMIT),
    )(place, *[piece for row in pieces for piece in row])


def on_device(ctx_size, tp_size, hidden_in, w_q, w_k, w_v, event_pos):
    _, rows, _ = hidden_in.shape
    features = w_q.shape[1]
    ways = math.gcd(features // HD, ctx_size // 2)
    rest = ctx_size // ways
    ctx_me = lax.axis_index("ctx").astype(jnp.int32)
    tp_me = lax.axis_index("tp").astype(jnp.int32)
    core = ctx_me % 2
    place = jnp.stack([tp_me, ctx_me // rest, core, ctx_me])
    away = list(range(ways - 1, -1, -1))

    def over_ctx(value, offset):
        return exchange(value, "ctx", ctx_size, offset) if offset else value

    def other_shares(own):
        shares = [own]
        bit = 1
        while bit < tp_size:
            shares += [exchange(share, "tp", tp_size, bit) for share in shares]
            bit *= 2
        return shares[1:]

    mine = lax.dynamic_index_in_dim(hidden_in, core, 0, keepdims=False)
    other = over_ctx(lax.dynamic_index_in_dim(hidden_in, 1 - core, 0, keepdims=False), 1)
    received = [other_shares(mine), other_shares(other)]

    firsts = jnp.broadcast_to((event_pos[:, 0] // (rows // 2))[None], (ctx_size, 2))
    table = lax.all_to_all(firsts, "ctx", 0, 0, tiled=True)

    start_k, start_v, start_q = own_products(hidden_in, other, [w_k, w_v, w_q], place, ways)

    later = jnp.concatenate([place, table.reshape(-1)])
    (made_0,) = rest_products(received, [0], [w_k, w_v], [start_k, start_v], later, ways, away)
    (made_1,) = rest_products(received, [1], [w_k, w_v], [start_k, start_v], place, ways, away)
    received, made_1 = lax.optimization_barrier((received, made_1))
    asked = rest_products(received, [0, 1], [w_q], [start_q], place, ways, away)
    first = {a: over_ctx(made_0[a], a * rest) for a in away}
    for a in away:
        first[a], asked[0][a] = lax.optimization_barrier((first[a], asked[0][a]))
    blocks = {a * rest: first[a] for a in away}
    queries = [{}, {}]
    for a in away:
        last = first[a]
        for made, keep, key in ((made_1, blocks, a * rest + 1), (asked[0], queries[0], a), (asked[1], queries[1], a)):
            value, last = lax.optimization_barrier((made[a], last))
            last = keep[key] = over_ctx(value, a * rest)
    bit = rest // 2
    while bit > 1:
        for i in list(blocks):
            blocks[i ^ bit] = over_ctx(blocks[i], bit)
        bit //= 2
    pieces = [[None] * 2 for _ in range(ways)]
    for b in range(2):
        outs = attend(b, [queries[b][a] for a in range(ways)], blocks, table, place)
        for a in away:
            pieces[a][b] = over_ctx(outs[a], a * rest + b)
    return assemble(pieces, place)


def solution(mesh):
    sizes = dict(mesh.shape)
    placed = (P(None, "ctx", "tp"), P(None, "tp"), P(None, "tp"), P(None, "tp"), P(None, "ctx"))
    return jax.shard_map(
        functools.partial(on_device, sizes["ctx"], sizes["tp"]),
        mesh=mesh,
        in_specs=placed,
        out_specs=P(None, "ctx", "tp"),
        check_vma=False,
    )
```

```python
import functools
import math

import jax
import jax.numpy as jnp
from jax import lax
from jax.experimental import pallas as pl
from jax.experimental.pallas import tpu as pltpu
from jax.sharding import PartitionSpec as P

HD = 128
LOG2_E = 1.4426950408889634
HIDDEN = -1e30
VMEM_LIMIT = 56 * 2**20


def exchange(value, axis, size, bit):
    return lax.ppermute(value, axis, [(i, i ^ bit) for i in range(size)])


EXTRA = 16


def own_body(weights, place, mine_ref, other_ref, *refs):
    flat_ref = refs[-1]
    rows = other_ref.shape[0]

    @pl.when(pl.program_id(0) == 0)
    def _():
        flat_ref[:rows] = mine_ref[0]
        flat_ref[rows:] = other_ref[...]

    for weight_ref, out_ref in zip(refs[:weights], refs[weights:-1]):
        result = jnp.dot(flat_ref[...], weight_ref[...], preferred_element_type=jnp.float32)
        out_ref[...] = result.reshape(2, rows, -1)


def own_products(hidden_in, other, weights, place, ways):
    rows, feats = other.shape
    features = weights[0].shape[1]
    width = features // ways
    return pl.pallas_call(
        functools.partial(own_body, len(weights)),
        out_shape=[jax.ShapeDtypeStruct((2, rows, features), jnp.float32)] * len(weights),
        grid_spec=pltpu.PrefetchScalarGridSpec(
            num_scalar_prefetch=1,
            grid=(ways,),
            in_specs=[
                pl.BlockSpec((1, rows, feats), lambda g, place: (place[2], 0, 0)),
                pl.BlockSpec((rows, feats), lambda g, place: (0, 0)),
            ]
            + [pl.BlockSpec((feats, width), lambda g, place: (place[0], g))] * len(weights),
            out_specs=[pl.BlockSpec((2, rows, width), lambda g, place: (0, 0, g))] * len(weights),
            scratch_shapes=[pltpu.VMEM((2 * rows, feats), jnp.bfloat16)],
        ),
        compiler_params=pltpu.CompilerParams(vmem_limit_bytes=VMEM_LIMIT),
        cost_estimate=pl.CostEstimate(
            flops=4 * rows * feats * features * len(weights),
            bytes_accessed=2 * feats * features * len(weights),
            transcendentals=0,
        ),
    )(place, hidden_in, other, *weights)


def rest_body(shares, weights, chunks, away, extra, place, *refs):
    inputs = refs[: shares * chunks]
    refs = refs[shares * chunks :]
    weight_refs, refs = refs[: weights * shares], refs[weights * shares :]
    start_refs, refs = refs[:weights], refs[weights:]
    out_refs, flats = refs[: chunks * len(away)], refs[chunks * len(away) :]
    rows, width = out_refs[0].shape
    rows -= extra
    width //= weights
    step = pl.program_id(0)
    if chunks > 1:

        @pl.when(step == 0)
        def _():
            for share in range(shares):
                for c in range(chunks):
                    flats[share][c * rows : (c + 1) * rows] = inputs[c * shares + share][...]

    else:
        flats = inputs
    made = []
    for n in range(weights):
        total = start_refs[n][...].reshape(chunks * rows, width)
        for share in range(shares):
            total += jnp.dot(
                flats[share][...], weight_refs[n * shares + share][...], preferred_element_type=jnp.float32
            )
        made.append(total.astype(jnp.bfloat16))
    for index in range(len(away)):

        @pl.when(step == index)
        def _():
            for c in range(chunks):
                for n in range(weights):
                    out_refs[c * len(away) + index][:rows, n * width : (n + 1) * width] = made[n][
                        c * rows : (c + 1) * rows
                    ]
            if extra:
                line = lax.broadcasted_iota(jnp.int32, (extra, weights * width), 0)
                spans = jnp.where(line < extra // 2, place[4], place[5]).astype(jnp.float32)
                out_refs[index][rows:] = spans.astype(jnp.bfloat16)


def rest_products(received, chosen, weights, starts, place, ways, away, extra=0):
    shares = len(received[0])
    rows, feats = received[0][0].shape
    width = weights[0].shape[1] // ways
    chunks = len(chosen)
    top = away[0]

    def weight_map(share, i, place):
        return (place[0] ^ (share + 1), place[1] ^ (top - i))

    in_specs = [pl.BlockSpec((rows, feats), lambda i, place: (0, 0))] * (shares * chunks)
    for _ in weights:
        for share in range(shares):
            in_specs.append(pl.BlockSpec((feats, width), functools.partial(weight_map, share)))
    in_specs += [
        pl.BlockSpec((chunks, rows, width), lambda i, place: (chosen[0] // chunks, 0, place[1] ^ (top - i)))
    ] * len(weights)
    columns = width * len(weights)
    scratch = [pltpu.VMEM((chunks * rows, feats), jnp.bfloat16)] * (shares if chunks > 1 else 0)
    outs = pl.pallas_call(
        functools.partial(rest_body, shares, len(weights), chunks, away, extra),
        out_shape=[jax.ShapeDtypeStruct((rows + extra, columns), jnp.bfloat16)] * (chunks * len(away)),
        grid_spec=pltpu.PrefetchScalarGridSpec(
            num_scalar_prefetch=1,
            grid=(len(away),),
            in_specs=in_specs,
            out_specs=[pl.BlockSpec((rows + extra, columns), lambda i, place: (0, 0))] * (chunks * len(away)),
            scratch_shapes=scratch,
        ),
        compiler_params=pltpu.CompilerParams(vmem_limit_bytes=VMEM_LIMIT),
        cost_estimate=pl.CostEstimate(
            flops=2 * chunks * rows * feats * shares * columns * len(away),
            bytes_accessed=2 * feats * shares * columns * len(away),
            transcendentals=0,
        ),
    )(
        place,
        *[share for c in chosen for share in received[c]],
        *[weight for weight in weights for _ in range(shares)],
        *starts,
    )
    return [dict(zip(away, outs[c * len(away) : (c + 1) * len(away)])) for c in range(chunks)]


def attend_body(block, ways, offsets, spans, tile, table, *refs):
    count = len(offsets)
    query_refs = refs[:ways]
    block_refs = refs[ways : ways + count]
    out_refs = refs[ways + count : 2 * ways + count]
    ordered, asked, scores, highest, sums, total, position, sems = refs[2 * ways + count :]
    rows, width = out_refs[0].shape
    half = rows // 2
    heads = width // HD
    rest = count // ways

    copies = []
    for slot, offset in enumerate(offsets):
        low = table[offset]
        for part, span in ((0, low), (1, spans - 1 - low)):
            copies.append(
                pltpu.make_async_copy(
                    block_refs[slot].at[pl.ds(part * half, half)],
                    ordered.at[pl.ds(pl.multiple_of(span * half, 16), half)],
                    sems.at[2 * slot + part],
                )
            )
    for copy in copies:
        copy.start()

    from_lane = lax.broadcasted_iota(jnp.int32, (half, 128), 0) - lax.broadcasted_iota(
        jnp.int32, (half, 128), 1
    )
    for a in range(ways):
        low = table[a * rest + block]
        here = slice(a * half, (a + 1) * half)
        for part, span in ((0, low), (1, spans - 1 - low)):
            asked[part, here] = query_refs[a][part * half : (part + 1) * half]
            position[part, here] = from_lane + span * half
    highest[...] = jnp.full_like(highest, HIDDEN)
    sums[...] = jnp.zeros_like(sums)
    total[...] = jnp.zeros_like(total)
    for copy in copies:
        copy.wait()

    slope = LOG2_E / math.sqrt(HD)
    middle = spans * half // 2
    for part in range(2):
        starts = range(0, middle * (part + 1), tile)
        for start in starts:
            for h in range(heads):
                found = lax.dot_general(
                    asked[part, :, h * HD : (h + 1) * HD],
                    ordered[start : start + tile, h * HD : (h + 1) * HD],
                    (((1,), (1,)), ((), ())),
                    preferred_element_type=jnp.float32,
                )
                top = highest[h]
                for j in range(tile // 128):
                    piece = found[:, j * 128 : (j + 1) * 128]
                    if start >= middle * part:
                        piece = jnp.where(position[part] >= start + j * 128, piece, HIDDEN)
                    scores[h, :, start + j * 128 : start + (j + 1) * 128] = piece
                    top = jnp.maximum(top, piece)
                highest[h] = top
        for h in range(heads):
            highest[h] = jnp.broadcast_to(
                jnp.max(highest[h], axis=1, keepdims=True), highest.shape[1:]
            )
        for start in starts:
            for h in range(heads):
                top = highest[h]
                added = sums[h]
                weights = []
                for j in range(tile // 128):
                    piece = scores[h, :, start + j * 128 : start + (j + 1) * 128]
                    piece = jnp.exp2((piece - top) * slope)
                    added = added + piece
                    weights.append(piece.astype(jnp.bfloat16))
                sums[h] = added
                total[h] += jnp.dot(
                    jnp.concatenate(weights, axis=1),
                    ordered[start : start + tile, width + h * HD : width + (h + 1) * HD],
                    preferred_element_type=jnp.float32,
                )
        for h in range(heads):
            result = total[h] / jnp.sum(sums[h], axis=1, keepdims=True)
            for a in range(ways):
                out_refs[a][part * half : (part + 1) * half, h * HD : (h + 1) * HD] = result[
                    a * half : (a + 1) * half
                ].astype(jnp.bfloat16)
        if part == 0:
            highest[...] = jnp.full_like(highest, HIDDEN)
            sums[...] = jnp.zeros_like(sums)
            total[...] = jnp.zeros_like(total)


def attend(block, queries, blocks, table):
    rows, width = queries[0].shape
    ways, count = len(queries), len(blocks)
    offsets = sorted(blocks)
    spans = 2 * count
    half = rows // 2
    length = count * rows
    tile = 8 * half
    heads = width // HD
    many = ways * half
    smem = pl.BlockSpec(memory_space=pltpu.SMEM)
    flops = 6 * many * heads * length * HD
    return pl.pallas_call(
        functools.partial(attend_body, block, ways, offsets, spans, tile),
        out_shape=[jax.ShapeDtypeStruct((rows, width), jnp.bfloat16)] * ways,
        grid=(1,),
        in_specs=[smem]
        + [pl.BlockSpec((rows, width), lambda i: (0, 0))] * ways
        + [pl.BlockSpec(memory_space=pl.ANY)] * count,
        out_specs=[pl.BlockSpec((rows, width), lambda i: (0, 0))] * ways,
        scratch_shapes=[
            pltpu.VMEM((length, 2 * width), jnp.bfloat16),
            pltpu.VMEM((2, many, width), jnp.bfloat16),
            pltpu.VMEM((heads, many, length), jnp.float32),
            pltpu.VMEM((heads, many, 128), jnp.float32),
            pltpu.VMEM((heads, many, 128), jnp.float32),
            pltpu.VMEM((heads, many, HD), jnp.float32),
            pltpu.VMEM((2, many, 128), jnp.int32),
            pltpu.SemaphoreType.DMA((2 * count,)),
        ],
        compiler_params=pltpu.CompilerParams(vmem_limit_bytes=VMEM_LIMIT),
        cost_estimate=pl.CostEstimate(
            flops=flops,
            bytes_accessed=4 * length * width + 4 * ways * rows * width,
            transcendentals=flops // (4 * HD),
        ),
    )(table, *queries, *[blocks[i] for i in offsets])


def assemble_body(ways, sequences, place, *refs):
    out_ref = refs[-1]
    for a in range(ways):

        @pl.when(pl.program_id(0) == a)
        def _():
            for b in range(sequences):
                out_ref[place[2] ^ b] = refs[a * sequences + b][...]


def assemble(pieces, place):
    ways, sequences = len(pieces), len(pieces[0])
    rows, width = pieces[0][0].shape
    return pl.pallas_call(
        functools.partial(assemble_body, ways, sequences),
        out_shape=jax.ShapeDtypeStruct((sequences, rows, ways * width), jnp.bfloat16),
        grid_spec=pltpu.PrefetchScalarGridSpec(
            num_scalar_prefetch=1,
            grid=(ways,),
            in_specs=[pl.BlockSpec((rows, width), lambda a, place: (0, 0))] * (ways * sequences),
            out_specs=pl.BlockSpec((sequences, rows, width), lambda a, place: (0, 0, place[1] ^ a)),
        ),
        compiler_params=pltpu.CompilerParams(vmem_limit_bytes=VMEM_LIMIT),
    )(place, *[piece for row in pieces for piece in row])


def on_device(ctx_size, tp_size, hidden_in, w_q, w_k, w_v, event_pos):
    _, rows, _ = hidden_in.shape
    features = w_q.shape[1]
    ways = math.gcd(features // HD, ctx_size // 2)
    rest = ctx_size // ways
    ctx_me = lax.axis_index("ctx").astype(jnp.int32)
    tp_me = lax.axis_index("tp").astype(jnp.int32)
    core = ctx_me % 2
    place = jnp.stack([tp_me, ctx_me // rest, core, ctx_me])
    away = list(range(ways - 1, -1, -1))

    def over_ctx(value, offset):
        return exchange(value, "ctx", ctx_size, offset) if offset else value

    def other_shares(own):
        shares = [own]
        bit = 1
        while bit < tp_size:
            shares += [exchange(share, "tp", tp_size, bit) for share in shares]
            bit *= 2
        return shares[1:]

    mine = lax.dynamic_index_in_dim(hidden_in, core, 0, keepdims=False)
    other = over_ctx(lax.dynamic_index_in_dim(hidden_in, 1 - core, 0, keepdims=False), 1)
    received = [other_shares(mine), other_shares(other)]

    start_k, start_v, start_q = own_products(hidden_in, other, [w_k, w_v, w_q], place, ways)

    spans = event_pos[:, 0] // (rows // 2)
    span_other = over_ctx(lax.dynamic_index_in_dim(spans, 1 - core, 0), 1)
    later = jnp.concatenate([place, lax.dynamic_index_in_dim(spans, core, 0), span_other])
    made_0 = {}
    for part in (away[: ways // 2], away[ways // 2 :]):
        if part:
            made_0.update(
                rest_products(received, [0], [w_k, w_v], [start_k, start_v], later, ways, part, EXTRA)[0]
            )
    first = {a: over_ctx(made_0[a], a * rest) for a in away}
    ahead = over_ctx(made_0[0], rest // 2)
    (made_1,) = rest_products(received, [1], [w_k, w_v], [start_k, start_v], place, ways, away)
    received, made_1 = lax.optimization_barrier((received, made_1))
    ahead_1 = over_ctx(made_1[0], rest // 2)
    asked = rest_products(received, [0, 1], [w_q], [start_q], place, ways, away)
    for a in away:
        first[a], asked[0][a] = lax.optimization_barrier((first[a], asked[0][a]))
    blocks = {a * rest: first[a] for a in away}
    blocks[rest // 2] = ahead
    blocks[rest // 2 + 1] = ahead_1
    queries = [{}, {}]
    for a in away:
        last = (first[a], ahead)
        for made, keep, key in ((made_1, blocks, a * rest + 1), (asked[0], queries[0], a), (asked[1], queries[1], a)):
            value, last = lax.optimization_barrier((made[a], last))
            last = keep[key] = over_ctx(value, a * rest)
            if keep is blocks:
                last = (last, ahead_1)
    bit = rest // 2
    while bit > 1:
        for i in list(blocks):
            if i ^ bit not in blocks:
                blocks[i ^ bit] = over_ctx(blocks[i], bit)
        bit //= 2
    table = []
    for i in range(0, ctx_size, 2):
        table += [blocks[i][rows, :1], blocks[i][rows + EXTRA // 2, :1]]
    table = jnp.concatenate(table).astype(jnp.int32)
    pieces = [[None] * 2 for _ in range(ways)]
    for b in range(2):
        outs = attend(b, [queries[b][a] for a in range(ways)], blocks, table)
        for a in away:
            pieces[a][b] = over_ctx(outs[a], a * rest + b)
    return assemble(pieces, place)


def solution(mesh):
    sizes = dict(mesh.shape)
    placed = (P(None, "ctx", "tp"), P(None, "tp"), P(None, "tp"), P(None, "tp"), P(None, "ctx"))
    return jax.shard_map(
        functools.partial(on_device, sizes["ctx"], sizes["tp"]),
        mesh=mesh,
        in_specs=placed,
        out_specs=P(None, "ctx", "tp"),
        check_vma=False,
    )
```

```python
import functools
import math

import jax
import jax.numpy as jnp
from jax import lax
from jax.experimental import pallas as pl
from jax.experimental.pallas import tpu as pltpu
from jax.sharding import PartitionSpec as P

HD = 128
LOG2_E = 1.4426950408889634
HIDDEN = -1e30
VMEM_LIMIT = 56 * 2**20


def exchange(value, axis, size, bit):
    return lax.ppermute(value, axis, [(i, i ^ bit) for i in range(size)])


EXTRA = 16


def own_body(weights, place, mine_ref, other_ref, *refs):
    flat_ref = refs[-1]
    rows = other_ref.shape[0]

    @pl.when(pl.program_id(0) == 0)
    def _():
        flat_ref[:rows] = mine_ref[0]
        flat_ref[rows:] = other_ref[...]

    for weight_ref, out_ref in zip(refs[:weights], refs[weights:-1]):
        result = jnp.dot(flat_ref[...], weight_ref[...], preferred_element_type=jnp.float32)
        out_ref[...] = result.reshape(2, rows, -1)


def own_products(hidden_in, other, weights, place, ways):
    rows, feats = other.shape
    features = weights[0].shape[1]
    width = features // ways
    return pl.pallas_call(
        functools.partial(own_body, len(weights)),
        out_shape=[jax.ShapeDtypeStruct((2, rows, features), jnp.float32)] * len(weights),
        grid_spec=pltpu.PrefetchScalarGridSpec(
            num_scalar_prefetch=1,
            grid=(ways,),
            in_specs=[
                pl.BlockSpec((1, rows, feats), lambda g, place: (place[2], 0, 0)),
                pl.BlockSpec((rows, feats), lambda g, place: (0, 0)),
            ]
            + [pl.BlockSpec((feats, width), lambda g, place: (place[0], g))] * len(weights),
            out_specs=[pl.BlockSpec((2, rows, width), lambda g, place: (0, 0, g))] * len(weights),
            scratch_shapes=[pltpu.VMEM((2 * rows, feats), jnp.bfloat16)],
        ),
        compiler_params=pltpu.CompilerParams(vmem_limit_bytes=VMEM_LIMIT),
        cost_estimate=pl.CostEstimate(
            flops=4 * rows * feats * features * len(weights),
            bytes_accessed=2 * feats * features * len(weights),
            transcendentals=0,
        ),
    )(place, hidden_in, other, *weights)


def rest_body(shares, weights, chunks, away, extra, place, *refs):
    inputs = refs[: shares * chunks]
    refs = refs[shares * chunks :]
    weight_refs, refs = refs[: weights * shares], refs[weights * shares :]
    start_refs, refs = refs[:weights], refs[weights:]
    out_refs, flats = refs[: chunks * len(away)], refs[chunks * len(away) :]
    rows, width = out_refs[0].shape
    rows -= extra
    width //= weights
    step = pl.program_id(0)
    if chunks > 1:

        @pl.when(step == 0)
        def _():
            for share in range(shares):
                for c in range(chunks):
                    flats[share][c * rows : (c + 1) * rows] = inputs[c * shares + share][...]

    else:
        flats = inputs
    made = []
    for n in range(weights):
        total = start_refs[n][...].reshape(chunks * rows, width)
        for share in range(shares):
            total += jnp.dot(
                flats[share][...], weight_refs[n * shares + share][...], preferred_element_type=jnp.float32
            )
        made.append(total.astype(jnp.bfloat16))
    for index in range(len(away)):

        @pl.when(step == index)
        def _():
            for c in range(chunks):
                for n in range(weights):
                    out_refs[c * len(away) + index][:rows, n * width : (n + 1) * width] = made[n][
                        c * rows : (c + 1) * rows
                    ]
            if extra:
                line = lax.broadcasted_iota(jnp.int32, (extra, weights * width), 0)
                spans = jnp.where(line < extra // 2, place[4], place[5]).astype(jnp.float32)
                out_refs[index][rows:] = spans.astype(jnp.bfloat16)


def rest_products(received, chosen, weights, starts, place, ways, away, extra=0):
    shares = len(received[0])
    rows, feats = received[0][0].shape
    width = weights[0].shape[1] // ways
    chunks = len(chosen)
    top = away[0]

    def weight_map(share, i, place):
        return (place[0] ^ (share + 1), place[1] ^ (top - i))

    in_specs = [pl.BlockSpec((rows, feats), lambda i, place: (0, 0))] * (shares * chunks)
    for _ in weights:
        for share in range(shares):
            in_specs.append(pl.BlockSpec((feats, width), functools.partial(weight_map, share)))
    in_specs += [
        pl.BlockSpec((chunks, rows, width), lambda i, place: (chosen[0] // chunks, 0, place[1] ^ (top - i)))
    ] * len(weights)
    columns = width * len(weights)
    scratch = [pltpu.VMEM((chunks * rows, feats), jnp.bfloat16)] * (shares if chunks > 1 else 0)
    outs = pl.pallas_call(
        functools.partial(rest_body, shares, len(weights), chunks, away, extra),
        out_shape=[jax.ShapeDtypeStruct((rows + extra, columns), jnp.bfloat16)] * (chunks * len(away)),
        grid_spec=pltpu.PrefetchScalarGridSpec(
            num_scalar_prefetch=1,
            grid=(len(away),),
            in_specs=in_specs,
            out_specs=[pl.BlockSpec((rows + extra, columns), lambda i, place: (0, 0))] * (chunks * len(away)),
            scratch_shapes=scratch,
        ),
        compiler_params=pltpu.CompilerParams(vmem_limit_bytes=VMEM_LIMIT),
        cost_estimate=pl.CostEstimate(
            flops=2 * chunks * rows * feats * shares * columns * len(away),
            bytes_accessed=2 * feats * shares * columns * len(away),
            transcendentals=0,
        ),
    )(
        place,
        *[share for c in chosen for share in received[c]],
        *[weight for weight in weights for _ in range(shares)],
        *starts,
    )
    return [dict(zip(away, outs[c * len(away) : (c + 1) * len(away)])) for c in range(chunks)]


def attend_body(block, ways, slots, arrays, spans, tile, table, *refs):
    count = len(slots)
    query_refs = refs[:ways]
    block_refs = refs[ways : ways + arrays]
    out_refs = refs[ways + arrays : 2 * ways + arrays]
    ordered, asked, scores, highest, sums, total, position, sems = refs[2 * ways + arrays :]
    rows, width = out_refs[0].shape
    half = rows // 2
    heads = width // HD
    rest = count // ways

    copies = []
    for slot, (offset, array, row) in enumerate(slots):
        low = table[offset]
        for part, span in ((0, low), (1, spans - 1 - low)):
            copies.append(
                pltpu.make_async_copy(
                    block_refs[array].at[pl.ds(row + part * half, half)],
                    ordered.at[pl.ds(pl.multiple_of(span * half, 16), half)],
                    sems.at[2 * slot + part],
                )
            )
    for copy in copies:
        copy.start()

    from_lane = lax.broadcasted_iota(jnp.int32, (half, 128), 0) - lax.broadcasted_iota(
        jnp.int32, (half, 128), 1
    )
    for a in range(ways):
        low = table[a * rest + block]
        here = slice(a * half, (a + 1) * half)
        for part, span in ((0, low), (1, spans - 1 - low)):
            asked[part, here] = query_refs[a][part * half : (part + 1) * half]
            position[part, here] = from_lane + span * half
    highest[...] = jnp.full_like(highest, HIDDEN)
    sums[...] = jnp.zeros_like(sums)
    total[...] = jnp.zeros_like(total)
    for copy in copies:
        copy.wait()

    slope = LOG2_E / math.sqrt(HD)
    middle = spans * half // 2

    def visible(part, h, column):
        piece = scores[h, :, column : column + 128]
        if column < middle * part:
            return piece
        return jnp.where(position[part] >= column, piece, HIDDEN)

    for part in range(2):
        starts = range(0, middle * (part + 1), tile)
        for start in starts:
            for h in range(heads):
                scores[h, :, start : start + tile] = lax.dot_general(
                    asked[part, :, h * HD : (h + 1) * HD],
                    ordered[start : start + tile, h * HD : (h + 1) * HD],
                    (((1,), (1,)), ((), ())),
                    preferred_element_type=jnp.float32,
                )
                top = highest[h]
                for column in range(start, start + tile, 128):
                    top = jnp.maximum(top, visible(part, h, column))
                highest[h] = top
        for h in range(heads):
            highest[h] = jnp.broadcast_to(
                jnp.max(highest[h], axis=1, keepdims=True), highest.shape[1:]
            )
        for start in starts:
            for h in range(heads):
                top = highest[h]
                added = sums[h]
                weights = []
                for column in range(start, start + tile, 128):
                    piece = jnp.exp2((visible(part, h, column) - top) * slope)
                    added = added + piece
                    weights.append(piece.astype(jnp.bfloat16))
                sums[h] = added
                total[h] += jnp.dot(
                    jnp.concatenate(weights, axis=1),
                    ordered[start : start + tile, width + h * HD : width + (h + 1) * HD],
                    preferred_element_type=jnp.float32,
                )
        for h in range(heads):
            result = total[h] / jnp.sum(sums[h], axis=1, keepdims=True)
            for a in range(ways):
                out_refs[a][part * half : (part + 1) * half, h * HD : (h + 1) * HD] = result[
                    a * half : (a + 1) * half
                ].astype(jnp.bfloat16)
        if part == 0:
            highest[...] = jnp.full_like(highest, HIDDEN)
            sums[...] = jnp.zeros_like(sums)
            total[...] = jnp.zeros_like(total)


def attend(block, queries, blocks, table):
    rows, width = queries[0].shape
    ways, count = len(queries), len(blocks)
    arrays = []
    slots = []
    for offset in sorted(blocks):
        array, row = blocks[offset]
        if not any(array is other for other in arrays):
            arrays.append(array)
        slots.append((offset, [array is other for other in arrays].index(True), row))
    spans = 2 * count
    half = rows // 2
    length = count * rows
    tile = 8 * half
    heads = width // HD
    many = ways * half
    smem = pl.BlockSpec(memory_space=pltpu.SMEM)
    flops = 6 * many * heads * length * HD
    return pl.pallas_call(
        functools.partial(attend_body, block, ways, slots, len(arrays), spans, tile),
        out_shape=[jax.ShapeDtypeStruct((rows, width), jnp.bfloat16)] * ways,
        grid=(1,),
        in_specs=[smem]
        + [pl.BlockSpec((rows, width), lambda i: (0, 0))] * ways
        + [pl.BlockSpec(memory_space=pl.ANY)] * len(arrays),
        out_specs=[pl.BlockSpec((rows, width), lambda i: (0, 0))] * ways,
        scratch_shapes=[
            pltpu.VMEM((length, 2 * width), jnp.bfloat16),
            pltpu.VMEM((2, many, width), jnp.bfloat16),
            pltpu.VMEM((heads, many, length), jnp.float32),
            pltpu.VMEM((heads, many, 128), jnp.float32),
            pltpu.VMEM((heads, many, 128), jnp.float32),
            pltpu.VMEM((heads, many, HD), jnp.float32),
            pltpu.VMEM((2, many, 128), jnp.int32),
            pltpu.SemaphoreType.DMA((2 * count,)),
        ],
        compiler_params=pltpu.CompilerParams(vmem_limit_bytes=VMEM_LIMIT),
        cost_estimate=pl.CostEstimate(
            flops=flops,
            bytes_accessed=4 * length * width + 4 * ways * rows * width,
            transcendentals=flops // (4 * HD),
        ),
    )(table, *queries, *arrays)


def table_body(offsets, *refs):
    table = refs[-1]
    for offset, ref in zip(offsets, refs):
        found = ref[...].astype(jnp.float32)
        for part in range(2):
            table[offset + part] = jnp.max(found[part * EXTRA // 2 : (part + 1) * EXTRA // 2]).astype(jnp.int32)


def span_table(blocks, rows):
    offsets = sorted(blocks)
    return pl.pallas_call(
        functools.partial(table_body, offsets),
        out_shape=jax.ShapeDtypeStruct((2 * len(offsets),), jnp.int32),
        grid=(1,),
        in_specs=[
            pl.BlockSpec((EXTRA, 128), functools.partial(lambda row, i: (row, 0), (blocks[i][1] + rows) // EXTRA))
            for i in offsets
        ],
        out_specs=pl.BlockSpec(memory_space=pltpu.SMEM),
        compiler_params=pltpu.CompilerParams(vmem_limit_bytes=VMEM_LIMIT),
    )(*[blocks[i][0] for i in offsets])


def pack_body(*refs):
    for n, ref in enumerate(refs[:-1]):

        @pl.when(pl.program_id(0) == n)
        def _():
            refs[-1][...] = ref[...]


def pack(pieces):
    if len(pieces) == 1:
        return pieces[0]
    rows, columns = pieces[0].shape
    return pl.pallas_call(
        pack_body,
        out_shape=jax.ShapeDtypeStruct((len(pieces) * rows, columns), jnp.bfloat16),
        grid=(len(pieces),),
        in_specs=[pl.BlockSpec((rows, columns), lambda i: (0, 0))] * len(pieces),
        out_specs=pl.BlockSpec((rows, columns), lambda i: (i, 0)),
        compiler_params=pltpu.CompilerParams(vmem_limit_bytes=VMEM_LIMIT),
    )(*pieces)


def assemble_body(ways, place, *refs):
    for a in range(ways):

        @pl.when(pl.program_id(0) == a)
        def _():
            refs[-1][0] = refs[a][...]


def assemble(pieces, b, before, place):
    ways = len(pieces)
    rows, width = pieces[0].shape
    in_specs = [pl.BlockSpec((rows, width), lambda a, place: (0, 0))] * ways
    operands = list(pieces)
    aliases = {}
    if before is not None:
        in_specs.append(pl.BlockSpec(memory_space=pl.ANY))
        operands.append(before)
        aliases = {1 + ways: 0}
    return pl.pallas_call(
        functools.partial(assemble_body, ways),
        out_shape=jax.ShapeDtypeStruct((2, rows, ways * width), jnp.bfloat16),
        grid_spec=pltpu.PrefetchScalarGridSpec(
            num_scalar_prefetch=1,
            grid=(ways,),
            in_specs=in_specs,
            out_specs=pl.BlockSpec((1, rows, width), lambda a, place: (place[2] ^ b, 0, place[1] ^ a)),
        ),
        input_output_aliases=aliases,
        compiler_params=pltpu.CompilerParams(vmem_limit_bytes=VMEM_LIMIT),
    )(place, *operands)


def on_device(ctx_size, tp_size, hidden_in, w_q, w_k, w_v, event_pos):
    _, rows, _ = hidden_in.shape
    features = w_q.shape[1]
    ways = math.gcd(features // HD, ctx_size // 2)
    rest = ctx_size // ways
    ctx_me = lax.axis_index("ctx").astype(jnp.int32)
    tp_me = lax.axis_index("tp").astype(jnp.int32)
    core = ctx_me % 2
    place = jnp.stack([tp_me, ctx_me // rest, core, ctx_me])
    away = list(range(ways - 1, -1, -1))

    def over_ctx(value, offset):
        return exchange(value, "ctx", ctx_size, offset) if offset else value

    def other_shares(own):
        shares = [own]
        bit = 1
        while bit < tp_size:
            shares += [exchange(share, "tp", tp_size, bit) for share in shares]
            bit *= 2
        return shares[1:]

    mine = lax.dynamic_index_in_dim(hidden_in, core, 0, keepdims=False)
    other = over_ctx(lax.dynamic_index_in_dim(hidden_in, 1 - core, 0, keepdims=False), 1)
    received = [other_shares(mine), other_shares(other)]

    start_k, start_v, start_q = own_products(hidden_in, other, [w_k, w_v, w_q], place, ways)

    spans = event_pos[:, 0] // (rows // 2)
    span_other = over_ctx(lax.dynamic_index_in_dim(spans, 1 - core, 0), 1)
    later = jnp.concatenate([place, lax.dynamic_index_in_dim(spans, core, 0), span_other])
    made_0 = {}
    for part in (away[: ways // 2], away[ways // 2 :]):
        if part:
            made_0.update(
                rest_products(received, [0], [w_k, w_v], [start_k, start_v], later, ways, part, EXTRA)[0]
            )
    first = {a: over_ctx(made_0[a], a * rest) for a in away}
    (made_1,) = rest_products(received, [1], [w_k, w_v], [start_k, start_v], place, ways, away)
    ahead_1 = over_ctx(made_1[0], rest // 2)
    for a in away:
        first[a], made_1[a] = lax.optimization_barrier((first[a], made_1[a]))
    packed = pack([first[a] for a in range(ways)])
    received, packed, made_1[0] = lax.optimization_barrier((received, packed, made_1[0]))
    asked = rest_products(received, [0, 1], [w_q], [start_q], place, ways, away)

    whole = {0: packed}
    bit = rest // 2
    while bit > 1:
        for i in list(whole):
            whole[i ^ bit] = over_ctx(whole[i], bit)
        bit //= 2
    blocks = {}
    for i, array in whole.items():
        for a in range(ways):
            blocks[i ^ (a * rest)] = (array, a * (rows + EXTRA))
    table = span_table(blocks, rows)

    second = {}
    queries = [{}, {}]
    for a in away:
        last = first[a]
        for made, keep, key in ((made_1, second, a * rest + 1), (asked[0], queries[0], a), (asked[1], queries[1], a)):
            value, last = lax.optimization_barrier((made[a], last))
            last = keep[key] = over_ctx(value, a * rest)
            if keep is second and a:
                last = (last, ahead_1)
    freed = whole[rest // 2]
    for a in away[:-1]:
        second[a * rest + 1], freed = lax.optimization_barrier((second[a * rest + 1], freed))
    second[rest // 2 + 1] = ahead_1
    bit = rest // 2
    while bit > 1:
        for i in list(second):
            if i ^ bit not in second:
                second[i ^ bit] = over_ctx(second[i], bit)
        bit //= 2
    blocks.update({i: (array, 0) for i, array in second.items()})
    out = None
    for b in range(2):
        outs = attend(b, [queries[b][a] for a in range(ways)], blocks, table)
        pieces = {a: over_ctx(outs[a], a * rest + b) for a in away}
        out = assemble([pieces[a] for a in range(ways)], b, out, place)
    return out


def solution(mesh):
    sizes = dict(mesh.shape)
    placed = (P(None, "ctx", "tp"), P(None, "tp"), P(None, "tp"), P(None, "tp"), P(None, "ctx"))
    return jax.shard_map(
        functools.partial(on_device, sizes["ctx"], sizes["tp"]),
        mesh=mesh,
        in_specs=placed,
        out_specs=P(None, "ctx", "tp"),
        check_vma=False,
    )
```

```python
import functools
import math

import jax
import jax.numpy as jnp
from jax import lax
from jax.experimental import pallas as pl
from jax.experimental.pallas import tpu as pltpu
from jax.sharding import PartitionSpec as P

HD = 128
LOG2_E = 1.4426950408889634
HIDDEN = -1e30
VMEM_LIMIT = 56 * 2**20


def exchange(value, axis, size, bit):
    return lax.ppermute(value, axis, [(i, i ^ bit) for i in range(size)])


EXTRA = 16


def own_body(weights, place, mine_ref, other_ref, *refs):
    flat_ref = refs[-1]
    rows = other_ref.shape[0]

    @pl.when(pl.program_id(0) == 0)
    def _():
        flat_ref[:rows] = mine_ref[0]
        flat_ref[rows:] = other_ref[...]

    for weight_ref, out_ref in zip(refs[:weights], refs[weights:-1]):
        result = jnp.dot(flat_ref[...], weight_ref[...], preferred_element_type=jnp.float32)
        out_ref[...] = result.reshape(2, rows, -1)


def own_products(hidden_in, other, weights, place, ways):
    rows, feats = other.shape
    features = weights[0].shape[1]
    width = features // ways
    return pl.pallas_call(
        functools.partial(own_body, len(weights)),
        out_shape=[jax.ShapeDtypeStruct((2, rows, features), jnp.float32)] * len(weights),
        grid_spec=pltpu.PrefetchScalarGridSpec(
            num_scalar_prefetch=1,
            grid=(ways,),
            in_specs=[
                pl.BlockSpec((1, rows, feats), lambda g, place: (place[2], 0, 0)),
                pl.BlockSpec((rows, feats), lambda g, place: (0, 0)),
            ]
            + [pl.BlockSpec((feats, width), lambda g, place: (place[0], g))] * len(weights),
            out_specs=[pl.BlockSpec((2, rows, width), lambda g, place: (0, 0, g))] * len(weights),
            scratch_shapes=[pltpu.VMEM((2 * rows, feats), jnp.bfloat16)],
        ),
        compiler_params=pltpu.CompilerParams(vmem_limit_bytes=VMEM_LIMIT),
        cost_estimate=pl.CostEstimate(
            flops=4 * rows * feats * features * len(weights),
            bytes_accessed=2 * feats * features * len(weights),
            transcendentals=0,
        ),
    )(place, hidden_in, other, *weights)


def rest_body(shares, weights, chunks, away, extra, place, *refs):
    inputs = refs[: shares * chunks]
    refs = refs[shares * chunks :]
    weight_refs, refs = refs[: weights * shares], refs[weights * shares :]
    start_refs, refs = refs[:weights], refs[weights:]
    out_refs, flats = refs[: chunks * len(away)], refs[chunks * len(away) :]
    rows, width = out_refs[0].shape
    rows -= extra
    width //= weights
    step = pl.program_id(0)
    if chunks > 1:

        @pl.when(step == 0)
        def _():
            for share in range(shares):
                for c in range(chunks):
                    flats[share][c * rows : (c + 1) * rows] = inputs[c * shares + share][...]

    else:
        flats = inputs
    made = []
    for n in range(weights):
        total = start_refs[n][...].reshape(chunks * rows, width)
        for share in range(shares):
            total += jnp.dot(
                flats[share][...], weight_refs[n * shares + share][...], preferred_element_type=jnp.float32
            )
        made.append(total.astype(jnp.bfloat16))
    for index in range(len(away)):

        @pl.when(step == index)
        def _():
            for c in range(chunks):
                for n in range(weights):
                    out_refs[c * len(away) + index][:rows, n * width : (n + 1) * width] = made[n][
                        c * rows : (c + 1) * rows
                    ]
            if extra:
                line = lax.broadcasted_iota(jnp.int32, (extra, weights * width), 0)
                spans = jnp.where(line < extra // 2, place[4], place[5]).astype(jnp.float32)
                out_refs[index][rows:] = spans.astype(jnp.bfloat16)


def rest_products(received, chosen, weights, starts, place, ways, away, extra=0):
    shares = len(received[0])
    rows, feats = received[0][0].shape
    width = weights[0].shape[1] // ways
    chunks = len(chosen)
    top = away[0]
    stride = away[1] - top if len(away) > 1 else 0

    def weight_map(share, i, place):
        return (place[0] ^ (share + 1), place[1] ^ (top + stride * i))

    in_specs = [pl.BlockSpec((rows, feats), lambda i, place: (0, 0))] * (shares * chunks)
    for _ in weights:
        for share in range(shares):
            in_specs.append(pl.BlockSpec((feats, width), functools.partial(weight_map, share)))
    in_specs += [
        pl.BlockSpec((chunks, rows, width), lambda i, place: (chosen[0] // chunks, 0, place[1] ^ (top + stride * i)))
    ] * len(weights)
    columns = width * len(weights)
    scratch = [pltpu.VMEM((chunks * rows, feats), jnp.bfloat16)] * (shares if chunks > 1 else 0)
    outs = pl.pallas_call(
        functools.partial(rest_body, shares, len(weights), chunks, away, extra),
        out_shape=[jax.ShapeDtypeStruct((rows + extra, columns), jnp.bfloat16)] * (chunks * len(away)),
        grid_spec=pltpu.PrefetchScalarGridSpec(
            num_scalar_prefetch=1,
            grid=(len(away),),
            in_specs=in_specs,
            out_specs=[pl.BlockSpec((rows + extra, columns), lambda i, place: (0, 0))] * (chunks * len(away)),
            scratch_shapes=scratch,
        ),
        compiler_params=pltpu.CompilerParams(vmem_limit_bytes=VMEM_LIMIT),
        cost_estimate=pl.CostEstimate(
            flops=2 * chunks * rows * feats * shares * columns * len(away),
            bytes_accessed=2 * feats * shares * columns * len(away),
            transcendentals=0,
        ),
    )(
        place,
        *[share for c in chosen for share in received[c]],
        *[weight for weight in weights for _ in range(shares)],
        *starts,
    )
    return [dict(zip(away, outs[c * len(away) : (c + 1) * len(away)])) for c in range(chunks)]


def attend_body(block, ways, slots, arrays, spans, tile, table, *refs):
    count = len(slots)
    query_refs = refs[:ways]
    block_refs = refs[ways : ways + arrays]
    out_refs = refs[ways + arrays : 2 * ways + arrays]
    ordered, asked, scores, highest, sums, total, position, sems = refs[2 * ways + arrays :]
    rows, width = out_refs[0].shape
    half = rows // 2
    heads = width // HD
    rest = count // ways

    copies = []
    for slot, (offset, array, row) in enumerate(slots):
        low = table[offset]
        for part, span in ((0, low), (1, spans - 1 - low)):
            copies.append(
                pltpu.make_async_copy(
                    block_refs[array].at[pl.ds(row + part * half, half)],
                    ordered.at[pl.ds(pl.multiple_of(span * half, 16), half)],
                    sems.at[2 * slot + part],
                )
            )
    for copy in copies:
        copy.start()

    from_lane = lax.broadcasted_iota(jnp.int32, (half, 128), 0) - lax.broadcasted_iota(
        jnp.int32, (half, 128), 1
    )
    for a in range(ways):
        low = table[a * rest + block]
        here = slice(a * half, (a + 1) * half)
        for part, span in ((0, low), (1, spans - 1 - low)):
            asked[part, here] = query_refs[a][part * half : (part + 1) * half]
            position[part, here] = from_lane + span * half
    for copy in copies:
        copy.wait()

    slope = LOG2_E / math.sqrt(HD)
    middle = spans * half // 2

    def starts(part):
        return range(0, middle * (part + 1), tile)

    def visible(unit, slot, column):
        piece = scores[slot, :, column : column + 128]
        if column < middle * unit[0]:
            return piece
        return jnp.where(position[unit[0]] >= column, piece, HIDDEN)

    def score_tile(unit, slot, start):
        part, h = unit
        scores[slot, :, start : start + tile] = lax.dot_general(
            asked[part, :, h * HD : (h + 1) * HD],
            ordered[start : start + tile, h * HD : (h + 1) * HD],
            (((1,), (1,)), ((), ())),
            preferred_element_type=jnp.float32,
        )
        top = None if start == 0 else highest[slot]
        for column in range(start, start + tile, 128):
            piece = visible(unit, slot, column)
            top = piece if top is None else jnp.maximum(top, piece)
        highest[slot] = top

    def value_tile(unit, slot, start):
        part, h = unit
        top = highest[slot]
        added = None if start == 0 else sums[slot]
        weights = []
        for column in range(start, start + tile, 128):
            piece = jnp.exp2((visible(unit, slot, column) - top) * slope)
            added = piece if added is None else added + piece
            weights.append(piece.astype(jnp.bfloat16))
        sums[slot] = added
        product = jnp.dot(
            jnp.concatenate(weights, axis=1),
            ordered[start : start + tile, width + h * HD : width + (h + 1) * HD],
            preferred_element_type=jnp.float32,
        )
        if start == 0:
            total[slot] = product
        else:
            total[slot] += product

    units = [(0, 0)] + [(1, h) for h in range(heads)] + [(0, h) for h in range(1, heads)]
    for n in range(len(units) + 1):
        todo = []
        if n < len(units):
            todo.append([functools.partial(score_tile, units[n], n % 2, start) for start in starts(units[n][0])])
        if n > 0:
            slot = (n - 1) % 2
            highest[slot] = jnp.broadcast_to(jnp.max(highest[slot], axis=1, keepdims=True), highest.shape[1:])
            todo.append([functools.partial(value_tile, units[n - 1], slot, start) for start in starts(units[n - 1][0])])
        for index in range(max(len(steps) for steps in todo)):
            for steps in todo:
                if index < len(steps):
                    steps[index]()
        if n > 0:
            part, h = units[n - 1]
            result = total[slot] / jnp.sum(sums[slot], axis=1, keepdims=True)
            for a in range(ways):
                out_refs[a][part * half : (part + 1) * half, h * HD : (h + 1) * HD] = result[
                    a * half : (a + 1) * half
                ].astype(jnp.bfloat16)


def attend(block, queries, blocks, table):
    rows, width = queries[0].shape
    ways, count = len(queries), len(blocks)
    arrays = []
    slots = []
    for offset in sorted(blocks):
        array, row = blocks[offset]
        if not any(array is other for other in arrays):
            arrays.append(array)
        slots.append((offset, [array is other for other in arrays].index(True), row))
    spans = 2 * count
    half = rows // 2
    length = count * rows
    tile = 8 * half
    heads = width // HD
    many = ways * half
    smem = pl.BlockSpec(memory_space=pltpu.SMEM)
    flops = 6 * many * heads * length * HD
    return pl.pallas_call(
        functools.partial(attend_body, block, ways, slots, len(arrays), spans, tile),
        out_shape=[jax.ShapeDtypeStruct((rows, width), jnp.bfloat16)] * ways,
        grid=(1,),
        in_specs=[smem]
        + [pl.BlockSpec((rows, width), lambda i: (0, 0))] * ways
        + [pl.BlockSpec(memory_space=pl.ANY)] * len(arrays),
        out_specs=[pl.BlockSpec((rows, width), lambda i: (0, 0))] * ways,
        scratch_shapes=[
            pltpu.VMEM((length, 2 * width), jnp.bfloat16),
            pltpu.VMEM((2, many, width), jnp.bfloat16),
            pltpu.VMEM((2, many, length), jnp.float32),
            pltpu.VMEM((2, many, 128), jnp.float32),
            pltpu.VMEM((2, many, 128), jnp.float32),
            pltpu.VMEM((2, many, HD), jnp.float32),
            pltpu.VMEM((2, many, 128), jnp.int32),
            pltpu.SemaphoreType.DMA((2 * count,)),
        ],
        compiler_params=pltpu.CompilerParams(vmem_limit_bytes=VMEM_LIMIT),
        cost_estimate=pl.CostEstimate(
            flops=flops,
            bytes_accessed=4 * length * width + 4 * ways * rows * width,
            transcendentals=flops // (4 * HD),
        ),
    )(table, *queries, *arrays)


def table_body(offsets, *refs):
    table = refs[-1]
    for offset, ref in zip(offsets, refs):
        found = ref[...].astype(jnp.float32)
        for part in range(2):
            table[offset + part] = jnp.max(found[part * EXTRA // 2 : (part + 1) * EXTRA // 2]).astype(jnp.int32)


def span_table(blocks, rows):
    offsets = sorted(blocks)
    return pl.pallas_call(
        functools.partial(table_body, offsets),
        out_shape=jax.ShapeDtypeStruct((2 * len(offsets),), jnp.int32),
        grid=(1,),
        in_specs=[
            pl.BlockSpec((EXTRA, 128), functools.partial(lambda row, i: (row, 0), (blocks[i][1] + rows) // EXTRA))
            for i in offsets
        ],
        out_specs=pl.BlockSpec(memory_space=pltpu.SMEM),
        compiler_params=pltpu.CompilerParams(vmem_limit_bytes=VMEM_LIMIT),
    )(*[blocks[i][0] for i in offsets])


def assemble_body(ways, place, *refs):
    for a in range(ways):

        @pl.when(pl.program_id(0) == a)
        def _():
            refs[-1][0] = refs[a][...]


def assemble(pieces, b, before, place):
    ways = len(pieces)
    rows, width = pieces[0].shape
    in_specs = [pl.BlockSpec((rows, width), lambda a, place: (0, 0))] * ways
    operands = list(pieces)
    aliases = {}
    if before is not None:
        in_specs.append(pl.BlockSpec(memory_space=pl.ANY))
        operands.append(before)
        aliases = {1 + ways: 0}
    return pl.pallas_call(
        functools.partial(assemble_body, ways),
        out_shape=jax.ShapeDtypeStruct((2, rows, ways * width), jnp.bfloat16),
        grid_spec=pltpu.PrefetchScalarGridSpec(
            num_scalar_prefetch=1,
            grid=(ways,),
            in_specs=in_specs,
            out_specs=pl.BlockSpec((1, rows, width), lambda a, place: (place[2] ^ b, 0, place[1] ^ a)),
        ),
        input_output_aliases=aliases,
        compiler_params=pltpu.CompilerParams(vmem_limit_bytes=VMEM_LIMIT),
    )(place, *operands)


def on_device(ctx_size, tp_size, hidden_in, w_q, w_k, w_v, event_pos):
    _, rows, _ = hidden_in.shape
    features = w_q.shape[1]
    ways = math.gcd(features // HD, ctx_size // 2)
    rest = ctx_size // ways
    ctx_me = lax.axis_index("ctx").astype(jnp.int32)
    tp_me = lax.axis_index("tp").astype(jnp.int32)
    core = ctx_me % 2
    place = jnp.stack([tp_me, ctx_me // rest, core, ctx_me])
    away = list(range(ways - 1, -1, -1))

    def over_ctx(value, offset):
        return exchange(value, "ctx", ctx_size, offset) if offset else value

    def other_shares(own):
        shares = [own]
        bit = 1
        while bit < tp_size:
            shares += [exchange(share, "tp", tp_size, bit) for share in shares]
            bit *= 2
        return shares[1:]

    mine = lax.dynamic_index_in_dim(hidden_in, core, 0, keepdims=False)
    other = over_ctx(lax.dynamic_index_in_dim(hidden_in, 1 - core, 0, keepdims=False), 1)
    received = [other_shares(mine), other_shares(other)]

    start_k, start_v, start_q = own_products(hidden_in, other, [w_k, w_v, w_q], place, ways)

    spans = event_pos[:, 0] // (rows // 2)
    span_other = over_ctx(lax.dynamic_index_in_dim(spans, 1 - core, 0), 1)
    later = jnp.concatenate([place, lax.dynamic_index_in_dim(spans, core, 0), span_other])
    (made_0,) = rest_products(received, [0], [w_k, w_v], [start_k, start_v], later, ways, away, EXTRA)
    first = {a: over_ctx(made_0[a], a * rest) for a in away}
    ahead = over_ctx(made_0[0], rest // 2)
    asked = rest_products(received, [0], [w_q], [start_q], place, ways, away)
    received, asked = lax.optimization_barrier((received, asked))
    (made_1,) = rest_products(received, [1], [w_k, w_v], [start_k, start_v], place, ways, away)
    ahead_1 = over_ctx(made_1[0], rest // 2)
    received, made_1 = lax.optimization_barrier((received, made_1))
    asked += rest_products(received, [1], [w_q], [start_q], place, ways, away)
    for a in away:
        first[a], asked[1][a] = lax.optimization_barrier((first[a], asked[1][a]))

    second = {}
    queries = [{}, {}]
    for a in away:
        last = (first[a], ahead)
        for made, keep, key in ((made_1, second, a * rest + 1), (asked[0], queries[0], a), (asked[1], queries[1], a)):
            value, last = lax.optimization_barrier((made[a], last))
            last = keep[key] = over_ctx(value, a * rest)
            if keep is second and a:
                last = (last, ahead_1)

    def over_y(blocks):
        bit = rest // 2
        while bit > 1:
            for i in list(blocks):
                if i ^ bit not in blocks:
                    blocks[i ^ bit] = over_ctx(blocks[i], bit)
            bit //= 2
        return blocks

    blocks = {a * rest: first[a] for a in away}
    blocks[rest // 2] = ahead
    blocks = over_y(blocks)
    table = span_table({i: (array, 0) for i, array in blocks.items()}, rows)
    second[rest // 2 + 1] = ahead_1
    blocks.update(over_y(second))
    blocks = {i: (array, 0) for i, array in blocks.items()}
    out = None
    for b in range(2):
        outs = attend(b, [queries[b][a] for a in range(ways)], blocks, table)
        pieces = {a: over_ctx(outs[a], a * rest + b) for a in away}
        out = assemble([pieces[a] for a in range(ways)], b, out, place)
    return out


def solution(mesh):
    sizes = dict(mesh.shape)
    placed = (P(None, "ctx", "tp"), P(None, "tp"), P(None, "tp"), P(None, "tp"), P(None, "ctx"))
    return jax.shard_map(
        functools.partial(on_device, sizes["ctx"], sizes["tp"]),
        mesh=mesh,
        in_specs=placed,
        out_specs=P(None, "ctx", "tp"),
        check_vma=False,
    )
```

```python
import functools
import math

import jax
import jax.numpy as jnp
from jax import lax
from jax.experimental import pallas as pl
from jax.experimental.pallas import tpu as pltpu
from jax.sharding import PartitionSpec as P

HD = 128
LOG2_E = 1.4426950408889634
HIDDEN = -1e30
VMEM_LIMIT = 44 * 2**20


def exchange(value, axis, size, bit):
    return lax.ppermute(value, axis, [(i, i ^ bit) for i in range(size)])


EXTRA = 16


def own_body(weights, place, mine_ref, other_ref, *refs):
    flat_ref = refs[-1]
    rows = other_ref.shape[0]

    @pl.when(pl.program_id(0) == 0)
    def _():
        flat_ref[:rows] = mine_ref[0]
        flat_ref[rows:] = other_ref[...]

    for weight_ref, out_ref in zip(refs[:weights], refs[weights:-1]):
        result = jnp.dot(flat_ref[...], weight_ref[...], preferred_element_type=jnp.float32)
        out_ref[...] = result.reshape(2, rows, -1)


def own_products(hidden_in, other, weights, place, ways):
    rows, feats = other.shape
    features = weights[0].shape[1]
    width = features // ways
    return pl.pallas_call(
        functools.partial(own_body, len(weights)),
        out_shape=[jax.ShapeDtypeStruct((2, rows, features), jnp.float32)] * len(weights),
        grid_spec=pltpu.PrefetchScalarGridSpec(
            num_scalar_prefetch=1,
            grid=(ways,),
            in_specs=[
                pl.BlockSpec((1, rows, feats), lambda g, place: (place[2], 0, 0)),
                pl.BlockSpec((rows, feats), lambda g, place: (0, 0)),
            ]
            + [pl.BlockSpec((feats, width), lambda g, place: (place[0], g))] * len(weights),
            out_specs=[pl.BlockSpec((2, rows, width), lambda g, place: (0, 0, g))] * len(weights),
            scratch_shapes=[pltpu.VMEM((2 * rows, feats), jnp.bfloat16)],
        ),
        compiler_params=pltpu.CompilerParams(vmem_limit_bytes=VMEM_LIMIT),
        cost_estimate=pl.CostEstimate(
            flops=4 * rows * feats * features * len(weights),
            bytes_accessed=2 * feats * features * len(weights),
            transcendentals=0,
        ),
    )(place, hidden_in, other, *weights)


def rest_body(shares, weights, chunks, away, extra, place, *refs):
    inputs = refs[: shares * chunks]
    refs = refs[shares * chunks :]
    weight_refs, refs = refs[: weights * shares], refs[weights * shares :]
    start_refs, refs = refs[:weights], refs[weights:]
    out_refs, flats = refs[: chunks * len(away)], refs[chunks * len(away) :]
    rows, width = out_refs[0].shape
    rows -= extra
    width //= weights
    step = pl.program_id(0)
    if chunks > 1:

        @pl.when(step == 0)
        def _():
            for share in range(shares):
                for c in range(chunks):
                    flats[share][c * rows : (c + 1) * rows] = inputs[c * shares + share][...]

    else:
        flats = inputs
    made = []
    for n in range(weights):
        total = start_refs[n][...].reshape(chunks * rows, width)
        for share in range(shares):
            total += jnp.dot(
                flats[share][...], weight_refs[n * shares + share][...], preferred_element_type=jnp.float32
            )
        made.append(total.astype(jnp.bfloat16))
    for index in range(len(away)):

        @pl.when(step == index)
        def _():
            for c in range(chunks):
                for n in range(weights):
                    out_refs[c * len(away) + index][:rows, n * width : (n + 1) * width] = made[n][
                        c * rows : (c + 1) * rows
                    ]
            if extra:
                line = lax.broadcasted_iota(jnp.int32, (extra, weights * width), 0)
                spans = jnp.where(line < extra // 2, place[4], place[5]).astype(jnp.float32)
                out_refs[index][rows:] = spans.astype(jnp.bfloat16)


def rest_products(received, chosen, weights, starts, place, ways, away, extra=0):
    shares = len(received[0])
    rows, feats = received[0][0].shape
    width = weights[0].shape[1] // ways
    chunks = len(chosen)
    top = away[0]
    stride = away[1] - top if len(away) > 1 else 0

    def weight_map(share, i, place):
        return (place[0] ^ (share + 1), place[1] ^ (top + stride * i))

    in_specs = [pl.BlockSpec((rows, feats), lambda i, place: (0, 0))] * (shares * chunks)
    for _ in weights:
        for share in range(shares):
            in_specs.append(pl.BlockSpec((feats, width), functools.partial(weight_map, share)))
    in_specs += [
        pl.BlockSpec((chunks, rows, width), lambda i, place: (chosen[0] // chunks, 0, place[1] ^ (top + stride * i)))
    ] * len(weights)
    columns = width * len(weights)
    scratch = [pltpu.VMEM((chunks * rows, feats), jnp.bfloat16)] * (shares if chunks > 1 else 0)
    outs = pl.pallas_call(
        functools.partial(rest_body, shares, len(weights), chunks, away, extra),
        out_shape=[jax.ShapeDtypeStruct((rows + extra, columns), jnp.bfloat16)] * (chunks * len(away)),
        grid_spec=pltpu.PrefetchScalarGridSpec(
            num_scalar_prefetch=1,
            grid=(len(away),),
            in_specs=in_specs,
            out_specs=[pl.BlockSpec((rows + extra, columns), lambda i, place: (0, 0))] * (chunks * len(away)),
            scratch_shapes=scratch,
        ),
        compiler_params=pltpu.CompilerParams(vmem_limit_bytes=VMEM_LIMIT),
        cost_estimate=pl.CostEstimate(
            flops=2 * chunks * rows * feats * shares * columns * len(away),
            bytes_accessed=2 * feats * shares * columns * len(away),
            transcendentals=0,
        ),
    )(
        place,
        *[share for c in chosen for share in received[c]],
        *[weight for weight in weights for _ in range(shares)],
        *starts,
    )
    return [dict(zip(away, outs[c * len(away) : (c + 1) * len(away)])) for c in range(chunks)]


def attend_body(block, ways, slots, arrays, spans, tile, table, *refs):
    count = len(slots)
    query_refs = refs[:ways]
    block_refs = refs[ways : ways + arrays]
    out_refs = refs[ways + arrays : 2 * ways + arrays]
    ordered, asked, scores, highest, sums, total, position, sems = refs[2 * ways + arrays :]
    rows, width = out_refs[0].shape
    half = rows // 2
    heads = width // HD
    rest = count // ways

    copies = []
    for slot, (offset, array, row) in enumerate(slots):
        low = table[offset]
        for part, span in ((0, low), (1, spans - 1 - low)):
            copies.append(
                pltpu.make_async_copy(
                    block_refs[array].at[pl.ds(row + part * half, half)],
                    ordered.at[pl.ds(pl.multiple_of(span * half, 16), half)],
                    sems.at[2 * slot + part],
                )
            )
    for copy in copies:
        copy.start()

    from_lane = lax.broadcasted_iota(jnp.int32, (half, 128), 0) - lax.broadcasted_iota(
        jnp.int32, (half, 128), 1
    )
    for a in range(ways):
        low = table[a * rest + block]
        here = slice(a * half, (a + 1) * half)
        for part, span in ((0, low), (1, spans - 1 - low)):
            asked[part, here] = query_refs[a][part * half : (part + 1) * half]
            position[part, here] = from_lane + span * half
    for copy in copies:
        copy.wait()

    slope = LOG2_E / math.sqrt(HD)
    middle = spans * half // 2

    def starts(part):
        return range(0, middle * (part + 1), tile)

    def visible(unit, slot, column):
        piece = scores[slot, :, column : column + 128]
        if column < middle * unit[0]:
            return piece
        return jnp.where(position[unit[0]] >= column, piece, HIDDEN)

    def score_tile(unit, slot, start):
        part, h = unit
        scores[slot, :, start : start + tile] = lax.dot_general(
            asked[part, :, h * HD : (h + 1) * HD],
            ordered[start : start + tile, h * HD : (h + 1) * HD],
            (((1,), (1,)), ((), ())),
            preferred_element_type=jnp.float32,
        )
        top = None if start == 0 else highest[slot]
        for column in range(start, start + tile, 128):
            piece = visible(unit, slot, column)
            top = piece if top is None else jnp.maximum(top, piece)
        highest[slot] = top

    def value_tile(unit, slot, start):
        part, h = unit
        top = highest[slot]
        added = None if start == 0 else sums[slot]
        weights = []
        for column in range(start, start + tile, 128):
            piece = jnp.exp2((visible(unit, slot, column) - top) * slope)
            added = piece if added is None else added + piece
            weights.append(piece.astype(jnp.bfloat16))
        sums[slot] = added
        product = jnp.dot(
            jnp.concatenate(weights, axis=1),
            ordered[start : start + tile, width + h * HD : width + (h + 1) * HD],
            preferred_element_type=jnp.float32,
        )
        if start == 0:
            total[slot] = product
        else:
            total[slot] += product

    units = [(0, 0)] + [(1, h) for h in range(heads)] + [(0, h) for h in range(1, heads)]
    for n in range(len(units) + 1):
        todo = []
        if n < len(units):
            todo.append([functools.partial(score_tile, units[n], n % 2, start) for start in starts(units[n][0])])
        if n > 0:
            slot = (n - 1) % 2
            highest[slot] = jnp.broadcast_to(jnp.max(highest[slot], axis=1, keepdims=True), highest.shape[1:])
            todo.append([functools.partial(value_tile, units[n - 1], slot, start) for start in starts(units[n - 1][0])])
        for index in range(max(len(steps) for steps in todo)):
            for steps in todo:
                if index < len(steps):
                    steps[index]()
        if n > 0:
            part, h = units[n - 1]
            result = total[slot] / jnp.sum(sums[slot], axis=1, keepdims=True)
            for a in range(ways):
                out_refs[a][part * half : (part + 1) * half, h * HD : (h + 1) * HD] = result[
                    a * half : (a + 1) * half
                ].astype(jnp.bfloat16)


def attend(block, queries, blocks, table):
    rows, width = queries[0].shape
    ways, count = len(queries), len(blocks)
    arrays = []
    slots = []
    for offset in sorted(blocks):
        array, row = blocks[offset]
        if not any(array is other for other in arrays):
            arrays.append(array)
        slots.append((offset, [array is other for other in arrays].index(True), row))
    spans = 2 * count
    half = rows // 2
    length = count * rows
    tile = 8 * half
    heads = width // HD
    many = ways * half
    smem = pl.BlockSpec(memory_space=pltpu.SMEM)
    flops = 6 * many * heads * length * HD
    return pl.pallas_call(
        functools.partial(attend_body, block, ways, slots, len(arrays), spans, tile),
        out_shape=[jax.ShapeDtypeStruct((rows, width), jnp.bfloat16)] * ways,
        grid=(1,),
        in_specs=[smem]
        + [pl.BlockSpec((rows, width), lambda i: (0, 0))] * ways
        + [pl.BlockSpec(memory_space=pl.ANY)] * len(arrays),
        out_specs=[pl.BlockSpec((rows, width), lambda i: (0, 0))] * ways,
        scratch_shapes=[
            pltpu.VMEM((length, 2 * width), jnp.bfloat16),
            pltpu.VMEM((2, many, width), jnp.bfloat16),
            pltpu.VMEM((2, many, length), jnp.float32),
            pltpu.VMEM((2, many, 128), jnp.float32),
            pltpu.VMEM((2, many, 128), jnp.float32),
            pltpu.VMEM((2, many, HD), jnp.float32),
            pltpu.VMEM((2, many, 128), jnp.int32),
            pltpu.SemaphoreType.DMA((2 * count,)),
        ],
        compiler_params=pltpu.CompilerParams(vmem_limit_bytes=VMEM_LIMIT),
        cost_estimate=pl.CostEstimate(
            flops=flops,
            bytes_accessed=4 * length * width + 4 * ways * rows * width,
            transcendentals=flops // (4 * HD),
        ),
    )(table, *queries, *arrays)


def table_body(offsets, *refs):
    table = refs[-1]
    for offset, ref in zip(offsets, refs):
        found = ref[...].astype(jnp.float32)
        for part in range(2):
            table[offset + part] = jnp.max(found[part * EXTRA // 2 : (part + 1) * EXTRA // 2]).astype(jnp.int32)


def span_table(blocks, rows):
    offsets = sorted(blocks)
    return pl.pallas_call(
        functools.partial(table_body, offsets),
        out_shape=jax.ShapeDtypeStruct((2 * len(offsets),), jnp.int32),
        grid=(1,),
        in_specs=[
            pl.BlockSpec((EXTRA, 128), functools.partial(lambda row, i: (row, 0), (blocks[i][1] + rows) // EXTRA))
            for i in offsets
        ],
        out_specs=pl.BlockSpec(memory_space=pltpu.SMEM),
        compiler_params=pltpu.CompilerParams(vmem_limit_bytes=VMEM_LIMIT),
    )(*[blocks[i][0] for i in offsets])


def assemble_body(ways, place, *refs):
    for a in range(ways):

        @pl.when(pl.program_id(0) == a)
        def _():
            refs[-1][0] = refs[a][...]


def assemble(pieces, b, before, place):
    ways = len(pieces)
    rows, width = pieces[0].shape
    in_specs = [pl.BlockSpec((rows, width), lambda a, place: (0, 0))] * ways
    operands = list(pieces)
    aliases = {}
    if before is not None:
        in_specs.append(pl.BlockSpec(memory_space=pl.ANY))
        operands.append(before)
        aliases = {1 + ways: 0}
    return pl.pallas_call(
        functools.partial(assemble_body, ways),
        out_shape=jax.ShapeDtypeStruct((2, rows, ways * width), jnp.bfloat16),
        grid_spec=pltpu.PrefetchScalarGridSpec(
            num_scalar_prefetch=1,
            grid=(ways,),
            in_specs=in_specs,
            out_specs=pl.BlockSpec((1, rows, width), lambda a, place: (place[2] ^ b, 0, place[1] ^ a)),
        ),
        input_output_aliases=aliases,
        compiler_params=pltpu.CompilerParams(vmem_limit_bytes=VMEM_LIMIT),
    )(place, *operands)


def on_device(ctx_size, tp_size, hidden_in, w_q, w_k, w_v, event_pos):
    _, rows, _ = hidden_in.shape
    features = w_q.shape[1]
    ways = math.gcd(features // HD, ctx_size // 2)
    rest = ctx_size // ways
    ctx_me = lax.axis_index("ctx").astype(jnp.int32)
    tp_me = lax.axis_index("tp").astype(jnp.int32)
    core = ctx_me % 2
    place = jnp.stack([tp_me, ctx_me // rest, core, ctx_me])
    away = list(range(ways - 1, -1, -1))

    def over_ctx(value, offset):
        return exchange(value, "ctx", ctx_size, offset) if offset else value

    def other_shares(own):
        shares = [own]
        bit = 1
        while bit < tp_size:
            shares += [exchange(share, "tp", tp_size, bit) for share in shares]
            bit *= 2
        return shares[1:]

    mine = lax.dynamic_index_in_dim(hidden_in, core, 0, keepdims=False)
    other = over_ctx(lax.dynamic_index_in_dim(hidden_in, 1 - core, 0, keepdims=False), 1)
    received = [other_shares(mine), other_shares(other)]

    start_k, start_v, start_q = own_products(hidden_in, other, [w_k, w_v, w_q], place, ways)

    spans = event_pos[:, 0] // (rows // 2)
    span_other = over_ctx(lax.dynamic_index_in_dim(spans, 1 - core, 0), 1)
    later = jnp.concatenate([place, lax.dynamic_index_in_dim(spans, core, 0), span_other])
    (made_0,) = rest_products(received, [0], [w_k, w_v], [start_k, start_v], later, ways, away, EXTRA)
    first = {a: over_ctx(made_0[a], a * rest) for a in away}
    ahead = over_ctx(made_0[0], rest // 2)
    asked = rest_products(received, [0], [w_q], [start_q], place, ways, away)
    received, asked = lax.optimization_barrier((received, asked))
    (made_1,) = rest_products(received, [1], [w_k, w_v], [start_k, start_v], place, ways, away)
    ahead_1 = over_ctx(made_1[0], rest // 2)
    received, made_1 = lax.optimization_barrier((received, made_1))
    asked += rest_products(received, [1], [w_q], [start_q], place, ways, away)
    for a in away:
        first[a], asked[1][a] = lax.optimization_barrier((first[a], asked[1][a]))

    second = {}
    queries = [{}, {}]
    for a in away:
        last = (first[a], ahead)
        for made, keep, key in ((made_1, second, a * rest + 1), (asked[0], queries[0], a), (asked[1], queries[1], a)):
            value, last = lax.optimization_barrier((made[a], last))
            last = keep[key] = over_ctx(value, a * rest)
            if keep is second and a:
                last = (last, ahead_1)

    def over_y(blocks):
        bit = rest // 2
        while bit > 1:
            for i in list(blocks):
                if i ^ bit not in blocks:
                    blocks[i ^ bit] = over_ctx(blocks[i], bit)
            bit //= 2
        return blocks

    blocks = {a * rest: first[a] for a in away}
    blocks[rest // 2] = ahead
    blocks = over_y(blocks)
    table = span_table({i: (array, 0) for i, array in blocks.items()}, rows)
    second[rest // 2 + 1] = ahead_1
    blocks.update(over_y(second))
    blocks = {i: (array, 0) for i, array in blocks.items()}
    out = None
    for b in range(2):
        outs = attend(b, [queries[b][a] for a in range(ways)], blocks, table)
        pieces = {a: over_ctx(outs[a], a * rest + b) for a in away}
        out = assemble([pieces[a] for a in range(ways)], b, out, place)
    return out


def solution(mesh):
    sizes = dict(mesh.shape)
    placed = (P(None, "ctx", "tp"), P(None, "tp"), P(None, "tp"), P(None, "tp"), P(None, "ctx"))
    return jax.shard_map(
        functools.partial(on_device, sizes["ctx"], sizes["tp"]),
        mesh=mesh,
        in_specs=placed,
        out_specs=P(None, "ctx", "tp"),
        check_vma=False,
    )
```

```python
import functools
import math

import jax
import jax.numpy as jnp
from jax import lax
from jax.experimental import pallas as pl
from jax.experimental.pallas import tpu as pltpu
from jax.sharding import PartitionSpec as P

HD = 128
LOG2_E = 1.4426950408889634
HIDDEN = -1e30
VMEM_LIMIT = 44 * 2**20
ATTEND_LIMIT = 56 * 2**20


def exchange(value, axis, size, bit):
    return lax.ppermute(value, axis, [(i, i ^ bit) for i in range(size)])


EXTRA = 16


def own_body(weights, place, mine_ref, other_ref, *refs):
    flat_ref = refs[-1]
    rows = other_ref.shape[0]

    @pl.when(pl.program_id(0) == 0)
    def _():
        flat_ref[:rows] = mine_ref[0]
        flat_ref[rows:] = other_ref[...]

    for weight_ref, out_ref in zip(refs[:weights], refs[weights:-1]):
        result = jnp.dot(flat_ref[...], weight_ref[...], preferred_element_type=jnp.float32)
        out_ref[...] = result.reshape(2, rows, -1)


def own_products(hidden_in, other, weights, place, ways):
    rows, feats = other.shape
    features = weights[0].shape[1]
    width = features // ways
    return pl.pallas_call(
        functools.partial(own_body, len(weights)),
        out_shape=[jax.ShapeDtypeStruct((2, rows, features), jnp.float32)] * len(weights),
        grid_spec=pltpu.PrefetchScalarGridSpec(
            num_scalar_prefetch=1,
            grid=(ways,),
            in_specs=[
                pl.BlockSpec((1, rows, feats), lambda g, place: (place[2], 0, 0)),
                pl.BlockSpec((rows, feats), lambda g, place: (0, 0)),
            ]
            + [pl.BlockSpec((feats, width), lambda g, place: (place[0], g))] * len(weights),
            out_specs=[pl.BlockSpec((2, rows, width), lambda g, place: (0, 0, g))] * len(weights),
            scratch_shapes=[pltpu.VMEM((2 * rows, feats), jnp.bfloat16)],
        ),
        compiler_params=pltpu.CompilerParams(vmem_limit_bytes=VMEM_LIMIT),
        cost_estimate=pl.CostEstimate(
            flops=4 * rows * feats * features * len(weights),
            bytes_accessed=2 * feats * features * len(weights),
            transcendentals=0,
        ),
    )(place, hidden_in, other, *weights)


def rest_body(shares, weights, chunks, away, extra, place, *refs):
    inputs = refs[: shares * chunks]
    refs = refs[shares * chunks :]
    weight_refs, refs = refs[: weights * shares], refs[weights * shares :]
    start_refs, refs = refs[:weights], refs[weights:]
    out_refs, flats = refs[: chunks * len(away)], refs[chunks * len(away) :]
    rows, width = out_refs[0].shape
    rows -= extra
    width //= weights
    step = pl.program_id(0)
    if chunks > 1:

        @pl.when(step == 0)
        def _():
            for share in range(shares):
                for c in range(chunks):
                    flats[share][c * rows : (c + 1) * rows] = inputs[c * shares + share][...]

    else:
        flats = inputs
    made = []
    for n in range(weights):
        total = start_refs[n][...].reshape(chunks * rows, width)
        for share in range(shares):
            total += jnp.dot(
                flats[share][...], weight_refs[n * shares + share][...], preferred_element_type=jnp.float32
            )
        made.append(total.astype(jnp.bfloat16))
    for index in range(len(away)):

        @pl.when(step == index)
        def _():
            for c in range(chunks):
                for n in range(weights):
                    out_refs[c * len(away) + index][:rows, n * width : (n + 1) * width] = made[n][
                        c * rows : (c + 1) * rows
                    ]
            if extra:
                line = lax.broadcasted_iota(jnp.int32, (extra, weights * width), 0)
                spans = jnp.where(line < extra // 2, place[4], place[5]).astype(jnp.float32)
                out_refs[index][rows:] = spans.astype(jnp.bfloat16)


def rest_products(received, chosen, weights, starts, place, ways, away, extra=0):
    shares = len(received[0])
    rows, feats = received[0][0].shape
    width = weights[0].shape[1] // ways
    chunks = len(chosen)
    top = away[0]
    stride = away[1] - top if len(away) > 1 else 0

    def weight_map(share, i, place):
        return (place[0] ^ (share + 1), place[1] ^ (top + stride * i))

    in_specs = [pl.BlockSpec((rows, feats), lambda i, place: (0, 0))] * (shares * chunks)
    for _ in weights:
        for share in range(shares):
            in_specs.append(pl.BlockSpec((feats, width), functools.partial(weight_map, share)))
    in_specs += [
        pl.BlockSpec((chunks, rows, width), lambda i, place: (chosen[0] // chunks, 0, place[1] ^ (top + stride * i)))
    ] * len(weights)
    columns = width * len(weights)
    scratch = [pltpu.VMEM((chunks * rows, feats), jnp.bfloat16)] * (shares if chunks > 1 else 0)
    outs = pl.pallas_call(
        functools.partial(rest_body, shares, len(weights), chunks, away, extra),
        out_shape=[jax.ShapeDtypeStruct((rows + extra, columns), jnp.bfloat16)] * (chunks * len(away)),
        grid_spec=pltpu.PrefetchScalarGridSpec(
            num_scalar_prefetch=1,
            grid=(len(away),),
            in_specs=in_specs,
            out_specs=[pl.BlockSpec((rows + extra, columns), lambda i, place: (0, 0))] * (chunks * len(away)),
            scratch_shapes=scratch,
        ),
        compiler_params=pltpu.CompilerParams(vmem_limit_bytes=VMEM_LIMIT),
        cost_estimate=pl.CostEstimate(
            flops=2 * chunks * rows * feats * shares * columns * len(away),
            bytes_accessed=2 * feats * shares * columns * len(away),
            transcendentals=0,
        ),
    )(
        place,
        *[share for c in chosen for share in received[c]],
        *[weight for weight in weights for _ in range(shares)],
        *starts,
    )
    return [dict(zip(away, outs[c * len(away) : (c + 1) * len(away)])) for c in range(chunks)]


def attend_body(block, ways, slots, arrays, spans, tile, table, *refs):
    count = len(slots)
    query_refs = refs[:ways]
    block_refs = refs[ways : ways + arrays]
    out_refs = refs[ways + arrays : 2 * ways + arrays]
    ordered, asked, scores, highest, sums, total, position, sems = refs[2 * ways + arrays :]
    rows, width = out_refs[0].shape
    half = rows // 2
    heads = width // HD
    rest = count // ways

    copies = [[], []]
    for slot, (offset, array, row) in enumerate(slots):
        low = table[offset]
        for part, span in ((0, low), (1, spans - 1 - low)):
            copies[part].append(
                pltpu.make_async_copy(
                    block_refs[array].at[pl.ds(row + part * half, half)],
                    ordered.at[pl.ds(pl.multiple_of(span * half, 16), half)],
                    sems.at[2 * slot + part],
                )
            )
    for copy in copies[0] + copies[1]:
        copy.start()

    many = ways * half
    from_lane = lax.broadcasted_iota(jnp.int32, (half, 128), 0) - lax.broadcasted_iota(
        jnp.int32, (half, 128), 1
    )
    for a in range(ways):
        low = table[a * rest + block]
        for part, span in ((0, low), (1, spans - 1 - low)):
            here = slice(part * many + a * half, part * many + (a + 1) * half)
            asked[here] = query_refs[a][part * half : (part + 1) * half]
            position[here] = from_lane + span * half
    for copy in copies[0]:
        copy.wait()

    slope = LOG2_E / math.sqrt(HD)
    middle = spans * half // 2
    starts = range(0, 2 * middle, tile)

    def first_row(start):
        return 0 if start < middle else many

    def visible(slot, column):
        piece = scores[slot, first_row(column) :, column : column + 128]
        if column >= middle:
            return jnp.where(position[many:] >= column, piece, HIDDEN)
        masked = jnp.where(position[:many] >= column, piece[:many], HIDDEN)
        return jnp.concatenate([masked, piece[many:]], axis=0)

    def score_tile(h, slot, start):
        first = first_row(start)
        scores[slot, first:, start : start + tile] = lax.dot_general(
            asked[first:, h * HD : (h + 1) * HD],
            ordered[start : start + tile, h * HD : (h + 1) * HD],
            (((1,), (1,)), ((), ())),
            preferred_element_type=jnp.float32,
        )
        top = None if start == 0 else highest[slot, first:]
        for column in range(start, start + tile, 128):
            piece = visible(slot, column)
            top = piece if top is None else jnp.maximum(top, piece)
        highest[slot, first:] = top

    def value_tile(h, slot, start):
        first = first_row(start)
        top = highest[slot, first:]
        added = None if start == 0 else sums[slot, first:]
        weights = []
        for column in range(start, start + tile, 128):
            piece = jnp.exp2((visible(slot, column) - top) * slope)
            added = piece if added is None else added + piece
            weights.append(piece.astype(jnp.bfloat16))
        sums[slot, first:] = added
        product = jnp.dot(
            jnp.concatenate(weights, axis=1),
            ordered[start : start + tile, width + h * HD : width + (h + 1) * HD],
            preferred_element_type=jnp.float32,
        )
        if start == 0:
            total[slot] = product
        else:
            total[slot, first:] += product

    for n in range(heads + 1):
        slot = (n - 1) % 2
        if n > 0:
            highest[slot] = jnp.broadcast_to(jnp.max(highest[slot], axis=1, keepdims=True), highest.shape[1:])
        for start in starts:
            if n == 0 and start == middle:
                for copy in copies[1]:
                    copy.wait()
            if n < heads:
                score_tile(n, n % 2, start)
            if n > 0:
                value_tile(n - 1, slot, start)
        if n > 0:
            result = total[slot] / jnp.sum(sums[slot], axis=1, keepdims=True)
            result = result.astype(jnp.bfloat16)
            for a in range(ways):
                for part in range(2):
                    out_refs[a][part * half : (part + 1) * half, (n - 1) * HD : n * HD] = result[
                        part * many + a * half : part * many + (a + 1) * half
                    ]


def attend(block, queries, blocks, table):
    rows, width = queries[0].shape
    ways, count = len(queries), len(blocks)
    arrays = []
    slots = []
    for offset in sorted(blocks):
        array, row = blocks[offset]
        if not any(array is other for other in arrays):
            arrays.append(array)
        slots.append((offset, [array is other for other in arrays].index(True), row))
    spans = 2 * count
    half = rows // 2
    length = count * rows
    tile = 8 * half
    heads = width // HD
    many = ways * half
    smem = pl.BlockSpec(memory_space=pltpu.SMEM)
    flops = 6 * many * heads * length * HD
    return pl.pallas_call(
        functools.partial(attend_body, block, ways, slots, len(arrays), spans, tile),
        out_shape=[jax.ShapeDtypeStruct((rows, width), jnp.bfloat16)] * ways,
        grid=(1,),
        in_specs=[smem]
        + [pl.BlockSpec((rows, width), lambda i: (0, 0))] * ways
        + [pl.BlockSpec(memory_space=pl.ANY)] * len(arrays),
        out_specs=[pl.BlockSpec((rows, width), lambda i: (0, 0))] * ways,
        scratch_shapes=[
            pltpu.VMEM((length, 2 * width), jnp.bfloat16),
            pltpu.VMEM((2 * many, width), jnp.bfloat16),
            pltpu.VMEM((2, 2 * many, length), jnp.float32),
            pltpu.VMEM((2, 2 * many, 128), jnp.float32),
            pltpu.VMEM((2, 2 * many, 128), jnp.float32),
            pltpu.VMEM((2, 2 * many, HD), jnp.float32),
            pltpu.VMEM((2 * many, 128), jnp.int32),
            pltpu.SemaphoreType.DMA((2 * count,)),
        ],
        compiler_params=pltpu.CompilerParams(vmem_limit_bytes=ATTEND_LIMIT),
        cost_estimate=pl.CostEstimate(
            flops=flops,
            bytes_accessed=4 * length * width + 4 * ways * rows * width,
            transcendentals=flops // (4 * HD),
        ),
    )(table, *queries, *arrays)


def table_body(offsets, *refs):
    table = refs[-1]
    for offset, ref in zip(offsets, refs):
        found = ref[...].astype(jnp.float32)
        for part in range(2):
            table[offset + part] = jnp.max(found[part * EXTRA // 2 : (part + 1) * EXTRA // 2]).astype(jnp.int32)


def span_table(blocks, rows):
    offsets = sorted(blocks)
    return pl.pallas_call(
        functools.partial(table_body, offsets),
        out_shape=jax.ShapeDtypeStruct((2 * len(offsets),), jnp.int32),
        grid=(1,),
        in_specs=[
            pl.BlockSpec((EXTRA, 128), functools.partial(lambda row, i: (row, 0), (blocks[i][1] + rows) // EXTRA))
            for i in offsets
        ],
        out_specs=pl.BlockSpec(memory_space=pltpu.SMEM),
        compiler_params=pltpu.CompilerParams(vmem_limit_bytes=VMEM_LIMIT),
    )(*[blocks[i][0] for i in offsets])


def assemble_body(ways, place, *refs):
    for a in range(ways):

        @pl.when(pl.program_id(0) == a)
        def _():
            refs[-1][0] = refs[a][...]


def assemble(pieces, b, before, place):
    ways = len(pieces)
    rows, width = pieces[0].shape
    in_specs = [pl.BlockSpec((rows, width), lambda a, place: (0, 0))] * ways
    operands = list(pieces)
    aliases = {}
    if before is not None:
        in_specs.append(pl.BlockSpec(memory_space=pl.ANY))
        operands.append(before)
        aliases = {1 + ways: 0}
    return pl.pallas_call(
        functools.partial(assemble_body, ways),
        out_shape=jax.ShapeDtypeStruct((2, rows, ways * width), jnp.bfloat16),
        grid_spec=pltpu.PrefetchScalarGridSpec(
            num_scalar_prefetch=1,
            grid=(ways,),
            in_specs=in_specs,
            out_specs=pl.BlockSpec((1, rows, width), lambda a, place: (place[2] ^ b, 0, place[1] ^ a)),
        ),
        input_output_aliases=aliases,
        compiler_params=pltpu.CompilerParams(vmem_limit_bytes=VMEM_LIMIT),
    )(place, *operands)


def on_device(ctx_size, tp_size, hidden_in, w_q, w_k, w_v, event_pos):
    _, rows, _ = hidden_in.shape
    features = w_q.shape[1]
    ways = math.gcd(features // HD, ctx_size // 2)
    rest = ctx_size // ways
    ctx_me = lax.axis_index("ctx").astype(jnp.int32)
    tp_me = lax.axis_index("tp").astype(jnp.int32)
    core = ctx_me % 2
    place = jnp.stack([tp_me, ctx_me // rest, core, ctx_me])
    away = list(range(ways - 1, -1, -1))

    def over_ctx(value, offset):
        return exchange(value, "ctx", ctx_size, offset) if offset else value

    def other_shares(own):
        shares = [own]
        bit = 1
        while bit < tp_size:
            shares += [exchange(share, "tp", tp_size, bit) for share in shares]
            bit *= 2
        return shares[1:]

    mine = lax.dynamic_index_in_dim(hidden_in, core, 0, keepdims=False)
    other = over_ctx(lax.dynamic_index_in_dim(hidden_in, 1 - core, 0, keepdims=False), 1)
    received = [other_shares(mine), other_shares(other)]

    start_k, start_v, start_q = own_products(hidden_in, other, [w_k, w_v, w_q], place, ways)

    spans = event_pos[:, 0] // (rows // 2)
    span_other = over_ctx(lax.dynamic_index_in_dim(spans, 1 - core, 0), 1)
    later = jnp.concatenate([place, lax.dynamic_index_in_dim(spans, core, 0), span_other])
    (made_0,) = rest_products(received, [0], [w_k, w_v], [start_k, start_v], later, ways, away, EXTRA)
    first = {a: over_ctx(made_0[a], a * rest) for a in away}
    ahead = over_ctx(made_0[0], rest // 2)
    asked = rest_products(received, [0], [w_q], [start_q], place, ways, away)
    received, asked = lax.optimization_barrier((received, asked))
    (made_1,) = rest_products(received, [1], [w_k, w_v], [start_k, start_v], place, ways, away)
    ahead_1 = over_ctx(made_1[0], rest // 2)
    received, made_1 = lax.optimization_barrier((received, made_1))
    asked += rest_products(received, [1], [w_q], [start_q], place, ways, away)
    for a in away:
        first[a], asked[1][a] = lax.optimization_barrier((first[a], asked[1][a]))

    second = {}
    queries = [{}, {}]
    for a in away:
        last = (first[a], ahead)
        for made, keep, key in ((made_1, second, a * rest + 1), (asked[0], queries[0], a), (asked[1], queries[1], a)):
            value, last = lax.optimization_barrier((made[a], last))
            last = keep[key] = over_ctx(value, a * rest)
            if keep is second and a:
                last = (last, ahead_1)

    def over_y(blocks):
        bit = rest // 2
        while bit > 1:
            for i in list(blocks):
                if i ^ bit not in blocks:
                    blocks[i ^ bit] = over_ctx(blocks[i], bit)
            bit //= 2
        return blocks

    blocks = {a * rest: first[a] for a in away}
    blocks[rest // 2] = ahead
    blocks = over_y(blocks)
    table = span_table({i: (array, 0) for i, array in blocks.items()}, rows)
    second[rest // 2 + 1] = ahead_1
    blocks.update(over_y(second))
    blocks = {i: (array, 0) for i, array in blocks.items()}
    out = None
    for b in range(2):
        outs = attend(b, [queries[b][a] for a in range(ways)], blocks, table)
        pieces = {a: over_ctx(outs[a], a * rest + b) for a in away}
        out = assemble([pieces[a] for a in range(ways)], b, out, place)
    return out


def solution(mesh):
    sizes = dict(mesh.shape)
    placed = (P(None, "ctx", "tp"), P(None, "tp"), P(None, "tp"), P(None, "tp"), P(None, "ctx"))
    return jax.shard_map(
        functools.partial(on_device, sizes["ctx"], sizes["tp"]),
        mesh=mesh,
        in_specs=placed,
        out_specs=P(None, "ctx", "tp"),
        check_vma=False,
    )
```

```python
import functools
import math

import jax
import jax.numpy as jnp
from jax import lax
from jax.experimental import pallas as pl
from jax.experimental.pallas import tpu as pltpu
from jax.sharding import PartitionSpec as P

HD = 128
LOG2_E = 1.4426950408889634
HIDDEN = -1e30
VMEM_LIMIT = 44 * 2**20
ATTEND_LIMIT = 56 * 2**20


def exchange(value, axis, size, bit):
    return lax.ppermute(value, axis, [(i, i ^ bit) for i in range(size)])


EXTRA = 16


def own_body(weights, place, mine_ref, other_ref, *refs):
    flat_ref = refs[-1]
    rows = other_ref.shape[0]

    @pl.when(pl.program_id(0) == 0)
    def _():
        flat_ref[:rows] = mine_ref[0]
        flat_ref[rows:] = other_ref[...]

    for weight_ref, out_ref in zip(refs[:weights], refs[weights:-1]):
        result = jnp.dot(flat_ref[...], weight_ref[...], preferred_element_type=jnp.float32)
        out_ref[...] = result.reshape(2, rows, -1)


def own_products(hidden_in, other, weights, place, ways):
    rows, feats = other.shape
    features = weights[0].shape[1]
    width = features // ways
    return pl.pallas_call(
        functools.partial(own_body, len(weights)),
        out_shape=[jax.ShapeDtypeStruct((2, rows, features), jnp.float32)] * len(weights),
        grid_spec=pltpu.PrefetchScalarGridSpec(
            num_scalar_prefetch=1,
            grid=(ways,),
            in_specs=[
                pl.BlockSpec((1, rows, feats), lambda g, place: (place[2], 0, 0)),
                pl.BlockSpec((rows, feats), lambda g, place: (0, 0)),
            ]
            + [pl.BlockSpec((feats, width), lambda g, place: (place[0], g))] * len(weights),
            out_specs=[pl.BlockSpec((2, rows, width), lambda g, place: (0, 0, g))] * len(weights),
            scratch_shapes=[pltpu.VMEM((2 * rows, feats), jnp.bfloat16)],
        ),
        compiler_params=pltpu.CompilerParams(vmem_limit_bytes=VMEM_LIMIT),
        cost_estimate=pl.CostEstimate(
            flops=4 * rows * feats * features * len(weights),
            bytes_accessed=2 * feats * features * len(weights),
            transcendentals=0,
        ),
    )(place, hidden_in, other, *weights)


def rest_body(shares, weights, chunks, away, extra, place, *refs):
    inputs = refs[: shares * chunks]
    refs = refs[shares * chunks :]
    weight_refs, refs = refs[: weights * shares], refs[weights * shares :]
    start_refs, refs = refs[:weights], refs[weights:]
    out_refs, flats = refs[: chunks * len(away)], refs[chunks * len(away) :]
    rows, width = out_refs[0].shape
    rows -= extra
    width //= weights
    step = pl.program_id(0)
    if chunks > 1:

        @pl.when(step == 0)
        def _():
            for share in range(shares):
                for c in range(chunks):
                    flats[share][c * rows : (c + 1) * rows] = inputs[c * shares + share][...]

    else:
        flats = inputs
    made = []
    for n in range(weights):
        total = start_refs[n][...].reshape(chunks * rows, width)
        for share in range(shares):
            total += jnp.dot(
                flats[share][...], weight_refs[n * shares + share][...], preferred_element_type=jnp.float32
            )
        made.append(total.astype(jnp.bfloat16))
    for index in range(len(away)):

        @pl.when(step == index)
        def _():
            for c in range(chunks):
                for n in range(weights):
                    out_refs[c * len(away) + index][:rows, n * width : (n + 1) * width] = made[n][
                        c * rows : (c + 1) * rows
                    ]
            if extra:
                line = lax.broadcasted_iota(jnp.int32, (extra, weights * width), 0)
                spans = jnp.where(line < extra // 2, place[4], place[5]).astype(jnp.float32)
                out_refs[index][rows:] = spans.astype(jnp.bfloat16)


def rest_products(received, chosen, weights, starts, place, ways, away, extra=0):
    shares = len(received[0])
    rows, feats = received[0][0].shape
    width = weights[0].shape[1] // ways
    chunks = len(chosen)
    top = away[0]
    stride = away[1] - top if len(away) > 1 else 0

    def weight_map(share, i, place):
        return (place[0] ^ (share + 1), place[1] ^ (top + stride * i))

    in_specs = [pl.BlockSpec((rows, feats), lambda i, place: (0, 0))] * (shares * chunks)
    for _ in weights:
        for share in range(shares):
            in_specs.append(pl.BlockSpec((feats, width), functools.partial(weight_map, share)))
    in_specs += [
        pl.BlockSpec((chunks, rows, width), lambda i, place: (chosen[0] // chunks, 0, place[1] ^ (top + stride * i)))
    ] * len(weights)
    columns = width * len(weights)
    scratch = [pltpu.VMEM((chunks * rows, feats), jnp.bfloat16)] * (shares if chunks > 1 else 0)
    outs = pl.pallas_call(
        functools.partial(rest_body, shares, len(weights), chunks, away, extra),
        out_shape=[jax.ShapeDtypeStruct((rows + extra, columns), jnp.bfloat16)] * (chunks * len(away)),
        grid_spec=pltpu.PrefetchScalarGridSpec(
            num_scalar_prefetch=1,
            grid=(len(away),),
            in_specs=in_specs,
            out_specs=[pl.BlockSpec((rows + extra, columns), lambda i, place: (0, 0))] * (chunks * len(away)),
            scratch_shapes=scratch,
        ),
        compiler_params=pltpu.CompilerParams(vmem_limit_bytes=VMEM_LIMIT),
        cost_estimate=pl.CostEstimate(
            flops=2 * chunks * rows * feats * shares * columns * len(away),
            bytes_accessed=2 * feats * shares * columns * len(away),
            transcendentals=0,
        ),
    )(
        place,
        *[share for c in chosen for share in received[c]],
        *[weight for weight in weights for _ in range(shares)],
        *starts,
    )
    return [dict(zip(away, outs[c * len(away) : (c + 1) * len(away)])) for c in range(chunks)]


def attend_body(block, ways, slots, arrays, spans, tile, table, *refs):
    count = len(slots)
    query_refs = refs[:ways][::-1]
    block_refs = refs[ways : ways + arrays]
    out_refs = refs[ways + arrays : 2 * ways + arrays]
    ordered, asked, scores, highest, sums, total, position, sems = refs[2 * ways + arrays :]
    rows, width = out_refs[0].shape
    half = rows // 2
    heads = width // HD
    rest = count // ways

    copies = [[], []]
    for slot, (offset, array, row) in enumerate(slots):
        low = table[offset]
        for part, span in ((0, low), (1, spans - 1 - low)):
            copies[part].append(
                pltpu.make_async_copy(
                    block_refs[array].at[pl.ds(row + part * half, half)],
                    ordered.at[pl.ds(pl.multiple_of(span * half, 16), half)],
                    sems.at[2 * slot + part],
                )
            )
    for copy in copies[0] + copies[1]:
        copy.start()

    from_lane = lax.broadcasted_iota(jnp.int32, (half, 128), 0) - lax.broadcasted_iota(
        jnp.int32, (half, 128), 1
    )
    for a in range(ways):
        low = table[a * rest + block]
        here = slice(a * half, (a + 1) * half)
        for part, span in ((0, low), (1, spans - 1 - low)):
            asked[part, here] = query_refs[a][part * half : (part + 1) * half]
            position[part, here] = from_lane + span * half
    for copy in copies[0]:
        copy.wait()

    slope = LOG2_E / math.sqrt(HD)
    middle = spans * half // 2

    def starts(part):
        return range(0, middle * (part + 1), tile)

    def visible(unit, slot, column):
        piece = scores[slot, :, column : column + 128]
        if column < middle * unit[0]:
            return piece
        return jnp.where(position[unit[0]] >= column, piece, HIDDEN)

    def score_tile(unit, slot, start):
        part, h = unit
        if unit == (1, 0) and start == middle:
            for copy in copies[1]:
                copy.wait()
        scores[slot, :, start : start + tile] = lax.dot_general(
            asked[part, :, h * HD : (h + 1) * HD],
            ordered[start : start + tile, h * HD : (h + 1) * HD],
            (((1,), (1,)), ((), ())),
            preferred_element_type=jnp.float32,
        )
        top = None if start == 0 else highest[slot]
        for column in range(start, start + tile, 128):
            piece = visible(unit, slot, column)
            top = piece if top is None else jnp.maximum(top, piece)
        highest[slot] = top

    def value_tile(unit, slot, start):
        part, h = unit
        top = highest[slot]
        added = None if start == 0 else sums[slot]
        weights = []
        for column in range(start, start + tile, 128):
            piece = jnp.exp2((visible(unit, slot, column) - top) * slope)
            added = piece if added is None else added + piece
            weights.append(piece.astype(jnp.bfloat16))
        sums[slot] = added
        product = jnp.dot(
            jnp.concatenate(weights, axis=1),
            ordered[start : start + tile, width + h * HD : width + (h + 1) * HD],
            preferred_element_type=jnp.float32,
        )
        if start == 0:
            total[slot] = product
        else:
            total[slot] += product

    units = [(0, 0)] + [(1, h) for h in range(heads)] + [(0, h) for h in range(1, heads)]
    for n in range(len(units) + 1):
        todo = []
        if n < len(units):
            todo.append([functools.partial(score_tile, units[n], n % 2, start) for start in starts(units[n][0])])
        if n > 0:
            slot = (n - 1) % 2
            highest[slot] = jnp.broadcast_to(jnp.max(highest[slot], axis=1, keepdims=True), highest.shape[1:])
            todo.append([functools.partial(value_tile, units[n - 1], slot, start) for start in starts(units[n - 1][0])])
        for index in range(max(len(steps) for steps in todo)):
            for steps in todo:
                if index < len(steps):
                    steps[index]()
        if n > 0:
            part, h = units[n - 1]
            result = total[slot] / jnp.sum(sums[slot], axis=1, keepdims=True)
            for a in range(ways):
                out_refs[a][part * half : (part + 1) * half, h * HD : (h + 1) * HD] = result[
                    a * half : (a + 1) * half
                ].astype(jnp.bfloat16)


def attend(block, queries, blocks, table):
    rows, width = queries[0].shape
    ways, count = len(queries), len(blocks)
    arrays = []
    slots = []
    for offset in sorted(blocks, reverse=True):
        array, row = blocks[offset]
        if not any(array is other for other in arrays):
            arrays.append(array)
        slots.append((offset, [array is other for other in arrays].index(True), row))
    spans = 2 * count
    half = rows // 2
    length = count * rows
    tile = 8 * half
    heads = width // HD
    many = ways * half
    smem = pl.BlockSpec(memory_space=pltpu.SMEM)
    flops = 6 * many * heads * length * HD
    return pl.pallas_call(
        functools.partial(attend_body, block, ways, slots, len(arrays), spans, tile),
        out_shape=[jax.ShapeDtypeStruct((rows, width), jnp.bfloat16)] * ways,
        grid=(1,),
        in_specs=[smem]
        + [pl.BlockSpec((rows, width), lambda i: (0, 0))] * ways
        + [pl.BlockSpec(memory_space=pl.ANY)] * len(arrays),
        out_specs=[pl.BlockSpec((rows, width), lambda i: (0, 0))] * ways,
        scratch_shapes=[
            pltpu.VMEM((length, 2 * width), jnp.bfloat16),
            pltpu.VMEM((2, many, width), jnp.bfloat16),
            pltpu.VMEM((2, many, length), jnp.float32),
            pltpu.VMEM((2, many, 128), jnp.float32),
            pltpu.VMEM((2, many, 128), jnp.float32),
            pltpu.VMEM((2, many, HD), jnp.float32),
            pltpu.VMEM((2, many, 128), jnp.int32),
            pltpu.SemaphoreType.DMA((2 * count,)),
        ],
        compiler_params=pltpu.CompilerParams(vmem_limit_bytes=ATTEND_LIMIT),
        cost_estimate=pl.CostEstimate(
            flops=flops,
            bytes_accessed=4 * length * width + 4 * ways * rows * width,
            transcendentals=flops // (4 * HD),
        ),
    )(table, *queries[::-1], *arrays)


def table_body(offsets, *refs):
    table = refs[-1]
    for offset, ref in zip(offsets, refs):
        found = ref[...].astype(jnp.float32)
        for part in range(2):
            table[offset + part] = jnp.max(found[part * EXTRA // 2 : (part + 1) * EXTRA // 2]).astype(jnp.int32)


def span_table(blocks, rows):
    offsets = sorted(blocks, reverse=True)
    return pl.pallas_call(
        functools.partial(table_body, offsets),
        out_shape=jax.ShapeDtypeStruct((2 * len(offsets),), jnp.int32),
        grid=(1,),
        in_specs=[
            pl.BlockSpec((EXTRA, 128), functools.partial(lambda row, i: (row, 0), (blocks[i][1] + rows) // EXTRA))
            for i in offsets
        ],
        out_specs=pl.BlockSpec(memory_space=pltpu.SMEM),
        compiler_params=pltpu.CompilerParams(vmem_limit_bytes=VMEM_LIMIT),
    )(*[blocks[i][0] for i in offsets])


def assemble_body(ways, place, *refs):
    for a in range(ways):

        @pl.when(pl.program_id(0) == a)
        def _():
            refs[-1][0] = refs[ways - 1 - a][...]


def assemble(pieces, b, before, place):
    ways = len(pieces)
    rows, width = pieces[0].shape
    in_specs = [pl.BlockSpec((rows, width), lambda a, place: (0, 0))] * ways
    operands = list(pieces[::-1])
    aliases = {}
    if before is not None:
        in_specs.append(pl.BlockSpec(memory_space=pl.ANY))
        operands.append(before)
        aliases = {1 + ways: 0}
    return pl.pallas_call(
        functools.partial(assemble_body, ways),
        out_shape=jax.ShapeDtypeStruct((2, rows, ways * width), jnp.bfloat16),
        grid_spec=pltpu.PrefetchScalarGridSpec(
            num_scalar_prefetch=1,
            grid=(ways,),
            in_specs=in_specs,
            out_specs=pl.BlockSpec((1, rows, width), lambda a, place: (place[2] ^ b, 0, place[1] ^ a)),
        ),
        input_output_aliases=aliases,
        compiler_params=pltpu.CompilerParams(vmem_limit_bytes=VMEM_LIMIT),
    )(place, *operands)


def on_device(ctx_size, tp_size, hidden_in, w_q, w_k, w_v, event_pos):
    _, rows, _ = hidden_in.shape
    features = w_q.shape[1]
    ways = math.gcd(features // HD, ctx_size // 2)
    rest = ctx_size // ways
    ctx_me = lax.axis_index("ctx").astype(jnp.int32)
    tp_me = lax.axis_index("tp").astype(jnp.int32)
    core = ctx_me % 2
    place = jnp.stack([tp_me, ctx_me // rest, core, ctx_me])
    away = list(range(ways))

    def over_ctx(value, offset):
        return exchange(value, "ctx", ctx_size, offset) if offset else value

    def other_shares(own):
        shares = [own]
        bit = 1
        while bit < tp_size:
            shares += [exchange(share, "tp", tp_size, bit) for share in shares]
            bit *= 2
        return shares[1:]

    mine = lax.dynamic_index_in_dim(hidden_in, core, 0, keepdims=False)
    other = over_ctx(lax.dynamic_index_in_dim(hidden_in, 1 - core, 0, keepdims=False), 1)
    received = [other_shares(mine), other_shares(other)]

    start_k, start_v, start_q = own_products(hidden_in, other, [w_k, w_v, w_q], place, ways)

    spans = event_pos[:, 0] // (rows // 2)
    span_other = over_ctx(lax.dynamic_index_in_dim(spans, 1 - core, 0), 1)
    later = jnp.concatenate([place, lax.dynamic_index_in_dim(spans, core, 0), span_other])
    (made_0,) = rest_products(received, [0], [w_k, w_v], [start_k, start_v], later, ways, away, EXTRA)
    first = {a: over_ctx(made_0[a], a * rest) for a in away}
    ahead = over_ctx(made_0[0], rest // 2)
    asked = rest_products(received, [0], [w_q], [start_q], place, ways, away)
    received, asked = lax.optimization_barrier((received, asked))
    (made_1,) = rest_products(received, [1], [w_k, w_v], [start_k, start_v], place, ways, away)
    ahead_1 = over_ctx(made_1[0], rest // 2)
    for a in away:
        first[a], made_1[a] = lax.optimization_barrier((first[a], made_1[a]))
    received, ahead_1 = lax.optimization_barrier((received, ahead_1))
    asked += rest_products(received, [1], [w_q], [start_q], place, ways, away)

    second = {}
    queries = [{}, {}]
    for a in away:
        last = (first[a], ahead)
        for made, keep, key in ((made_1, second, a * rest + 1), (asked[0], queries[0], a), (asked[1], queries[1], a)):
            value, last = lax.optimization_barrier((made[a], last))
            last = keep[key] = over_ctx(value, a * rest)
            if keep is second and a:
                last = (last, ahead_1)

    def over_y(blocks):
        bit = rest // 2
        while bit > 1:
            for i in list(blocks):
                if i ^ bit not in blocks:
                    blocks[i ^ bit] = over_ctx(blocks[i], bit)
            bit //= 2
        return blocks

    blocks = {a * rest: first[a] for a in away}
    blocks[rest // 2] = ahead
    blocks = over_y(blocks)
    table = span_table({i: (array, 0) for i, array in blocks.items()}, rows)
    second[rest // 2 + 1] = ahead_1
    blocks.update(over_y(second))
    blocks = {i: (array, 0) for i, array in blocks.items()}
    out = None
    for b in range(2):
        outs = attend(b, [queries[b][a] for a in range(ways)], blocks, table)
        pieces = {a: over_ctx(outs[a], a * rest + b) for a in away}
        out = assemble([pieces[a] for a in range(ways)], b, out, place)
    return out


def solution(mesh):
    sizes = dict(mesh.shape)
    placed = (P(None, "ctx", "tp"), P(None, "tp"), P(None, "tp"), P(None, "tp"), P(None, "ctx"))
    return jax.shard_map(
        functools.partial(on_device, sizes["ctx"], sizes["tp"]),
        mesh=mesh,
        in_specs=placed,
        out_specs=P(None, "ctx", "tp"),
        check_vma=False,
    )
```

```python
import functools
import math

import jax
import jax.numpy as jnp
from jax import lax
from jax.experimental import pallas as pl
from jax.experimental.pallas import tpu as pltpu
from jax.sharding import PartitionSpec as P

HD = 128
LOG2_E = 1.4426950408889634
HIDDEN = -1e30
VMEM_LIMIT = 44 * 2**20
ATTEND_LIMIT = 56 * 2**20


def exchange(value, axis, size, bit):
    return lax.ppermute(value, axis, [(i, i ^ bit) for i in range(size)])


EXTRA = 16


def own_body(weights, place, mine_ref, other_ref, *refs):
    flat_ref = refs[-1]
    rows = other_ref.shape[0]

    @pl.when(pl.program_id(0) == 0)
    def _():
        flat_ref[:rows] = mine_ref[0]
        flat_ref[rows:] = other_ref[...]

    for weight_ref, out_ref in zip(refs[:weights], refs[weights:-1]):
        result = jnp.dot(flat_ref[...], weight_ref[...], preferred_element_type=jnp.float32)
        out_ref[...] = result.reshape(2, rows, -1)


def own_products(hidden_in, other, weights, place, ways):
    rows, feats = other.shape
    features = weights[0].shape[1]
    width = features // ways
    return pl.pallas_call(
        functools.partial(own_body, len(weights)),
        out_shape=[jax.ShapeDtypeStruct((2, rows, features), jnp.float32)] * len(weights),
        grid_spec=pltpu.PrefetchScalarGridSpec(
            num_scalar_prefetch=1,
            grid=(ways,),
            in_specs=[
                pl.BlockSpec((1, rows, feats), lambda g, place: (place[2], 0, 0)),
                pl.BlockSpec((rows, feats), lambda g, place: (0, 0)),
            ]
            + [pl.BlockSpec((feats, width), lambda g, place: (place[0], g))] * len(weights),
            out_specs=[pl.BlockSpec((2, rows, width), lambda g, place: (0, 0, g))] * len(weights),
            scratch_shapes=[pltpu.VMEM((2 * rows, feats), jnp.bfloat16)],
        ),
        compiler_params=pltpu.CompilerParams(vmem_limit_bytes=VMEM_LIMIT),
        cost_estimate=pl.CostEstimate(
            flops=4 * rows * feats * features * len(weights),
            bytes_accessed=2 * feats * features * len(weights),
            transcendentals=0,
        ),
    )(place, hidden_in, other, *weights)


def rest_body(shares, weights, chunks, away, extra, place, *refs):
    inputs = refs[: shares * chunks]
    refs = refs[shares * chunks :]
    weight_refs, refs = refs[: weights * shares], refs[weights * shares :]
    start_refs, refs = refs[:weights], refs[weights:]
    out_refs, flats = refs[: chunks * len(away)], refs[chunks * len(away) :]
    rows, width = out_refs[0].shape
    rows -= extra
    width //= weights
    step = pl.program_id(0)
    if chunks > 1:

        @pl.when(step == 0)
        def _():
            for share in range(shares):
                for c in range(chunks):
                    flats[share][c * rows : (c + 1) * rows] = inputs[c * shares + share][...]

    else:
        flats = inputs
    made = []
    for n in range(weights):
        total = start_refs[n][...].reshape(chunks * rows, width)
        for share in range(shares):
            total += jnp.dot(
                flats[share][...], weight_refs[n * shares + share][...], preferred_element_type=jnp.float32
            )
        made.append(total.astype(jnp.bfloat16))
    for index in range(len(away)):

        @pl.when(step == index)
        def _():
            for c in range(chunks):
                for n in range(weights):
                    out_refs[c * len(away) + index][:rows, n * width : (n + 1) * width] = made[n][
                        c * rows : (c + 1) * rows
                    ]
            if extra:
                line = lax.broadcasted_iota(jnp.int32, (extra, weights * width), 0)
                spans = jnp.where(line < extra // 2, place[4], place[5]).astype(jnp.float32)
                out_refs[index][rows:] = spans.astype(jnp.bfloat16)


def rest_products(received, chosen, weights, starts, place, ways, away, extra=0):
    shares = len(received[0])
    rows, feats = received[0][0].shape
    width = weights[0].shape[1] // ways
    chunks = len(chosen)
    top = away[0]
    stride = away[1] - top if len(away) > 1 else 0

    def weight_map(share, i, place):
        return (place[0] ^ (share + 1), place[1] ^ (top + stride * i))

    in_specs = [pl.BlockSpec((rows, feats), lambda i, place: (0, 0))] * (shares * chunks)
    for _ in weights:
        for share in range(shares):
            in_specs.append(pl.BlockSpec((feats, width), functools.partial(weight_map, share)))
    in_specs += [
        pl.BlockSpec((chunks, rows, width), lambda i, place: (chosen[0] // chunks, 0, place[1] ^ (top + stride * i)))
    ] * len(weights)
    columns = width * len(weights)
    scratch = [pltpu.VMEM((chunks * rows, feats), jnp.bfloat16)] * (shares if chunks > 1 else 0)
    outs = pl.pallas_call(
        functools.partial(rest_body, shares, len(weights), chunks, away, extra),
        out_shape=[jax.ShapeDtypeStruct((rows + extra, columns), jnp.bfloat16)] * (chunks * len(away)),
        grid_spec=pltpu.PrefetchScalarGridSpec(
            num_scalar_prefetch=1,
            grid=(len(away),),
            in_specs=in_specs,
            out_specs=[pl.BlockSpec((rows + extra, columns), lambda i, place: (0, 0))] * (chunks * len(away)),
            scratch_shapes=scratch,
        ),
        compiler_params=pltpu.CompilerParams(vmem_limit_bytes=VMEM_LIMIT),
        cost_estimate=pl.CostEstimate(
            flops=2 * chunks * rows * feats * shares * columns * len(away),
            bytes_accessed=2 * feats * shares * columns * len(away),
            transcendentals=0,
        ),
    )(
        place,
        *[share for c in chosen for share in received[c]],
        *[weight for weight in weights for _ in range(shares)],
        *starts,
    )
    return [dict(zip(away, outs[c * len(away) : (c + 1) * len(away)])) for c in range(chunks)]


def attend_body(block, ways, slots, arrays, spans, tile, table, *refs):
    count = len(slots)
    query_refs = refs[:ways]
    block_refs = refs[ways : ways + arrays]
    out_refs = refs[ways + arrays : 2 * ways + arrays]
    ordered, asked, scores, highest, sums, total, position, sems = refs[2 * ways + arrays :]
    rows, width = out_refs[0].shape
    half = rows // 2
    heads = width // HD
    rest = count // ways

    copies = [[], []]
    for slot, (offset, array, row) in enumerate(slots):
        low = table[offset]
        for part, span in ((0, low), (1, spans - 1 - low)):
            copies[part].append(
                pltpu.make_async_copy(
                    block_refs[array].at[pl.ds(row + part * half, half)],
                    ordered.at[pl.ds(pl.multiple_of(span * half, 16), half)],
                    sems.at[2 * slot + part],
                )
            )
    for copy in copies[0] + copies[1]:
        copy.start()

    from_lane = lax.broadcasted_iota(jnp.int32, (half, 128), 0) - lax.broadcasted_iota(
        jnp.int32, (half, 128), 1
    )
    for a in range(ways):
        low = table[a * rest + block]
        here = slice(a * half, (a + 1) * half)
        for part, span in ((0, low), (1, spans - 1 - low)):
            asked[part, here] = query_refs[a][part * half : (part + 1) * half]
            position[part, here] = from_lane + span * half
    for copy in copies[0]:
        copy.wait()

    slope = LOG2_E / math.sqrt(HD)
    middle = spans * half // 2

    def starts(part):
        return range(0, middle * (part + 1), tile)

    def visible(unit, slot, column):
        piece = scores[slot, :, column : column + 128]
        if column < middle * unit[0]:
            return piece
        return jnp.where(position[unit[0]] >= column, piece, HIDDEN)

    def score_tile(unit, slot, start):
        part, h = unit
        if unit == (1, 0) and start == middle:
            for copy in copies[1]:
                copy.wait()
        scores[slot, :, start : start + tile] = lax.dot_general(
            asked[part, :, h * HD : (h + 1) * HD],
            ordered[start : start + tile, h * HD : (h + 1) * HD],
            (((1,), (1,)), ((), ())),
            preferred_element_type=jnp.float32,
        )
        top = None if start == 0 else highest[slot]
        for column in range(start, start + tile, 128):
            piece = visible(unit, slot, column)
            top = piece if top is None else jnp.maximum(top, piece)
        highest[slot] = top

    def value_tile(unit, slot, start):
        part, h = unit
        top = highest[slot]
        added = None if start == 0 else sums[slot]
        weights = []
        for column in range(start, start + tile, 128):
            piece = jnp.exp2((visible(unit, slot, column) - top) * slope)
            added = piece if added is None else added + piece
            weights.append(piece.astype(jnp.bfloat16))
        sums[slot] = added
        product = jnp.dot(
            jnp.concatenate(weights, axis=1),
            ordered[start : start + tile, width + h * HD : width + (h + 1) * HD],
            preferred_element_type=jnp.float32,
        )
        if start == 0:
            total[slot] = product
        else:
            total[slot] += product

    units = [(0, 0)] + [(1, h) for h in range(heads)] + [(0, h) for h in range(1, heads)]
    for n in range(len(units) + 1):
        todo = []
        if n < len(units):
            todo.append([functools.partial(score_tile, units[n], n % 2, start) for start in starts(units[n][0])])
        if n > 0:
            slot = (n - 1) % 2
            highest[slot] = jnp.broadcast_to(jnp.max(highest[slot], axis=1, keepdims=True), highest.shape[1:])
            todo.append([functools.partial(value_tile, units[n - 1], slot, start) for start in starts(units[n - 1][0])])
        for index in range(max(len(steps) for steps in todo)):
            for steps in todo:
                if index < len(steps):
                    steps[index]()
        if n > 0:
            part, h = units[n - 1]
            result = total[slot] / jnp.sum(sums[slot], axis=1, keepdims=True)
            for a in range(ways):
                out_refs[a][part * half : (part + 1) * half, h * HD : (h + 1) * HD] = result[
                    a * half : (a + 1) * half
                ].astype(jnp.bfloat16)


def attend(block, queries, blocks, table):
    rows, width = queries[0].shape
    ways, count = len(queries), len(blocks)
    arrays = []
    slots = []
    for offset in sorted(blocks):
        array, row = blocks[offset]
        if not any(array is other for other in arrays):
            arrays.append(array)
        slots.append((offset, [array is other for other in arrays].index(True), row))
    spans = 2 * count
    half = rows // 2
    length = count * rows
    tile = 8 * half
    heads = width // HD
    many = ways * half
    smem = pl.BlockSpec(memory_space=pltpu.SMEM)
    flops = 6 * many * heads * length * HD
    return pl.pallas_call(
        functools.partial(attend_body, block, ways, slots, len(arrays), spans, tile),
        out_shape=[jax.ShapeDtypeStruct((rows, width), jnp.bfloat16)] * ways,
        grid=(1,),
        in_specs=[smem]
        + [pl.BlockSpec((rows, width), lambda i: (0, 0))] * ways
        + [pl.BlockSpec(memory_space=pl.ANY)] * len(arrays),
        out_specs=[pl.BlockSpec((rows, width), lambda i: (0, 0))] * ways,
        scratch_shapes=[
            pltpu.VMEM((length, 2 * width), jnp.bfloat16),
            pltpu.VMEM((2, many, width), jnp.bfloat16),
            pltpu.VMEM((2, many, length), jnp.float32),
            pltpu.VMEM((2, many, 128), jnp.float32),
            pltpu.VMEM((2, many, 128), jnp.float32),
            pltpu.VMEM((2, many, HD), jnp.float32),
            pltpu.VMEM((2, many, 128), jnp.int32),
            pltpu.SemaphoreType.DMA((2 * count,)),
        ],
        compiler_params=pltpu.CompilerParams(vmem_limit_bytes=ATTEND_LIMIT),
        cost_estimate=pl.CostEstimate(
            flops=flops,
            bytes_accessed=4 * length * width + 4 * ways * rows * width,
            transcendentals=flops // (4 * HD),
        ),
    )(table, *queries, *arrays)


def table_body(offsets, *refs):
    table = refs[-1]
    for offset, ref in zip(offsets, refs):
        found = ref[...].astype(jnp.float32)
        for part in range(2):
            table[offset + part] = jnp.max(found[part * EXTRA // 2 : (part + 1) * EXTRA // 2]).astype(jnp.int32)


def span_table(blocks, rows):
    offsets = sorted(blocks)
    return pl.pallas_call(
        functools.partial(table_body, offsets),
        out_shape=jax.ShapeDtypeStruct((2 * len(offsets),), jnp.int32),
        grid=(1,),
        in_specs=[
            pl.BlockSpec((EXTRA, 128), functools.partial(lambda row, i: (row, 0), (blocks[i][1] + rows) // EXTRA))
            for i in offsets
        ],
        out_specs=pl.BlockSpec(memory_space=pltpu.SMEM),
        compiler_params=pltpu.CompilerParams(vmem_limit_bytes=VMEM_LIMIT),
    )(*[blocks[i][0] for i in offsets])


def assemble_body(ways, place, *refs):
    for a in range(ways):

        @pl.when(pl.program_id(0) == a)
        def _():
            refs[-1][0] = refs[ways - 1 - a][...]


def assemble(pieces, b, before, place):
    ways = len(pieces)
    rows, width = pieces[0].shape
    in_specs = [pl.BlockSpec((rows, width), lambda a, place: (0, 0))] * ways
    operands = list(pieces[::-1])
    aliases = {}
    if before is not None:
        in_specs.append(pl.BlockSpec(memory_space=pl.ANY))
        operands.append(before)
        aliases = {1 + ways: 0}
    return pl.pallas_call(
        functools.partial(assemble_body, ways),
        out_shape=jax.ShapeDtypeStruct((2, rows, ways * width), jnp.bfloat16),
        grid_spec=pltpu.PrefetchScalarGridSpec(
            num_scalar_prefetch=1,
            grid=(ways,),
            in_specs=in_specs,
            out_specs=pl.BlockSpec((1, rows, width), lambda a, place: (place[2] ^ b, 0, place[1] ^ a)),
        ),
        input_output_aliases=aliases,
        compiler_params=pltpu.CompilerParams(vmem_limit_bytes=VMEM_LIMIT),
    )(place, *operands)


def on_device(ctx_size, tp_size, hidden_in, w_q, w_k, w_v, event_pos):
    _, rows, _ = hidden_in.shape
    features = w_q.shape[1]
    ways = math.gcd(features // HD, ctx_size // 2)
    rest = ctx_size // ways
    ctx_me = lax.axis_index("ctx").astype(jnp.int32)
    tp_me = lax.axis_index("tp").astype(jnp.int32)
    core = ctx_me % 2
    place = jnp.stack([tp_me, ctx_me // rest, core, ctx_me])
    away = list(range(ways))

    def over_ctx(value, offset):
        return exchange(value, "ctx", ctx_size, offset) if offset else value

    def other_shares(own):
        shares = [own]
        bit = 1
        while bit < tp_size:
            shares += [exchange(share, "tp", tp_size, bit) for share in shares]
            bit *= 2
        return shares[1:]

    mine = lax.dynamic_index_in_dim(hidden_in, core, 0, keepdims=False)
    other = over_ctx(lax.dynamic_index_in_dim(hidden_in, 1 - core, 0, keepdims=False), 1)
    received = [other_shares(mine), other_shares(other)]

    start_k, start_v, start_q = own_products(hidden_in, other, [w_k, w_v, w_q], place, ways)

    spans = event_pos[:, 0] // (rows // 2)
    span_other = over_ctx(lax.dynamic_index_in_dim(spans, 1 - core, 0), 1)
    later = jnp.concatenate([place, lax.dynamic_index_in_dim(spans, core, 0), span_other])
    (made_0,) = rest_products(received, [0], [w_k, w_v], [start_k, start_v], later, ways, away, EXTRA)
    first = {a: over_ctx(made_0[a], a * rest) for a in away}
    ahead = over_ctx(made_0[0], rest // 2)
    asked = rest_products(received, [0], [w_q], [start_q], place, ways, away)
    received, asked = lax.optimization_barrier((received, asked))
    (made_1,) = rest_products(received, [1], [w_k, w_v], [start_k, start_v], place, ways, away)
    ahead_1 = over_ctx(made_1[0], rest // 2)
    for a in away:
        first[a], made_1[a] = lax.optimization_barrier((first[a], made_1[a]))
    received, ahead_1 = lax.optimization_barrier((received, ahead_1))
    asked += rest_products(received, [1], [w_q], [start_q], place, ways, away)

    def over_y(blocks):
        bit = rest // 2
        while bit > 1:
            for i in list(blocks):
                if i ^ bit not in blocks:
                    blocks[i ^ bit] = over_ctx(blocks[i], bit)
            bit //= 2
        return blocks

    blocks = {a * rest: first[a] for a in away}
    blocks[rest // 2] = ahead
    before = []
    for a in range(1, ways):
        value = lax.optimization_barrier((first[a], before))[0] if a == ways - 1 else first[a]
        before.append(over_ctx(value, rest // 2))
        blocks[a * rest + rest // 2] = before[-1]
    blocks = over_y(blocks)
    second = {}
    queries = [{}, {}]
    for a in away:
        last = (first[a], ahead)
        for made, keep, key in ((made_1, second, a * rest + 1), (asked[0], queries[0], a), (asked[1], queries[1], a)):
            value, last = lax.optimization_barrier((made[a], last))
            last = keep[key] = over_ctx(value, a * rest)
            if keep is second and a:
                last = (last, ahead_1)
            if keep is second and a == ways - 1:
                last = (last, [blocks[i] for i in sorted(blocks)])

    table = span_table({i: (array, 0) for i, array in blocks.items()}, rows)
    second[rest // 2 + 1] = ahead_1
    blocks.update(over_y(second))
    blocks = {i: (array, 0) for i, array in blocks.items()}
    out = None
    for b in range(2):
        outs = attend(b, [queries[b][a] for a in range(ways)], blocks, table)
        pieces = {a: over_ctx(outs[a], a * rest + b) for a in away}
        out = assemble([pieces[a] for a in range(ways)], b, out, place)
    return out


def solution(mesh):
    sizes = dict(mesh.shape)
    placed = (P(None, "ctx", "tp"), P(None, "tp"), P(None, "tp"), P(None, "tp"), P(None, "ctx"))
    return jax.shard_map(
        functools.partial(on_device, sizes["ctx"], sizes["tp"]),
        mesh=mesh,
        in_specs=placed,
        out_specs=P(None, "ctx", "tp"),
        check_vma=False,
    )
```

```python
import functools
import math

import jax
import jax.numpy as jnp
from jax import lax
from jax.experimental import pallas as pl
from jax.experimental.pallas import tpu as pltpu
from jax.sharding import PartitionSpec as P

HD = 128
LOG2_E = 1.4426950408889634
HIDDEN = -1e30
VMEM_LIMIT = 44 * 2**20
ATTEND_LIMIT = 56 * 2**20


def exchange(value, axis, size, bit):
    return lax.ppermute(value, axis, [(i, i ^ bit) for i in range(size)])


EXTRA = 16


def own_body(weights, place, mine_ref, other_ref, *refs):
    flat_ref = refs[-1]
    rows = other_ref.shape[0]

    @pl.when(pl.program_id(0) == 0)
    def _():
        flat_ref[:rows] = mine_ref[0]
        flat_ref[rows:] = other_ref[...]

    for weight_ref, out_ref in zip(refs[:weights], refs[weights:-1]):
        result = jnp.dot(flat_ref[...], weight_ref[...], preferred_element_type=jnp.float32)
        out_ref[...] = result.reshape(2, rows, -1)


def own_products(hidden_in, other, weights, place, ways):
    rows, feats = other.shape
    features = weights[0].shape[1]
    width = features // ways
    return pl.pallas_call(
        functools.partial(own_body, len(weights)),
        out_shape=[jax.ShapeDtypeStruct((2, rows, features), jnp.float32)] * len(weights),
        grid_spec=pltpu.PrefetchScalarGridSpec(
            num_scalar_prefetch=1,
            grid=(ways,),
            in_specs=[
                pl.BlockSpec((1, rows, feats), lambda g, place: (place[2], 0, 0)),
                pl.BlockSpec((rows, feats), lambda g, place: (0, 0)),
            ]
            + [pl.BlockSpec((feats, width), lambda g, place: (place[0], g))] * len(weights),
            out_specs=[pl.BlockSpec((2, rows, width), lambda g, place: (0, 0, g))] * len(weights),
            scratch_shapes=[pltpu.VMEM((2 * rows, feats), jnp.bfloat16)],
        ),
        compiler_params=pltpu.CompilerParams(vmem_limit_bytes=VMEM_LIMIT),
        cost_estimate=pl.CostEstimate(
            flops=4 * rows * feats * features * len(weights),
            bytes_accessed=2 * feats * features * len(weights),
            transcendentals=0,
        ),
    )(place, hidden_in, other, *weights)


def rest_body(shares, weights, chunks, away, extra, place, *refs):
    inputs = refs[: shares * chunks]
    refs = refs[shares * chunks :]
    weight_refs, refs = refs[: weights * shares], refs[weights * shares :]
    start_refs, refs = refs[:weights], refs[weights:]
    out_refs, flats = refs[: chunks * len(away)], refs[chunks * len(away) :]
    rows, width = out_refs[0].shape
    rows -= extra
    width //= weights
    step = pl.program_id(0)
    if chunks > 1:

        @pl.when(step == 0)
        def _():
            for share in range(shares):
                for c in range(chunks):
                    flats[share][c * rows : (c + 1) * rows] = inputs[c * shares + share][...]

    else:
        flats = inputs
    made = []
    for n in range(weights):
        total = start_refs[n][...].reshape(chunks * rows, width)
        for share in range(shares):
            total += jnp.dot(
                flats[share][...], weight_refs[n * shares + share][...], preferred_element_type=jnp.float32
            )
        made.append(total.astype(jnp.bfloat16))
    for index in range(len(away)):

        @pl.when(step == index)
        def _():
            for c in range(chunks):
                for n in range(weights):
                    out_refs[c * len(away) + index][:rows, n * width : (n + 1) * width] = made[n][
                        c * rows : (c + 1) * rows
                    ]
            if extra:
                line = lax.broadcasted_iota(jnp.int32, (extra, weights * width), 0)
                spans = jnp.where(line < extra // 2, place[4], place[5]).astype(jnp.float32)
                out_refs[index][rows:] = spans.astype(jnp.bfloat16)


def rest_products(received, chosen, weights, starts, place, ways, away, extra=0):
    shares = len(received[0])
    rows, feats = received[0][0].shape
    width = weights[0].shape[1] // ways
    chunks = len(chosen)
    top = away[0]
    stride = away[1] - top if len(away) > 1 else 0

    def weight_map(share, i, place):
        return (place[0] ^ (share + 1), place[1] ^ (top + stride * i))

    in_specs = [pl.BlockSpec((rows, feats), lambda i, place: (0, 0))] * (shares * chunks)
    for _ in weights:
        for share in range(shares):
            in_specs.append(pl.BlockSpec((feats, width), functools.partial(weight_map, share)))
    in_specs += [
        pl.BlockSpec((chunks, rows, width), lambda i, place: (chosen[0] // chunks, 0, place[1] ^ (top + stride * i)))
    ] * len(weights)
    columns = width * len(weights)
    scratch = [pltpu.VMEM((chunks * rows, feats), jnp.bfloat16)] * (shares if chunks > 1 else 0)
    outs = pl.pallas_call(
        functools.partial(rest_body, shares, len(weights), chunks, away, extra),
        out_shape=[jax.ShapeDtypeStruct((rows + extra, columns), jnp.bfloat16)] * (chunks * len(away)),
        grid_spec=pltpu.PrefetchScalarGridSpec(
            num_scalar_prefetch=1,
            grid=(len(away),),
            in_specs=in_specs,
            out_specs=[pl.BlockSpec((rows + extra, columns), lambda i, place: (0, 0))] * (chunks * len(away)),
            scratch_shapes=scratch,
        ),
        compiler_params=pltpu.CompilerParams(vmem_limit_bytes=VMEM_LIMIT),
        cost_estimate=pl.CostEstimate(
            flops=2 * chunks * rows * feats * shares * columns * len(away),
            bytes_accessed=2 * feats * shares * columns * len(away),
            transcendentals=0,
        ),
    )(
        place,
        *[share for c in chosen for share in received[c]],
        *[weight for weight in weights for _ in range(shares)],
        *starts,
    )
    return [dict(zip(away, outs[c * len(away) : (c + 1) * len(away)])) for c in range(chunks)]


def attend_body(block, ways, slots, arrays, spans, tile, table, *refs):
    count = len(slots)
    query_refs = refs[:ways]
    block_refs = refs[ways : ways + arrays]
    out_refs = refs[ways + arrays : 2 * ways + arrays]
    ordered, asked, scores, highest, sums, total, position, sems = refs[2 * ways + arrays :]
    rows, width = out_refs[0].shape
    half = rows // 2
    heads = width // HD
    rest = count // ways

    copies = [[], []]
    for slot, (offset, array, row) in enumerate(slots):
        low = table[offset]
        for part, span in ((0, low), (1, spans - 1 - low)):
            copies[part].append(
                pltpu.make_async_copy(
                    block_refs[array].at[pl.ds(row + part * half, half)],
                    ordered.at[pl.ds(pl.multiple_of(span * half, 16), half)],
                    sems.at[2 * slot + part],
                )
            )
    for copy in copies[0] + copies[1]:
        copy.start()

    from_lane = lax.broadcasted_iota(jnp.int32, (half, 128), 0) - lax.broadcasted_iota(
        jnp.int32, (half, 128), 1
    )
    for a in range(ways):
        low = table[a * rest + block]
        here = slice(a * half, (a + 1) * half)
        for part, span in ((0, low), (1, spans - 1 - low)):
            asked[part, here] = query_refs[a][part * half : (part + 1) * half]
            position[part, here] = from_lane + span * half
    for copy in copies[0]:
        copy.wait()

    slope = LOG2_E / math.sqrt(HD)
    middle = spans * half // 2

    def starts(part):
        return range(0, middle * (part + 1), tile)

    def visible(unit, slot, column):
        piece = scores[slot, :, column : column + 128]
        if column < middle * unit[0]:
            return piece
        return jnp.where(position[unit[0]] >= column, piece, HIDDEN)

    def score_tile(unit, slot, start):
        part, h = unit
        if unit == (1, 0) and start == middle:
            for copy in copies[1]:
                copy.wait()
        scores[slot, :, start : start + tile] = lax.dot_general(
            asked[part, :, h * HD : (h + 1) * HD],
            ordered[start : start + tile, h * HD : (h + 1) * HD],
            (((1,), (1,)), ((), ())),
            preferred_element_type=jnp.float32,
        )
        top = None if start == 0 else highest[slot]
        for column in range(start, start + tile, 128):
            piece = visible(unit, slot, column)
            top = piece if top is None else jnp.maximum(top, piece)
        highest[slot] = top

    def value_tile(unit, slot, start):
        part, h = unit
        top = highest[slot]
        added = None if start == 0 else sums[slot]
        weights = []
        for column in range(start, start + tile, 128):
            piece = jnp.exp2((visible(unit, slot, column) - top) * slope)
            added = piece if added is None else added + piece
            weights.append(piece.astype(jnp.bfloat16))
        sums[slot] = added
        product = jnp.dot(
            jnp.concatenate(weights, axis=1),
            ordered[start : start + tile, width + h * HD : width + (h + 1) * HD],
            preferred_element_type=jnp.float32,
        )
        if start == 0:
            total[slot] = product
        else:
            total[slot] += product

    units = [(0, 0)] + [(1, h) for h in range(heads)] + [(0, h) for h in range(1, heads)]
    for n in range(len(units) + 1):
        todo = []
        if n < len(units):
            todo.append([functools.partial(score_tile, units[n], n % 2, start) for start in starts(units[n][0])])
        if n > 0:
            slot = (n - 1) % 2
            highest[slot] = jnp.broadcast_to(jnp.max(highest[slot], axis=1, keepdims=True), highest.shape[1:])
            todo.append([functools.partial(value_tile, units[n - 1], slot, start) for start in starts(units[n - 1][0])])
        for index in range(max(len(steps) for steps in todo)):
            for steps in todo:
                if index < len(steps):
                    steps[index]()
        if n > 0:
            part, h = units[n - 1]
            result = total[slot] / jnp.sum(sums[slot], axis=1, keepdims=True)
            for a in range(ways):
                out_refs[a][part * half : (part + 1) * half, h * HD : (h + 1) * HD] = result[
                    a * half : (a + 1) * half
                ].astype(jnp.bfloat16)


def attend(block, queries, blocks, table):
    rows, width = queries[0].shape
    ways, count = len(queries), len(blocks)
    arrays = []
    slots = []
    for offset in sorted(blocks):
        array, row = blocks[offset]
        if not any(array is other for other in arrays):
            arrays.append(array)
        slots.append((offset, [array is other for other in arrays].index(True), row))
    spans = 2 * count
    half = rows // 2
    length = count * rows
    tile = 8 * half
    heads = width // HD
    many = ways * half
    smem = pl.BlockSpec(memory_space=pltpu.SMEM)
    flops = 6 * many * heads * length * HD
    return pl.pallas_call(
        functools.partial(attend_body, block, ways, slots, len(arrays), spans, tile),
        out_shape=[jax.ShapeDtypeStruct((rows, width), jnp.bfloat16)] * ways,
        grid=(1,),
        in_specs=[smem]
        + [pl.BlockSpec((rows, width), lambda i: (0, 0))] * ways
        + [pl.BlockSpec(memory_space=pl.ANY)] * len(arrays),
        out_specs=[pl.BlockSpec((rows, width), lambda i: (0, 0))] * ways,
        scratch_shapes=[
            pltpu.VMEM((length, 2 * width), jnp.bfloat16),
            pltpu.VMEM((2, many, width), jnp.bfloat16),
            pltpu.VMEM((2, many, length), jnp.float32),
            pltpu.VMEM((2, many, 128), jnp.float32),
            pltpu.VMEM((2, many, 128), jnp.float32),
            pltpu.VMEM((2, many, HD), jnp.float32),
            pltpu.VMEM((2, many, 128), jnp.int32),
            pltpu.SemaphoreType.DMA((2 * count,)),
        ],
        compiler_params=pltpu.CompilerParams(vmem_limit_bytes=ATTEND_LIMIT),
        cost_estimate=pl.CostEstimate(
            flops=flops,
            bytes_accessed=4 * length * width + 4 * ways * rows * width,
            transcendentals=flops // (4 * HD),
        ),
    )(table, *queries, *arrays)


def table_body(offsets, *refs):
    table = refs[-1]
    for offset, ref in zip(offsets, refs):
        found = ref[...].astype(jnp.float32)
        for part in range(2):
            table[offset + part] = jnp.max(found[part * EXTRA // 2 : (part + 1) * EXTRA // 2]).astype(jnp.int32)


def span_table(blocks, rows):
    offsets = sorted(blocks)
    return pl.pallas_call(
        functools.partial(table_body, offsets),
        out_shape=jax.ShapeDtypeStruct((2 * len(offsets),), jnp.int32),
        grid=(1,),
        in_specs=[
            pl.BlockSpec((EXTRA, 128), functools.partial(lambda row, i: (row, 0), (blocks[i][1] + rows) // EXTRA))
            for i in offsets
        ],
        out_specs=pl.BlockSpec(memory_space=pltpu.SMEM),
        compiler_params=pltpu.CompilerParams(vmem_limit_bytes=VMEM_LIMIT),
    )(*[blocks[i][0] for i in offsets])


def assemble_body(ways, place, *refs):
    for a in range(ways):

        @pl.when(pl.program_id(0) == a)
        def _():
            refs[-1][0] = refs[ways - 1 - a][...]


def assemble(pieces, b, before, place):
    ways = len(pieces)
    rows, width = pieces[0].shape
    in_specs = [pl.BlockSpec((rows, width), lambda a, place: (0, 0))] * ways
    operands = list(pieces[::-1])
    aliases = {}
    if before is not None:
        in_specs.append(pl.BlockSpec(memory_space=pl.ANY))
        operands.append(before)
        aliases = {1 + ways: 0}
    return pl.pallas_call(
        functools.partial(assemble_body, ways),
        out_shape=jax.ShapeDtypeStruct((2, rows, ways * width), jnp.bfloat16),
        grid_spec=pltpu.PrefetchScalarGridSpec(
            num_scalar_prefetch=1,
            grid=(ways,),
            in_specs=in_specs,
            out_specs=pl.BlockSpec((1, rows, width), lambda a, place: (place[2] ^ b, 0, place[1] ^ a)),
        ),
        input_output_aliases=aliases,
        compiler_params=pltpu.CompilerParams(vmem_limit_bytes=VMEM_LIMIT),
    )(place, *operands)


def on_device(ctx_size, tp_size, hidden_in, w_q, w_k, w_v, event_pos):
    _, rows, _ = hidden_in.shape
    features = w_q.shape[1]
    ways = math.gcd(features // HD, ctx_size // 2)
    rest = ctx_size // ways
    ctx_me = lax.axis_index("ctx").astype(jnp.int32)
    tp_me = lax.axis_index("tp").astype(jnp.int32)
    core = ctx_me % 2
    place = jnp.stack([tp_me, ctx_me // rest, core, ctx_me])
    away = list(range(ways))

    def over_ctx(value, offset):
        return exchange(value, "ctx", ctx_size, offset) if offset else value

    def other_shares(own):
        shares = [own]
        bit = 1
        while bit < tp_size:
            shares += [exchange(share, "tp", tp_size, bit) for share in shares]
            bit *= 2
        return shares[1:]

    mine = lax.dynamic_index_in_dim(hidden_in, core, 0, keepdims=False)
    other = over_ctx(lax.dynamic_index_in_dim(hidden_in, 1 - core, 0, keepdims=False), 1)
    received = [other_shares(mine), other_shares(other)]

    start_k, start_v, start_q = own_products(hidden_in, other, [w_k, w_v, w_q], place, ways)

    spans = event_pos[:, 0] // (rows // 2)
    span_other = over_ctx(lax.dynamic_index_in_dim(spans, 1 - core, 0), 1)
    later = jnp.concatenate([place, lax.dynamic_index_in_dim(spans, core, 0), span_other])
    made_0 = {}
    for part in (away[::-2], away[-2::-2]):
        if part:
            made_0.update(
                rest_products(received, [0], [w_k, w_v], [start_k, start_v], later, ways, part, EXTRA)[0]
            )
    first = {a: over_ctx(made_0[a], a * rest) for a in away}
    ahead = over_ctx(made_0[0], rest // 2)
    asked = rest_products(received, [0], [w_q], [start_q], place, ways, away)
    received, asked = lax.optimization_barrier((received, asked))
    (made_1,) = rest_products(received, [1], [w_k, w_v], [start_k, start_v], place, ways, away)
    ahead_1 = over_ctx(made_1[0], rest // 2)
    for a in away:
        first[a], made_1[a] = lax.optimization_barrier((first[a], made_1[a]))
    received, ahead_1 = lax.optimization_barrier((received, ahead_1))
    asked += rest_products(received, [1], [w_q], [start_q], place, ways, away)

    def over_y(blocks):
        bit = rest // 2
        while bit > 1:
            for i in list(blocks):
                if i ^ bit not in blocks:
                    blocks[i ^ bit] = over_ctx(blocks[i], bit)
            bit //= 2
        return blocks

    blocks = {a * rest: first[a] for a in away}
    blocks[rest // 2] = ahead
    before = []
    for a in range(1, ways):
        value = lax.optimization_barrier((first[a], before))[0] if a == ways - 1 else first[a]
        before.append(over_ctx(value, rest // 2))
        blocks[a * rest + rest // 2] = before[-1]
    blocks = over_y(blocks)
    second = {}
    for a in away:
        value, _ = lax.optimization_barrier((made_1[a], (first[a], ahead)))
        second[a * rest + 1] = over_ctx(value, a * rest)
    queries = [{}, {}]
    for a in away:
        wait = (second[a * rest + 1], ahead_1) if a else ()
        if a == ways - 1:
            wait = (wait, [blocks[i] for i in sorted(blocks)])
        value, _ = lax.optimization_barrier((asked[0][a], wait))
        queries[0][a] = over_ctx(value, a * rest)
    for a in away:
        value, _ = lax.optimization_barrier((asked[1][a], queries[0][min(1, ways - 1)]))
        queries[1][a] = over_ctx(value, a * rest)
    table = span_table({i: (array, 0) for i, array in blocks.items()}, rows)
    second[rest // 2 + 1] = ahead_1
    blocks.update(over_y(second))
    blocks = {i: (array, 0) for i, array in blocks.items()}
    out = None
    for b in range(2):
        outs = attend(b, [queries[b][a] for a in range(ways)], blocks, table)
        pieces = {a: over_ctx(outs[a], a * rest + b) for a in away}
        out = assemble([pieces[a] for a in range(ways)], b, out, place)
    return out


def solution(mesh):
    sizes = dict(mesh.shape)
    placed = (P(None, "ctx", "tp"), P(None, "tp"), P(None, "tp"), P(None, "tp"), P(None, "ctx"))
    return jax.shard_map(
        functools.partial(on_device, sizes["ctx"], sizes["tp"]),
        mesh=mesh,
        in_specs=placed,
        out_specs=P(None, "ctx", "tp"),
        check_vma=False,
    )
```

```python
import functools
import math

import jax
import jax.numpy as jnp
from jax import lax
from jax.experimental import pallas as pl
from jax.experimental.pallas import tpu as pltpu
from jax.sharding import PartitionSpec as P

HD = 128
LOG2_E = 1.4426950408889634
HIDDEN = -1e30
VMEM_LIMIT = 44 * 2**20
ATTEND_LIMIT = 56 * 2**20


def exchange(value, axis, size, bit):
    return lax.ppermute(value, axis, [(i, i ^ bit) for i in range(size)])


EXTRA = 16


def own_body(weights, place, mine_ref, other_ref, *refs):
    flat_ref = refs[-1]
    rows = other_ref.shape[0]

    @pl.when(pl.program_id(0) == 0)
    def _():
        flat_ref[:rows] = mine_ref[0]
        flat_ref[rows:] = other_ref[...]

    for weight_ref, out_ref in zip(refs[:weights], refs[weights:-1]):
        result = jnp.dot(flat_ref[...], weight_ref[...], preferred_element_type=jnp.float32)
        out_ref[...] = result.reshape(2, rows, -1)


def own_products(hidden_in, other, weights, place, ways):
    rows, feats = other.shape
    features = weights[0].shape[1]
    width = features // ways
    return pl.pallas_call(
        functools.partial(own_body, len(weights)),
        out_shape=[jax.ShapeDtypeStruct((2, rows, features), jnp.float32)] * len(weights),
        grid_spec=pltpu.PrefetchScalarGridSpec(
            num_scalar_prefetch=1,
            grid=(ways,),
            in_specs=[
                pl.BlockSpec((1, rows, feats), lambda g, place: (place[2], 0, 0)),
                pl.BlockSpec((rows, feats), lambda g, place: (0, 0)),
            ]
            + [pl.BlockSpec((feats, width), lambda g, place: (place[0], g))] * len(weights),
            out_specs=[pl.BlockSpec((2, rows, width), lambda g, place: (0, 0, g))] * len(weights),
            scratch_shapes=[pltpu.VMEM((2 * rows, feats), jnp.bfloat16)],
        ),
        compiler_params=pltpu.CompilerParams(vmem_limit_bytes=VMEM_LIMIT),
        cost_estimate=pl.CostEstimate(
            flops=4 * rows * feats * features * len(weights),
            bytes_accessed=2 * feats * features * len(weights),
            transcendentals=0,
        ),
    )(place, hidden_in, other, *weights)


def rest_body(shares, weights, chunks, away, extra, place, *refs):
    inputs = refs[: shares * chunks]
    refs = refs[shares * chunks :]
    weight_refs, refs = refs[: weights * shares], refs[weights * shares :]
    start_refs, refs = refs[:weights], refs[weights:]
    out_refs, flats = refs[: chunks * len(away)], refs[chunks * len(away) :]
    rows, width = out_refs[0].shape
    rows -= extra
    width //= weights
    step = pl.program_id(0)
    if chunks > 1:

        @pl.when(step == 0)
        def _():
            for share in range(shares):
                for c in range(chunks):
                    flats[share][c * rows : (c + 1) * rows] = inputs[c * shares + share][...]

    else:
        flats = inputs
    made = []
    for n in range(weights):
        total = start_refs[n][...].reshape(chunks * rows, width)
        for share in range(shares):
            total += jnp.dot(
                flats[share][...], weight_refs[n * shares + share][...], preferred_element_type=jnp.float32
            )
        made.append(total.astype(jnp.bfloat16))
    for index in range(len(away)):

        @pl.when(step == index)
        def _():
            for c in range(chunks):
                for n in range(weights):
                    out_refs[c * len(away) + index][:rows, n * width : (n + 1) * width] = made[n][
                        c * rows : (c + 1) * rows
                    ]
            if extra:
                line = lax.broadcasted_iota(jnp.int32, (extra, weights * width), 0)
                spans = jnp.where(line < extra // 2, place[4], place[5]).astype(jnp.float32)
                out_refs[index][rows:] = spans.astype(jnp.bfloat16)


def rest_products(received, chosen, weights, starts, place, ways, away, extra=0):
    shares = len(received[0])
    rows, feats = received[0][0].shape
    width = weights[0].shape[1] // ways
    chunks = len(chosen)
    top = away[0]
    stride = away[1] - top if len(away) > 1 else 0

    def weight_map(share, i, place):
        return (place[0] ^ (share + 1), place[1] ^ (top + stride * i))

    in_specs = [pl.BlockSpec((rows, feats), lambda i, place: (0, 0))] * (shares * chunks)
    for _ in weights:
        for share in range(shares):
            in_specs.append(pl.BlockSpec((feats, width), functools.partial(weight_map, share)))
    in_specs += [
        pl.BlockSpec((chunks, rows, width), lambda i, place: (chosen[0] // chunks, 0, place[1] ^ (top + stride * i)))
    ] * len(weights)
    columns = width * len(weights)
    scratch = [pltpu.VMEM((chunks * rows, feats), jnp.bfloat16)] * (shares if chunks > 1 else 0)
    outs = pl.pallas_call(
        functools.partial(rest_body, shares, len(weights), chunks, away, extra),
        out_shape=[jax.ShapeDtypeStruct((rows + extra, columns), jnp.bfloat16)] * (chunks * len(away)),
        grid_spec=pltpu.PrefetchScalarGridSpec(
            num_scalar_prefetch=1,
            grid=(len(away),),
            in_specs=in_specs,
            out_specs=[pl.BlockSpec((rows + extra, columns), lambda i, place: (0, 0))] * (chunks * len(away)),
            scratch_shapes=scratch,
        ),
        compiler_params=pltpu.CompilerParams(vmem_limit_bytes=VMEM_LIMIT),
        cost_estimate=pl.CostEstimate(
            flops=2 * chunks * rows * feats * shares * columns * len(away),
            bytes_accessed=2 * feats * shares * columns * len(away),
            transcendentals=0,
        ),
    )(
        place,
        *[share for c in chosen for share in received[c]],
        *[weight for weight in weights for _ in range(shares)],
        *starts,
    )
    return [dict(zip(away, outs[c * len(away) : (c + 1) * len(away)])) for c in range(chunks)]


def attend_body(block, ways, slots, arrays, spans, tile, table, *refs):
    count = len(slots)
    query_refs = refs[:ways]
    block_refs = refs[ways : ways + arrays]
    out_refs = refs[ways + arrays : 2 * ways + arrays]
    ordered, asked, scores, highest, sums, total, position, sems = refs[2 * ways + arrays :]
    rows, width = out_refs[0].shape
    half = rows // 2
    heads = width // HD
    rest = count // ways

    copies = [[], []]
    for slot, (offset, array, row) in enumerate(slots):
        low = table[offset]
        for part, span in ((0, low), (1, spans - 1 - low)):
            copies[part].append(
                pltpu.make_async_copy(
                    block_refs[array].at[pl.ds(row + part * half, half)],
                    ordered.at[pl.ds(pl.multiple_of(span * half, 16), half)],
                    sems.at[2 * slot + part],
                )
            )
    for copy in copies[0] + copies[1]:
        copy.start()

    from_lane = lax.broadcasted_iota(jnp.int32, (half, 128), 0) - lax.broadcasted_iota(
        jnp.int32, (half, 128), 1
    )
    for a in range(ways):
        low = table[a * rest + block]
        here = slice(a * half, (a + 1) * half)
        for part, span in ((0, low), (1, spans - 1 - low)):
            asked[part, here] = query_refs[a][part * half : (part + 1) * half]
            position[part, here] = from_lane + span * half
    for copy in copies[0]:
        copy.wait()

    slope = LOG2_E / math.sqrt(HD)
    middle = spans * half // 2

    def starts(part):
        return range(0, middle * (part + 1), tile)

    def visible(unit, slot, column):
        piece = scores[slot, :, column : column + 128]
        if column < middle * unit[0]:
            return piece
        return jnp.where(position[unit[0]] >= column, piece, HIDDEN)

    def score_tile(unit, slot, start):
        part, h = unit
        if unit == (1, 0) and start == middle:
            for copy in copies[1]:
                copy.wait()
        scores[slot, :, start : start + tile] = lax.dot_general(
            asked[part, :, h * HD : (h + 1) * HD],
            ordered[start : start + tile, h * HD : (h + 1) * HD],
            (((1,), (1,)), ((), ())),
            preferred_element_type=jnp.float32,
        )
        top = None if start == 0 else highest[slot]
        for column in range(start, start + tile, 128):
            piece = visible(unit, slot, column)
            top = piece if top is None else jnp.maximum(top, piece)
        highest[slot] = top

    def value_tile(unit, slot, start):
        part, h = unit
        top = highest[slot]
        added = None if start == 0 else sums[slot]
        weights = []
        for column in range(start, start + tile, 128):
            piece = jnp.exp2((visible(unit, slot, column) - top) * slope)
            added = piece if added is None else added + piece
            weights.append(piece.astype(jnp.bfloat16))
        sums[slot] = added
        product = jnp.dot(
            jnp.concatenate(weights, axis=1),
            ordered[start : start + tile, width + h * HD : width + (h + 1) * HD],
            preferred_element_type=jnp.float32,
        )
        if start == 0:
            total[slot] = product
        else:
            total[slot] += product

    units = [(0, 0)] + [(1, h) for h in range(heads)] + [(0, h) for h in range(1, heads)]
    for n in range(len(units) + 1):
        todo = []
        if n < len(units):
            todo.append([functools.partial(score_tile, units[n], n % 2, start) for start in starts(units[n][0])])
        if n > 0:
            slot = (n - 1) % 2
            highest[slot] = jnp.broadcast_to(jnp.max(highest[slot], axis=1, keepdims=True), highest.shape[1:])
            todo.append([functools.partial(value_tile, units[n - 1], slot, start) for start in starts(units[n - 1][0])])
        for index in range(max(len(steps) for steps in todo)):
            for steps in todo:
                if index < len(steps):
                    steps[index]()
        if n > 0:
            part, h = units[n - 1]
            result = total[slot] / jnp.sum(sums[slot], axis=1, keepdims=True)
            for a in range(ways):
                out_refs[a][part * half : (part + 1) * half, h * HD : (h + 1) * HD] = result[
                    a * half : (a + 1) * half
                ].astype(jnp.bfloat16)


def attend(block, queries, blocks, table):
    rows, width = queries[0].shape
    ways, count = len(queries), len(blocks)
    arrays = []
    slots = []
    for offset in sorted(blocks):
        array, row = blocks[offset]
        if not any(array is other for other in arrays):
            arrays.append(array)
        slots.append((offset, [array is other for other in arrays].index(True), row))
    spans = 2 * count
    half = rows // 2
    length = count * rows
    tile = 8 * half
    heads = width // HD
    many = ways * half
    smem = pl.BlockSpec(memory_space=pltpu.SMEM)
    flops = 6 * many * heads * length * HD
    return pl.pallas_call(
        functools.partial(attend_body, block, ways, slots, len(arrays), spans, tile),
        out_shape=[jax.ShapeDtypeStruct((rows, width), jnp.bfloat16)] * ways,
        grid=(1,),
        in_specs=[smem]
        + [pl.BlockSpec((rows, width), lambda i: (0, 0))] * ways
        + [pl.BlockSpec(memory_space=pl.ANY)] * len(arrays),
        out_specs=[pl.BlockSpec((rows, width), lambda i: (0, 0))] * ways,
        scratch_shapes=[
            pltpu.VMEM((length, 2 * width), jnp.bfloat16),
            pltpu.VMEM((2, many, width), jnp.bfloat16),
            pltpu.VMEM((2, many, length), jnp.float32),
            pltpu.VMEM((2, many, 128), jnp.float32),
            pltpu.VMEM((2, many, 128), jnp.float32),
            pltpu.VMEM((2, many, HD), jnp.float32),
            pltpu.VMEM((2, many, 128), jnp.int32),
            pltpu.SemaphoreType.DMA((2 * count,)),
        ],
        compiler_params=pltpu.CompilerParams(vmem_limit_bytes=ATTEND_LIMIT),
        cost_estimate=pl.CostEstimate(
            flops=flops,
            bytes_accessed=4 * length * width + 4 * ways * rows * width,
            transcendentals=flops // (4 * HD),
        ),
    )(table, *queries, *arrays)


def table_body(offsets, *refs):
    table = refs[-1]
    for offset, ref in zip(offsets, refs):
        found = ref[...].astype(jnp.float32)
        for part in range(2):
            table[offset + part] = jnp.max(found[part * EXTRA // 2 : (part + 1) * EXTRA // 2]).astype(jnp.int32)


def span_table(blocks, rows):
    offsets = sorted(blocks)
    return pl.pallas_call(
        functools.partial(table_body, offsets),
        out_shape=jax.ShapeDtypeStruct((2 * len(offsets),), jnp.int32),
        grid=(1,),
        in_specs=[
            pl.BlockSpec((EXTRA, 128), functools.partial(lambda row, i: (row, 0), (blocks[i][1] + rows) // EXTRA))
            for i in offsets
        ],
        out_specs=pl.BlockSpec(memory_space=pltpu.SMEM),
        compiler_params=pltpu.CompilerParams(vmem_limit_bytes=VMEM_LIMIT),
    )(*[blocks[i][0] for i in offsets])


def assemble_body(ways, place, *refs):
    for a in range(ways):

        @pl.when(pl.program_id(0) == a)
        def _():
            refs[-1][0] = refs[ways - 1 - a][...]


def assemble(pieces, b, before, place):
    ways = len(pieces)
    rows, width = pieces[0].shape
    in_specs = [pl.BlockSpec((rows, width), lambda a, place: (0, 0))] * ways
    operands = list(pieces[::-1])
    aliases = {}
    if before is not None:
        in_specs.append(pl.BlockSpec(memory_space=pl.ANY))
        operands.append(before)
        aliases = {1 + ways: 0}
    return pl.pallas_call(
        functools.partial(assemble_body, ways),
        out_shape=jax.ShapeDtypeStruct((2, rows, ways * width), jnp.bfloat16),
        grid_spec=pltpu.PrefetchScalarGridSpec(
            num_scalar_prefetch=1,
            grid=(ways,),
            in_specs=in_specs,
            out_specs=pl.BlockSpec((1, rows, width), lambda a, place: (place[2] ^ b, 0, place[1] ^ a)),
        ),
        input_output_aliases=aliases,
        compiler_params=pltpu.CompilerParams(vmem_limit_bytes=VMEM_LIMIT),
    )(place, *operands)


def on_device(ctx_size, tp_size, hidden_in, w_q, w_k, w_v, event_pos):
    _, rows, _ = hidden_in.shape
    features = w_q.shape[1]
    ways = math.gcd(features // HD, ctx_size // 2)
    rest = ctx_size // ways
    ctx_me = lax.axis_index("ctx").astype(jnp.int32)
    tp_me = lax.axis_index("tp").astype(jnp.int32)
    core = ctx_me % 2
    place = jnp.stack([tp_me, ctx_me // rest, core, ctx_me])
    away = list(range(ways))

    def over_ctx(value, offset):
        return exchange(value, "ctx", ctx_size, offset) if offset else value

    def other_shares(own):
        shares = [own]
        bit = 1
        while bit < tp_size:
            shares += [exchange(share, "tp", tp_size, bit) for share in shares]
            bit *= 2
        return shares[1:]

    mine = lax.dynamic_index_in_dim(hidden_in, core, 0, keepdims=False)
    other = over_ctx(lax.dynamic_index_in_dim(hidden_in, 1 - core, 0, keepdims=False), 1)
    received = [other_shares(mine), other_shares(other)]

    start_k, start_v, start_q = own_products(hidden_in, other, [w_k, w_v, w_q], place, ways)

    spans = event_pos[:, 0] // (rows // 2)
    span_other = over_ctx(lax.dynamic_index_in_dim(spans, 1 - core, 0), 1)
    later = jnp.concatenate([place, lax.dynamic_index_in_dim(spans, core, 0), span_other])
    made_0 = {}
    for part in (away[::-2], away[-2::-2]):
        if part:
            made_0.update(
                rest_products(received, [0], [w_k, w_v], [start_k, start_v], later, ways, part, EXTRA)[0]
            )
    first = {a: over_ctx(made_0[a], a * rest) for a in away}
    ahead = over_ctx(made_0[0], rest // 2)
    asked = rest_products(received, [0], [w_q], [start_q], place, ways, away)
    received, asked = lax.optimization_barrier((received, asked))
    (made_1,) = rest_products(received, [1], [w_k, w_v], [start_k, start_v], place, ways, away)
    ahead_1 = over_ctx(made_1[0], rest // 2)
    for a in away:
        first[a], made_1[a] = lax.optimization_barrier((first[a], made_1[a]))

    def over_y(blocks):
        bit = rest // 2
        while bit > 1:
            for i in list(blocks):
                if i ^ bit not in blocks:
                    blocks[i ^ bit] = over_ctx(blocks[i], bit)
            bit //= 2
        return blocks

    blocks = {a * rest: first[a] for a in away}
    blocks[rest // 2] = ahead
    before = []
    for a in range(1, ways):
        value = lax.optimization_barrier((first[a], before))[0] if a == ways - 1 else first[a]
        before.append(over_ctx(value, rest // 2))
        blocks[a * rest + rest // 2] = before[-1]
    blocks = over_y(blocks)
    received, _ = lax.optimization_barrier((received, blocks[(min(1, ways - 1) * rest) ^ (rest // 2)]))
    asked += rest_products(received, [1], [w_q], [start_q], place, ways, away)
    asked = lax.optimization_barrier(asked)
    second = {}
    for a in away:
        value, _ = lax.optimization_barrier((made_1[a], (first[a], ahead)))
        second[a * rest + 1] = over_ctx(value, a * rest)
    queries = [{}, {}]
    for a in away:
        wait = (second[a * rest + 1], ahead_1) if a else ()
        if a == ways - 1:
            wait = (wait, [blocks[i] for i in sorted(blocks)])
        value, _ = lax.optimization_barrier((asked[0][a], wait))
        queries[0][a] = over_ctx(value, a * rest)
    for a in away:
        value, _ = lax.optimization_barrier((asked[1][a], queries[0][min(1, ways - 1)]))
        queries[1][a] = over_ctx(value, a * rest)
    table = span_table({i: (array, 0) for i, array in blocks.items()}, rows)
    second[rest // 2 + 1] = ahead_1
    blocks.update(over_y(second))
    blocks = {i: (array, 0) for i, array in blocks.items()}
    out = None
    for b in range(2):
        outs = attend(b, [queries[b][a] for a in range(ways)], blocks, table)
        pieces = {a: over_ctx(outs[a], a * rest + b) for a in away}
        out = assemble([pieces[a] for a in range(ways)], b, out, place)
    return out


def solution(mesh):
    sizes = dict(mesh.shape)
    placed = (P(None, "ctx", "tp"), P(None, "tp"), P(None, "tp"), P(None, "tp"), P(None, "ctx"))
    return jax.shard_map(
        functools.partial(on_device, sizes["ctx"], sizes["tp"]),
        mesh=mesh,
        in_specs=placed,
        out_specs=P(None, "ctx", "tp"),
        check_vma=False,
    )
```

```python
import functools
import math

import jax
import jax.numpy as jnp
from jax import lax
from jax.experimental import pallas as pl
from jax.experimental.pallas import tpu as pltpu
from jax.sharding import PartitionSpec as P

HD = 128
LOG2_E = 1.4426950408889634
HIDDEN = -1e30
VMEM_LIMIT = 44 * 2**20
ATTEND_LIMIT = 56 * 2**20


def exchange(value, axis, size, bit):
    return lax.ppermute(value, axis, [(i, i ^ bit) for i in range(size)])


EXTRA = 16


def own_body(weights, place, mine_ref, other_ref, *refs):
    flat_ref = refs[-1]
    rows = other_ref.shape[0]

    @pl.when(pl.program_id(0) == 0)
    def _():
        flat_ref[:rows] = mine_ref[0]
        flat_ref[rows:] = other_ref[...]

    for weight_ref, out_ref in zip(refs[:weights], refs[weights:-1]):
        result = jnp.dot(flat_ref[...], weight_ref[...], preferred_element_type=jnp.float32)
        out_ref[...] = result.reshape(2, rows, -1)


def own_products(hidden_in, other, weights, place, ways):
    rows, feats = other.shape
    features = weights[0].shape[1]
    width = features // ways
    return pl.pallas_call(
        functools.partial(own_body, len(weights)),
        out_shape=[jax.ShapeDtypeStruct((2, rows, features), jnp.float32)] * len(weights),
        grid_spec=pltpu.PrefetchScalarGridSpec(
            num_scalar_prefetch=1,
            grid=(ways,),
            in_specs=[
                pl.BlockSpec((1, rows, feats), lambda g, place: (place[2], 0, 0)),
                pl.BlockSpec((rows, feats), lambda g, place: (0, 0)),
            ]
            + [pl.BlockSpec((feats, width), lambda g, place: (place[0], g))] * len(weights),
            out_specs=[pl.BlockSpec((2, rows, width), lambda g, place: (0, 0, g))] * len(weights),
            scratch_shapes=[pltpu.VMEM((2 * rows, feats), jnp.bfloat16)],
        ),
        compiler_params=pltpu.CompilerParams(vmem_limit_bytes=VMEM_LIMIT),
        cost_estimate=pl.CostEstimate(
            flops=4 * rows * feats * features * len(weights),
            bytes_accessed=2 * feats * features * len(weights),
            transcendentals=0,
        ),
    )(place, hidden_in, other, *weights)


def rest_body(shares, weights, chunks, away, extra, place, *refs):
    inputs = refs[: shares * chunks]
    refs = refs[shares * chunks :]
    weight_refs, refs = refs[: weights * shares], refs[weights * shares :]
    start_refs, refs = refs[:weights], refs[weights:]
    out_refs, flats = refs[: chunks * len(away)], refs[chunks * len(away) :]
    rows, width = out_refs[0].shape
    rows -= extra
    width //= weights
    step = pl.program_id(0)
    if chunks > 1:

        @pl.when(step == 0)
        def _():
            for share in range(shares):
                for c in range(chunks):
                    flats[share][c * rows : (c + 1) * rows] = inputs[c * shares + share][...]

    else:
        flats = inputs
    made = []
    for n in range(weights):
        total = start_refs[n][...].reshape(chunks * rows, width)
        for share in range(shares):
            total += jnp.dot(
                flats[share][...], weight_refs[n * shares + share][...], preferred_element_type=jnp.float32
            )
        made.append(total.astype(jnp.bfloat16))
    for index in range(len(away)):

        @pl.when(step == index)
        def _():
            for c in range(chunks):
                for n in range(weights):
                    out_refs[c * len(away) + index][:rows, n * width : (n + 1) * width] = made[n][
                        c * rows : (c + 1) * rows
                    ]
            if extra:
                line = lax.broadcasted_iota(jnp.int32, (extra, weights * width), 0)
                spans = jnp.where(line < extra // 2, place[4], place[5]).astype(jnp.float32)
                out_refs[index][rows:] = spans.astype(jnp.bfloat16)


def rest_products(received, chosen, weights, starts, place, ways, away, extra=0):
    shares = len(received[0])
    rows, feats = received[0][0].shape
    width = weights[0].shape[1] // ways
    chunks = len(chosen)
    top = away[0]
    stride = away[1] - top if len(away) > 1 else 0

    def weight_map(share, i, place):
        return (place[0] ^ (share + 1), place[1] ^ (top + stride * i))

    in_specs = [pl.BlockSpec((rows, feats), lambda i, place: (0, 0))] * (shares * chunks)
    for _ in weights:
        for share in range(shares):
            in_specs.append(pl.BlockSpec((feats, width), functools.partial(weight_map, share)))
    in_specs += [
        pl.BlockSpec((chunks, rows, width), lambda i, place: (chosen[0] // chunks, 0, place[1] ^ (top + stride * i)))
    ] * len(weights)
    columns = width * len(weights)
    scratch = [pltpu.VMEM((chunks * rows, feats), jnp.bfloat16)] * (shares if chunks > 1 else 0)
    outs = pl.pallas_call(
        functools.partial(rest_body, shares, len(weights), chunks, away, extra),
        out_shape=[jax.ShapeDtypeStruct((rows + extra, columns), jnp.bfloat16)] * (chunks * len(away)),
        grid_spec=pltpu.PrefetchScalarGridSpec(
            num_scalar_prefetch=1,
            grid=(len(away),),
            in_specs=in_specs,
            out_specs=[pl.BlockSpec((rows + extra, columns), lambda i, place: (0, 0))] * (chunks * len(away)),
            scratch_shapes=scratch,
        ),
        compiler_params=pltpu.CompilerParams(vmem_limit_bytes=VMEM_LIMIT),
        cost_estimate=pl.CostEstimate(
            flops=2 * chunks * rows * feats * shares * columns * len(away),
            bytes_accessed=2 * feats * shares * columns * len(away),
            transcendentals=0,
        ),
    )(
        place,
        *[share for c in chosen for share in received[c]],
        *[weight for weight in weights for _ in range(shares)],
        *starts,
    )
    return [dict(zip(away, outs[c * len(away) : (c + 1) * len(away)])) for c in range(chunks)]


def attend_body(block, ways, slots, arrays, spans, tile, table, *refs):
    count = len(slots)
    query_refs = refs[:ways]
    block_refs = refs[ways : ways + arrays]
    out_refs = refs[ways + arrays : 2 * ways + arrays]
    ordered, asked, scores, highest, sums, total, position, sems = refs[2 * ways + arrays :]
    rows, width = out_refs[0].shape
    half = rows // 2
    heads = width // HD
    rest = count // ways

    copies = [[], []]
    for slot, (offset, array, row) in enumerate(slots):
        low = table[offset]
        for part, span in ((0, low), (1, spans - 1 - low)):
            copies[part].append(
                pltpu.make_async_copy(
                    block_refs[array].at[pl.ds(row + part * half, half)],
                    ordered.at[pl.ds(pl.multiple_of(span * half, 16), half)],
                    sems.at[2 * slot + part],
                )
            )
    for copy in copies[0] + copies[1]:
        copy.start()

    from_lane = lax.broadcasted_iota(jnp.int32, (half, 128), 0) - lax.broadcasted_iota(
        jnp.int32, (half, 128), 1
    )
    for a in range(ways):
        low = table[a * rest + block]
        here = slice(a * half, (a + 1) * half)
        for part, span in ((0, low), (1, spans - 1 - low)):
            asked[part, here] = query_refs[a][part * half : (part + 1) * half]
            position[part, here] = from_lane + span * half
    for copy in copies[0]:
        copy.wait()

    slope = LOG2_E / math.sqrt(HD)
    middle = spans * half // 2

    def starts(part):
        return range(0, middle * (part + 1), tile)

    def visible(unit, slot, column):
        piece = scores[slot, :, column : column + 128]
        if column < middle * unit[0]:
            return piece
        return jnp.where(position[unit[0]] >= column, piece, HIDDEN)

    def score_tile(unit, slot, start):
        part, h = unit
        if unit == (1, 0) and start == middle:
            for copy in copies[1]:
                copy.wait()
        scores[slot, :, start : start + tile] = lax.dot_general(
            asked[part, :, h * HD : (h + 1) * HD],
            ordered[start : start + tile, h * HD : (h + 1) * HD],
            (((1,), (1,)), ((), ())),
            preferred_element_type=jnp.float32,
        )
        top = None if start == 0 else highest[slot]
        for column in range(start, start + tile, 128):
            piece = visible(unit, slot, column)
            top = piece if top is None else jnp.maximum(top, piece)
        highest[slot] = top

    def value_tile(unit, slot, start):
        part, h = unit
        top = highest[slot]
        added = None if start == 0 else sums[slot]
        weights = []
        for column in range(start, start + tile, 128):
            piece = jnp.exp2((visible(unit, slot, column) - top) * slope)
            added = piece if added is None else added + piece
            weights.append(piece.astype(jnp.bfloat16))
        sums[slot] = added
        product = jnp.dot(
            jnp.concatenate(weights, axis=1),
            ordered[start : start + tile, width + h * HD : width + (h + 1) * HD],
            preferred_element_type=jnp.float32,
        )
        if start == 0:
            total[slot] = product
        else:
            total[slot] += product

    units = [(0, 0)] + [(1, h) for h in range(heads)] + [(0, h) for h in range(1, heads)]
    for n in range(len(units) + 1):
        todo = []
        if n < len(units):
            todo.append([functools.partial(score_tile, units[n], n % 2, start) for start in starts(units[n][0])])
        if n > 0:
            slot = (n - 1) % 2
            highest[slot] = jnp.broadcast_to(jnp.max(highest[slot], axis=1, keepdims=True), highest.shape[1:])
            todo.append([functools.partial(value_tile, units[n - 1], slot, start) for start in starts(units[n - 1][0])])
        for index in range(max(len(steps) for steps in todo)):
            for steps in todo:
                if index < len(steps):
                    steps[index]()
        if n > 0:
            part, h = units[n - 1]
            result = total[slot] / jnp.sum(sums[slot], axis=1, keepdims=True)
            for a in range(ways):
                out_refs[a][part * half : (part + 1) * half, h * HD : (h + 1) * HD] = result[
                    a * half : (a + 1) * half
                ].astype(jnp.bfloat16)


def attend(block, queries, blocks, table):
    rows, width = queries[0].shape
    ways, count = len(queries), len(blocks)
    arrays = []
    slots = []
    for offset in sorted(blocks):
        array, row = blocks[offset]
        if not any(array is other for other in arrays):
            arrays.append(array)
        slots.append((offset, [array is other for other in arrays].index(True), row))
    spans = 2 * count
    half = rows // 2
    length = count * rows
    tile = 8 * half
    heads = width // HD
    many = ways * half
    smem = pl.BlockSpec(memory_space=pltpu.SMEM)
    flops = 6 * many * heads * length * HD
    return pl.pallas_call(
        functools.partial(attend_body, block, ways, slots, len(arrays), spans, tile),
        out_shape=[jax.ShapeDtypeStruct((rows, width), jnp.bfloat16)] * ways,
        grid=(1,),
        in_specs=[smem]
        + [pl.BlockSpec((rows, width), lambda i: (0, 0))] * ways
        + [pl.BlockSpec(memory_space=pl.ANY)] * len(arrays),
        out_specs=[pl.BlockSpec((rows, width), lambda i: (0, 0))] * ways,
        scratch_shapes=[
            pltpu.VMEM((length, 2 * width), jnp.bfloat16),
            pltpu.VMEM((2, many, width), jnp.bfloat16),
            pltpu.VMEM((2, many, length), jnp.float32),
            pltpu.VMEM((2, many, 128), jnp.float32),
            pltpu.VMEM((2, many, 128), jnp.float32),
            pltpu.VMEM((2, many, HD), jnp.float32),
            pltpu.VMEM((2, many, 128), jnp.int32),
            pltpu.SemaphoreType.DMA((2 * count,)),
        ],
        compiler_params=pltpu.CompilerParams(vmem_limit_bytes=ATTEND_LIMIT),
        cost_estimate=pl.CostEstimate(
            flops=flops,
            bytes_accessed=4 * length * width + 4 * ways * rows * width,
            transcendentals=flops // (4 * HD),
        ),
    )(table, *queries, *arrays)


def table_body(offsets, *refs):
    table = refs[-1]
    for offset, ref in zip(offsets, refs):
        found = ref[...].astype(jnp.float32)
        for part in range(2):
            table[offset + part] = jnp.max(found[part * EXTRA // 2 : (part + 1) * EXTRA // 2]).astype(jnp.int32)


def span_table(blocks, rows):
    offsets = sorted(blocks)
    return pl.pallas_call(
        functools.partial(table_body, offsets),
        out_shape=jax.ShapeDtypeStruct((2 * len(offsets),), jnp.int32),
        grid=(1,),
        in_specs=[
            pl.BlockSpec((EXTRA, 128), functools.partial(lambda row, i: (row, 0), (blocks[i][1] + rows) // EXTRA))
            for i in offsets
        ],
        out_specs=pl.BlockSpec(memory_space=pltpu.SMEM),
        compiler_params=pltpu.CompilerParams(vmem_limit_bytes=VMEM_LIMIT),
    )(*[blocks[i][0] for i in offsets])


def assemble_body(ways, place, *refs):
    for a in range(ways):

        @pl.when(pl.program_id(0) == a)
        def _():
            refs[-1][0] = refs[ways - 1 - a][...]


def assemble(pieces, b, before, place):
    ways = len(pieces)
    rows, width = pieces[0].shape
    in_specs = [pl.BlockSpec((rows, width), lambda a, place: (0, 0))] * ways
    operands = list(pieces[::-1])
    aliases = {}
    if before is not None:
        in_specs.append(pl.BlockSpec(memory_space=pl.ANY))
        operands.append(before)
        aliases = {1 + ways: 0}
    return pl.pallas_call(
        functools.partial(assemble_body, ways),
        out_shape=jax.ShapeDtypeStruct((2, rows, ways * width), jnp.bfloat16),
        grid_spec=pltpu.PrefetchScalarGridSpec(
            num_scalar_prefetch=1,
            grid=(ways,),
            in_specs=in_specs,
            out_specs=pl.BlockSpec((1, rows, width), lambda a, place: (place[2] ^ b, 0, place[1] ^ a)),
        ),
        input_output_aliases=aliases,
        compiler_params=pltpu.CompilerParams(vmem_limit_bytes=VMEM_LIMIT),
    )(place, *operands)


def on_device(ctx_size, tp_size, hidden_in, w_q, w_k, w_v, event_pos):
    _, rows, _ = hidden_in.shape
    features = w_q.shape[1]
    ways = math.gcd(features // HD, ctx_size // 2)
    rest = ctx_size // ways
    ctx_me = lax.axis_index("ctx").astype(jnp.int32)
    tp_me = lax.axis_index("tp").astype(jnp.int32)
    core = ctx_me % 2
    place = jnp.stack([tp_me, ctx_me // rest, core, ctx_me])
    away = list(range(ways))

    def over_ctx(value, offset):
        return exchange(value, "ctx", ctx_size, offset) if offset else value

    def other_shares(own):
        shares = [own]
        bit = 1
        while bit < tp_size:
            shares += [exchange(share, "tp", tp_size, bit) for share in shares]
            bit *= 2
        return shares[1:]

    mine = lax.dynamic_index_in_dim(hidden_in, core, 0, keepdims=False)
    other = over_ctx(lax.dynamic_index_in_dim(hidden_in, 1 - core, 0, keepdims=False), 1)
    received = [other_shares(mine), other_shares(other)]

    start_k, start_v, start_q = own_products(hidden_in, other, [w_k, w_v, w_q], place, ways)

    spans = event_pos[:, 0] // (rows // 2)
    span_other = over_ctx(lax.dynamic_index_in_dim(spans, 1 - core, 0), 1)
    later = jnp.concatenate([place, lax.dynamic_index_in_dim(spans, core, 0), span_other])
    made_0 = {}
    for part in (away[::-2], away[-2::-2]):
        if part:
            made_0.update(
                rest_products(received, [0], [w_k, w_v], [start_k, start_v], later, ways, part, EXTRA)[0]
            )
    first = {a: over_ctx(made_0[a], a * rest) for a in away}
    ahead = over_ctx(made_0[0], rest // 2)
    asked = rest_products(received, [0], [w_q], [start_q], place, ways, away)
    received, asked = lax.optimization_barrier((received, asked))
    (made_1,) = rest_products(received, [1], [w_k, w_v], [start_k, start_v], place, ways, away)
    ahead_1 = over_ctx(made_1[0], rest // 2)
    for a in away:
        first[a], made_1[a] = lax.optimization_barrier((first[a], made_1[a]))

    def over_y(blocks):
        bit = rest // 2
        while bit > 1:
            for i in list(blocks):
                if i ^ bit not in blocks:
                    blocks[i ^ bit] = over_ctx(blocks[i], bit)
            bit //= 2
        return blocks

    blocks = {a * rest: first[a] for a in away}
    blocks[rest // 2] = ahead
    before = []
    for a in range(1, ways - 1):
        before.append(over_ctx(first[a], rest // 2))
        blocks[a * rest + rest // 2] = before[-1]
    received, _ = lax.optimization_barrier((received, before[:1]))
    asked += rest_products(received, [1], [w_q], [start_q], place, ways, away)
    if ways > 1:
        value, _ = lax.optimization_barrier((first[ways - 1], (before, asked[1])))
        blocks[(ways - 1) * rest + rest // 2] = over_ctx(value, rest // 2)
    blocks = over_y(blocks)
    second = {}
    for a in away:
        value, _ = lax.optimization_barrier((made_1[a], (first[a], ahead)))
        second[a * rest + 1] = over_ctx(value, a * rest)
    queries = [{}, {}]
    for a in away:
        wait = (second[a * rest + 1], ahead_1) if a else ()
        if a == ways - 1:
            wait = (wait, [blocks[i] for i in sorted(blocks)])
        value, _ = lax.optimization_barrier((asked[0][a], wait))
        queries[0][a] = over_ctx(value, a * rest)
    for a in away:
        value, _ = lax.optimization_barrier((asked[1][a], queries[0][min(1, ways - 1)]))
        queries[1][a] = over_ctx(value, a * rest)
    table = span_table({i: (array, 0) for i, array in blocks.items()}, rows)
    second[rest // 2 + 1] = ahead_1
    blocks.update(over_y(second))
    blocks = {i: (array, 0) for i, array in blocks.items()}
    out = None
    for b in range(2):
        outs = attend(b, [queries[b][a] for a in range(ways)], blocks, table)
        pieces = {a: over_ctx(outs[a], a * rest + b) for a in away}
        out = assemble([pieces[a] for a in range(ways)], b, out, place)
    return out


def solution(mesh):
    sizes = dict(mesh.shape)
    placed = (P(None, "ctx", "tp"), P(None, "tp"), P(None, "tp"), P(None, "tp"), P(None, "ctx"))
    return jax.shard_map(
        functools.partial(on_device, sizes["ctx"], sizes["tp"]),
        mesh=mesh,
        in_specs=placed,
        out_specs=P(None, "ctx", "tp"),
        check_vma=False,
    )
```

```python
import functools
import math

import jax
import jax.numpy as jnp
from jax import lax
from jax.experimental import pallas as pl
from jax.experimental.pallas import tpu as pltpu
from jax.sharding import PartitionSpec as P

HD = 128
LOG2_E = 1.4426950408889634
HIDDEN = -1e30
VMEM_LIMIT = 44 * 2**20
ATTEND_LIMIT = 56 * 2**20


def exchange(value, axis, size, bit):
    return lax.ppermute(value, axis, [(i, i ^ bit) for i in range(size)])


EXTRA = 16


def own_body(weights, place, mine_ref, other_ref, *refs):
    flat_ref = refs[-1]
    rows = other_ref.shape[0]

    @pl.when(pl.program_id(0) == 0)
    def _():
        flat_ref[:rows] = mine_ref[0]
        flat_ref[rows:] = other_ref[...]

    for weight_ref, out_ref in zip(refs[:weights], refs[weights:-1]):
        result = jnp.dot(flat_ref[...], weight_ref[...], preferred_element_type=jnp.float32)
        out_ref[...] = result.reshape(2, rows, -1)


def own_products(hidden_in, other, weights, place, ways):
    rows, feats = other.shape
    features = weights[0].shape[1]
    width = features // ways
    return pl.pallas_call(
        functools.partial(own_body, len(weights)),
        out_shape=[jax.ShapeDtypeStruct((2, rows, features), jnp.float32)] * len(weights),
        grid_spec=pltpu.PrefetchScalarGridSpec(
            num_scalar_prefetch=1,
            grid=(ways,),
            in_specs=[
                pl.BlockSpec((1, rows, feats), lambda g, place: (place[2], 0, 0)),
                pl.BlockSpec((rows, feats), lambda g, place: (0, 0)),
            ]
            + [pl.BlockSpec((feats, width), lambda g, place: (place[0], g))] * len(weights),
            out_specs=[pl.BlockSpec((2, rows, width), lambda g, place: (0, 0, g))] * len(weights),
            scratch_shapes=[pltpu.VMEM((2 * rows, feats), jnp.bfloat16)],
        ),
        compiler_params=pltpu.CompilerParams(vmem_limit_bytes=VMEM_LIMIT),
        cost_estimate=pl.CostEstimate(
            flops=4 * rows * feats * features * len(weights),
            bytes_accessed=2 * feats * features * len(weights),
            transcendentals=0,
        ),
    )(place, hidden_in, other, *weights)


def rest_body(shares, weights, chunks, away, extra, place, *refs):
    inputs = refs[: shares * chunks]
    refs = refs[shares * chunks :]
    weight_refs, refs = refs[: weights * shares], refs[weights * shares :]
    start_refs, refs = refs[:weights], refs[weights:]
    out_refs, flats = refs[: chunks * len(away)], refs[chunks * len(away) :]
    rows, width = out_refs[0].shape
    rows -= extra
    width //= weights
    step = pl.program_id(0)
    if chunks > 1:

        @pl.when(step == 0)
        def _():
            for share in range(shares):
                for c in range(chunks):
                    flats[share][c * rows : (c + 1) * rows] = inputs[c * shares + share][...]

    else:
        flats = inputs
    made = []
    for n in range(weights):
        total = start_refs[n][...].reshape(chunks * rows, width)
        for share in range(shares):
            total += jnp.dot(
                flats[share][...], weight_refs[n * shares + share][...], preferred_element_type=jnp.float32
            )
        made.append(total.astype(jnp.bfloat16))
    for index in range(len(away)):

        @pl.when(step == index)
        def _():
            for c in range(chunks):
                for n in range(weights):
                    out_refs[c * len(away) + index][:rows, n * width : (n + 1) * width] = made[n][
                        c * rows : (c + 1) * rows
                    ]
            if extra:
                line = lax.broadcasted_iota(jnp.int32, (extra, weights * width), 0)
                spans = jnp.where(line < extra // 2, place[4], place[5]).astype(jnp.float32)
                out_refs[index][rows:] = spans.astype(jnp.bfloat16)


def rest_products(received, chosen, weights, starts, place, ways, away, extra=0):
    shares = len(received[0])
    rows, feats = received[0][0].shape
    width = weights[0].shape[1] // ways
    chunks = len(chosen)
    top = away[0]
    stride = away[1] - top if len(away) > 1 else 0

    def weight_map(share, i, place):
        return (place[0] ^ (share + 1), place[1] ^ (top + stride * i))

    in_specs = [pl.BlockSpec((rows, feats), lambda i, place: (0, 0))] * (shares * chunks)
    for _ in weights:
        for share in range(shares):
            in_specs.append(pl.BlockSpec((feats, width), functools.partial(weight_map, share)))
    in_specs += [
        pl.BlockSpec((chunks, rows, width), lambda i, place: (chosen[0] // chunks, 0, place[1] ^ (top + stride * i)))
    ] * len(weights)
    columns = width * len(weights)
    scratch = [pltpu.VMEM((chunks * rows, feats), jnp.bfloat16)] * (shares if chunks > 1 else 0)
    outs = pl.pallas_call(
        functools.partial(rest_body, shares, len(weights), chunks, away, extra),
        out_shape=[jax.ShapeDtypeStruct((rows + extra, columns), jnp.bfloat16)] * (chunks * len(away)),
        grid_spec=pltpu.PrefetchScalarGridSpec(
            num_scalar_prefetch=1,
            grid=(len(away),),
            in_specs=in_specs,
            out_specs=[pl.BlockSpec((rows + extra, columns), lambda i, place: (0, 0))] * (chunks * len(away)),
            scratch_shapes=scratch,
        ),
        compiler_params=pltpu.CompilerParams(vmem_limit_bytes=VMEM_LIMIT),
        cost_estimate=pl.CostEstimate(
            flops=2 * chunks * rows * feats * shares * columns * len(away),
            bytes_accessed=2 * feats * shares * columns * len(away),
            transcendentals=0,
        ),
    )(
        place,
        *[share for c in chosen for share in received[c]],
        *[weight for weight in weights for _ in range(shares)],
        *starts,
    )
    return [dict(zip(away, outs[c * len(away) : (c + 1) * len(away)])) for c in range(chunks)]


def attend_body(block, ways, slots, arrays, spans, tile, table, *refs):
    count = len(slots)
    query_refs = refs[:ways]
    block_refs = refs[ways : ways + arrays]
    out_refs = refs[ways + arrays : 2 * ways + arrays]
    ordered, asked, scores, highest, sums, total, position, sems = refs[2 * ways + arrays :]
    rows, width = out_refs[0].shape
    half = rows // 2
    heads = width // HD
    rest = count // ways

    copies = [[], []]
    for slot, (offset, array, row) in enumerate(slots):
        low = table[offset]
        for part, span in ((0, low), (1, spans - 1 - low)):
            copies[part].append(
                pltpu.make_async_copy(
                    block_refs[array].at[pl.ds(row + part * half, half)],
                    ordered.at[pl.ds(pl.multiple_of(span * half, 16), half)],
                    sems.at[2 * slot + part],
                )
            )
    for copy in copies[0] + copies[1]:
        copy.start()

    from_lane = lax.broadcasted_iota(jnp.int32, (half, 128), 0) - lax.broadcasted_iota(
        jnp.int32, (half, 128), 1
    )
    for a in range(ways):
        low = table[a * rest + block]
        here = slice(a * half, (a + 1) * half)
        for part, span in ((0, low), (1, spans - 1 - low)):
            asked[part, here] = query_refs[a][part * half : (part + 1) * half]
            position[part, here] = from_lane + span * half
    for copy in copies[0]:
        copy.wait()

    slope = LOG2_E / math.sqrt(HD)
    middle = spans * half // 2

    def starts(part):
        return range(0, middle * (part + 1), tile)

    def visible(unit, slot, column):
        piece = scores[slot, :, column : column + 128]
        if column < middle * unit[0]:
            return piece
        return jnp.where(position[unit[0]] >= column, piece, HIDDEN)

    def score_tile(unit, slot, start):
        part, h = unit
        if unit == (1, 0) and start == middle:
            for copy in copies[1]:
                copy.wait()
        scores[slot, :, start : start + tile] = lax.dot_general(
            asked[part, :, h * HD : (h + 1) * HD],
            ordered[start : start + tile, h * HD : (h + 1) * HD],
            (((1,), (1,)), ((), ())),
            preferred_element_type=jnp.float32,
        )
        top = None if start == 0 else highest[slot]
        for column in range(start, start + tile, 128):
            piece = visible(unit, slot, column)
            top = piece if top is None else jnp.maximum(top, piece)
        highest[slot] = top

    def value_tile(unit, slot, start):
        part, h = unit
        top = highest[slot]
        added = None if start == 0 else sums[slot]
        weights = []
        for column in range(start, start + tile, 128):
            piece = jnp.exp2((visible(unit, slot, column) - top) * slope)
            added = piece if added is None else added + piece
            weights.append(piece.astype(jnp.bfloat16))
        sums[slot] = added
        product = jnp.dot(
            jnp.concatenate(weights, axis=1),
            ordered[start : start + tile, width + h * HD : width + (h + 1) * HD],
            preferred_element_type=jnp.float32,
        )
        if start == 0:
            total[slot] = product
        else:
            total[slot] += product

    units = [(0, 0)] + [(1, h) for h in range(heads)] + [(0, h) for h in range(1, heads)]
    for n in range(len(units) + 1):
        todo = []
        if n < len(units):
            todo.append([functools.partial(score_tile, units[n], n % 2, start) for start in starts(units[n][0])])
        if n > 0:
            slot = (n - 1) % 2
            highest[slot] = jnp.broadcast_to(jnp.max(highest[slot], axis=1, keepdims=True), highest.shape[1:])
            todo.append([functools.partial(value_tile, units[n - 1], slot, start) for start in starts(units[n - 1][0])])
        for index in range(max(len(steps) for steps in todo)):
            for steps in todo:
                if index < len(steps):
                    steps[index]()
        if n > 0:
            part, h = units[n - 1]
            result = total[slot] / jnp.sum(sums[slot], axis=1, keepdims=True)
            for a in range(ways):
                out_refs[a][part * half : (part + 1) * half, h * HD : (h + 1) * HD] = result[
                    a * half : (a + 1) * half
                ].astype(jnp.bfloat16)


def attend(block, queries, blocks, table):
    rows, width = queries[0].shape
    ways, count = len(queries), len(blocks)
    arrays = []
    slots = []
    for offset in sorted(blocks):
        array, row = blocks[offset]
        if not any(array is other for other in arrays):
            arrays.append(array)
        slots.append((offset, [array is other for other in arrays].index(True), row))
    spans = 2 * count
    half = rows // 2
    length = count * rows
    tile = 8 * half
    heads = width // HD
    many = ways * half
    smem = pl.BlockSpec(memory_space=pltpu.SMEM)
    flops = 6 * many * heads * length * HD
    return pl.pallas_call(
        functools.partial(attend_body, block, ways, slots, len(arrays), spans, tile),
        out_shape=[jax.ShapeDtypeStruct((rows, width), jnp.bfloat16)] * ways,
        grid=(1,),
        in_specs=[smem]
        + [pl.BlockSpec((rows, width), lambda i: (0, 0))] * ways
        + [pl.BlockSpec(memory_space=pl.ANY)] * len(arrays),
        out_specs=[pl.BlockSpec((rows, width), lambda i: (0, 0))] * ways,
        scratch_shapes=[
            pltpu.VMEM((length, 2 * width), jnp.bfloat16),
            pltpu.VMEM((2, many, width), jnp.bfloat16),
            pltpu.VMEM((2, many, length), jnp.float32),
            pltpu.VMEM((2, many, 128), jnp.float32),
            pltpu.VMEM((2, many, 128), jnp.float32),
            pltpu.VMEM((2, many, HD), jnp.float32),
            pltpu.VMEM((2, many, 128), jnp.int32),
            pltpu.SemaphoreType.DMA((2 * count,)),
        ],
        compiler_params=pltpu.CompilerParams(vmem_limit_bytes=ATTEND_LIMIT),
        cost_estimate=pl.CostEstimate(
            flops=flops,
            bytes_accessed=4 * length * width + 4 * ways * rows * width,
            transcendentals=flops // (4 * HD),
        ),
    )(table, *queries, *arrays)


def table_body(offsets, *refs):
    table = refs[-1]
    for offset, ref in zip(offsets, refs):
        found = ref[...].astype(jnp.float32)
        for part in range(2):
            table[offset + part] = jnp.max(found[part * EXTRA // 2 : (part + 1) * EXTRA // 2]).astype(jnp.int32)


def span_table(blocks, rows):
    offsets = sorted(blocks)
    return pl.pallas_call(
        functools.partial(table_body, offsets),
        out_shape=jax.ShapeDtypeStruct((2 * len(offsets),), jnp.int32),
        grid=(1,),
        in_specs=[
            pl.BlockSpec((EXTRA, 128), functools.partial(lambda row, i: (row, 0), (blocks[i][1] + rows) // EXTRA))
            for i in offsets
        ],
        out_specs=pl.BlockSpec(memory_space=pltpu.SMEM),
        compiler_params=pltpu.CompilerParams(vmem_limit_bytes=VMEM_LIMIT),
    )(*[blocks[i][0] for i in offsets])


def assemble_body(ways, place, *refs):
    for a in range(ways):

        @pl.when(pl.program_id(0) == a)
        def _():
            refs[-1][0] = refs[ways - 1 - a][...]


def assemble(pieces, b, before, place):
    ways = len(pieces)
    rows, width = pieces[0].shape
    in_specs = [pl.BlockSpec((rows, width), lambda a, place: (0, 0))] * ways
    operands = list(pieces[::-1])
    aliases = {}
    if before is not None:
        in_specs.append(pl.BlockSpec(memory_space=pl.ANY))
        operands.append(before)
        aliases = {1 + ways: 0}
    return pl.pallas_call(
        functools.partial(assemble_body, ways),
        out_shape=jax.ShapeDtypeStruct((2, rows, ways * width), jnp.bfloat16),
        grid_spec=pltpu.PrefetchScalarGridSpec(
            num_scalar_prefetch=1,
            grid=(ways,),
            in_specs=in_specs,
            out_specs=pl.BlockSpec((1, rows, width), lambda a, place: (place[2] ^ b, 0, place[1] ^ a)),
        ),
        input_output_aliases=aliases,
        compiler_params=pltpu.CompilerParams(vmem_limit_bytes=VMEM_LIMIT),
    )(place, *operands)


def on_device(ctx_size, tp_size, hidden_in, w_q, w_k, w_v, event_pos):
    _, rows, _ = hidden_in.shape
    features = w_q.shape[1]
    ways = math.gcd(features // HD, ctx_size // 2)
    rest = ctx_size // ways
    ctx_me = lax.axis_index("ctx").astype(jnp.int32)
    tp_me = lax.axis_index("tp").astype(jnp.int32)
    core = ctx_me % 2
    place = jnp.stack([tp_me, ctx_me // rest, core, ctx_me])
    away = list(range(ways))

    def over_ctx(value, offset):
        return exchange(value, "ctx", ctx_size, offset) if offset else value

    def other_shares(own):
        shares = [own]
        bit = 1
        while bit < tp_size:
            shares += [exchange(share, "tp", tp_size, bit) for share in shares]
            bit *= 2
        return shares[1:]

    mine = lax.dynamic_index_in_dim(hidden_in, core, 0, keepdims=False)
    other = over_ctx(lax.dynamic_index_in_dim(hidden_in, 1 - core, 0, keepdims=False), 1)
    received = [other_shares(mine), other_shares(other)]

    start_k, start_v, start_q = own_products(hidden_in, other, [w_k, w_v, w_q], place, ways)

    spans = event_pos[:, 0] // (rows // 2)
    span_other = over_ctx(lax.dynamic_index_in_dim(spans, 1 - core, 0), 1)
    later = jnp.concatenate([place, lax.dynamic_index_in_dim(spans, core, 0), span_other])
    made_0 = {}
    for part in (away[: ways // 2 - 1 : -1] or away, away[: ways // 2][::-1] if ways > 1 else []):
        if part:
            made_0.update(
                rest_products(received, [0], [w_k, w_v], [start_k, start_v], later, ways, part, EXTRA)[0]
            )
    first = {a: over_ctx(made_0[a], a * rest) for a in away}
    ahead = over_ctx(made_0[0], rest // 2)
    asked = rest_products(received, [0], [w_q], [start_q], place, ways, away)
    received, asked = lax.optimization_barrier((received, asked))
    (made_1,) = rest_products(received, [1], [w_k, w_v], [start_k, start_v], place, ways, away)
    ahead_1 = over_ctx(made_1[0], rest // 2)
    for a in away:
        first[a], made_1[a] = lax.optimization_barrier((first[a], made_1[a]))
    received, ahead_1 = lax.optimization_barrier((received, ahead_1))
    asked += rest_products(received, [1], [w_q], [start_q], place, ways, away)

    def over_y(blocks):
        bit = rest // 2
        while bit > 1:
            for i in list(blocks):
                if i ^ bit not in blocks:
                    blocks[i ^ bit] = over_ctx(blocks[i], bit)
            bit //= 2
        return blocks

    blocks = {a * rest: first[a] for a in away}
    blocks[rest // 2] = ahead
    before = []
    for a in range(1, ways):
        value = lax.optimization_barrier((first[a], before))[0] if a == ways - 1 else first[a]
        before.append(over_ctx(value, rest // 2))
        blocks[a * rest + rest // 2] = before[-1]
    blocks = over_y(blocks)
    second = {}
    for a in away:
        value, _ = lax.optimization_barrier((made_1[a], (first[a], ahead)))
        second[a * rest + 1] = over_ctx(value, a * rest)
    queries = [{}, {}]
    for a in away:
        wait = (second[a * rest + 1], ahead_1) if a else ()
        if a == ways - 1:
            wait = (wait, [blocks[i] for i in sorted(blocks)])
        value, _ = lax.optimization_barrier((asked[0][a], wait))
        queries[0][a] = over_ctx(value, a * rest)
    for a in away:
        value, _ = lax.optimization_barrier((asked[1][a], queries[0][a]))
        queries[1][a] = over_ctx(value, a * rest)
    table = span_table({i: (array, 0) for i, array in blocks.items()}, rows)
    second[rest // 2 + 1] = ahead_1
    blocks.update(over_y(second))
    blocks = {i: (array, 0) for i, array in blocks.items()}
    out = None
    for b in range(2):
        outs = attend(b, [queries[b][a] for a in range(ways)], blocks, table)
        pieces = {a: over_ctx(outs[a], a * rest + b) for a in away}
        out = assemble([pieces[a] for a in range(ways)], b, out, place)
    return out


def solution(mesh):
    sizes = dict(mesh.shape)
    placed = (P(None, "ctx", "tp"), P(None, "tp"), P(None, "tp"), P(None, "tp"), P(None, "ctx"))
    return jax.shard_map(
        functools.partial(on_device, sizes["ctx"], sizes["tp"]),
        mesh=mesh,
        in_specs=placed,
        out_specs=P(None, "ctx", "tp"),
        check_vma=False,
    )
```

```python
import functools
import math

import jax
import jax.numpy as jnp
from jax import lax
from jax.experimental import pallas as pl
from jax.experimental.pallas import tpu as pltpu
from jax.sharding import PartitionSpec as P

HD = 128
LOG2_E = 1.4426950408889634
HIDDEN = -1e30
VMEM_LIMIT = 44 * 2**20
ATTEND_LIMIT = 56 * 2**20


def exchange(value, axis, size, bit):
    return lax.ppermute(value, axis, [(i, i ^ bit) for i in range(size)])


EXTRA = 16


def own_body(weights, place, mine_ref, other_ref, *refs):
    flat_ref = refs[-1]
    rows = other_ref.shape[0]

    @pl.when(pl.program_id(0) == 0)
    def _():
        flat_ref[:rows] = mine_ref[0]
        flat_ref[rows:] = other_ref[...]

    for weight_ref, out_ref in zip(refs[:weights], refs[weights:-1]):
        result = jnp.dot(flat_ref[...], weight_ref[...], preferred_element_type=jnp.float32)
        out_ref[...] = result.reshape(2, rows, -1)


def own_products(hidden_in, other, weights, place, ways):
    rows, feats = other.shape
    features = weights[0].shape[1]
    width = features // ways
    return pl.pallas_call(
        functools.partial(own_body, len(weights)),
        out_shape=[jax.ShapeDtypeStruct((2, rows, features), jnp.float32)] * len(weights),
        grid_spec=pltpu.PrefetchScalarGridSpec(
            num_scalar_prefetch=1,
            grid=(ways,),
            in_specs=[
                pl.BlockSpec((1, rows, feats), lambda g, place: (place[2], 0, 0)),
                pl.BlockSpec((rows, feats), lambda g, place: (0, 0)),
            ]
            + [pl.BlockSpec((feats, width), lambda g, place: (place[0], g))] * len(weights),
            out_specs=[pl.BlockSpec((2, rows, width), lambda g, place: (0, 0, g))] * len(weights),
            scratch_shapes=[pltpu.VMEM((2 * rows, feats), jnp.bfloat16)],
        ),
        compiler_params=pltpu.CompilerParams(vmem_limit_bytes=VMEM_LIMIT),
        cost_estimate=pl.CostEstimate(
            flops=4 * rows * feats * features * len(weights),
            bytes_accessed=2 * feats * features * len(weights),
            transcendentals=0,
        ),
    )(place, hidden_in, other, *weights)


def rest_body(shares, weights, chunks, away, extra, place, *refs):
    inputs = refs[: shares * chunks]
    refs = refs[shares * chunks :]
    weight_refs, refs = refs[: weights * shares], refs[weights * shares :]
    start_refs, refs = refs[:weights], refs[weights:]
    out_refs, flats = refs[: chunks * len(away)], refs[chunks * len(away) :]
    rows, width = out_refs[0].shape
    rows -= extra
    width //= weights
    step = pl.program_id(0)
    if chunks > 1:

        @pl.when(step == 0)
        def _():
            for share in range(shares):
                for c in range(chunks):
                    flats[share][c * rows : (c + 1) * rows] = inputs[c * shares + share][...]

    else:
        flats = inputs
    made = []
    for n in range(weights):
        total = start_refs[n][...].reshape(chunks * rows, width)
        for share in range(shares):
            total += jnp.dot(
                flats[share][...], weight_refs[n * shares + share][...], preferred_element_type=jnp.float32
            )
        made.append(total.astype(jnp.bfloat16))
    for index in range(len(away)):

        @pl.when(step == index)
        def _():
            for c in range(chunks):
                for n in range(weights):
                    out_refs[c * len(away) + index][:rows, n * width : (n + 1) * width] = made[n][
                        c * rows : (c + 1) * rows
                    ]
            if extra:
                line = lax.broadcasted_iota(jnp.int32, (extra, weights * width), 0)
                spans = jnp.where(line < extra // 2, place[4], place[5]).astype(jnp.float32)
                out_refs[index][rows:] = spans.astype(jnp.bfloat16)


def rest_products(received, chosen, weights, starts, place, ways, away, extra=0):
    shares = len(received[0])
    rows, feats = received[0][0].shape
    width = weights[0].shape[1] // ways
    chunks = len(chosen)
    top = away[0]
    stride = away[1] - top if len(away) > 1 else 0

    def weight_map(share, i, place):
        return (place[0] ^ (share + 1), place[1] ^ (top + stride * i))

    in_specs = [pl.BlockSpec((rows, feats), lambda i, place: (0, 0))] * (shares * chunks)
    for _ in weights:
        for share in range(shares):
            in_specs.append(pl.BlockSpec((feats, width), functools.partial(weight_map, share)))
    in_specs += [
        pl.BlockSpec((chunks, rows, width), lambda i, place: (chosen[0] // chunks, 0, place[1] ^ (top + stride * i)))
    ] * len(weights)
    columns = width * len(weights)
    scratch = [pltpu.VMEM((chunks * rows, feats), jnp.bfloat16)] * (shares if chunks > 1 else 0)
    outs = pl.pallas_call(
        functools.partial(rest_body, shares, len(weights), chunks, away, extra),
        out_shape=[jax.ShapeDtypeStruct((rows + extra, columns), jnp.bfloat16)] * (chunks * len(away)),
        grid_spec=pltpu.PrefetchScalarGridSpec(
            num_scalar_prefetch=1,
            grid=(len(away),),
            in_specs=in_specs,
            out_specs=[pl.BlockSpec((rows + extra, columns), lambda i, place: (0, 0))] * (chunks * len(away)),
            scratch_shapes=scratch,
        ),
        compiler_params=pltpu.CompilerParams(vmem_limit_bytes=VMEM_LIMIT),
        cost_estimate=pl.CostEstimate(
            flops=2 * chunks * rows * feats * shares * columns * len(away),
            bytes_accessed=2 * feats * shares * columns * len(away),
            transcendentals=0,
        ),
    )(
        place,
        *[share for c in chosen for share in received[c]],
        *[weight for weight in weights for _ in range(shares)],
        *starts,
    )
    return [dict(zip(away, outs[c * len(away) : (c + 1) * len(away)])) for c in range(chunks)]


def attend_body(block, ways, slots, arrays, spans, tile, table, *refs):
    count = len(slots)
    query_refs = refs[:ways]
    block_refs = refs[ways : ways + arrays]
    out_refs = refs[ways + arrays : 2 * ways + arrays]
    ordered, asked, scores, highest, sums, total, position, sems = refs[2 * ways + arrays :]
    rows, width = out_refs[0].shape
    half = rows // 2
    heads = width // HD
    rest = count // ways

    copies = [[], []]
    for slot, (offset, array, row) in enumerate(slots):
        low = table[offset]
        for part, span in ((0, low), (1, spans - 1 - low)):
            copies[part].append(
                pltpu.make_async_copy(
                    block_refs[array].at[pl.ds(row + part * half, half)],
                    ordered.at[pl.ds(pl.multiple_of(span * half, 16), half)],
                    sems.at[2 * slot + part],
                )
            )
    for copy in copies[0] + copies[1]:
        copy.start()

    from_lane = lax.broadcasted_iota(jnp.int32, (half, 128), 0) - lax.broadcasted_iota(
        jnp.int32, (half, 128), 1
    )
    for a in range(ways):
        low = table[a * rest + block]
        here = slice(a * half, (a + 1) * half)
        for part, span in ((0, low), (1, spans - 1 - low)):
            asked[part, here] = query_refs[a][part * half : (part + 1) * half]
            position[part, here] = from_lane + span * half
    for copy in copies[0]:
        copy.wait()

    slope = LOG2_E / math.sqrt(HD)
    middle = spans * half // 2

    def starts(part):
        return range(0, middle * (part + 1), tile)

    def visible(unit, slot, column):
        piece = scores[slot, :, column : column + 128]
        if column < middle * unit[0]:
            return piece
        return jnp.where(position[unit[0]] >= column, piece, HIDDEN)

    def score_tile(unit, slot, start):
        part, h = unit
        if unit == (1, 0) and start == middle:
            for copy in copies[1]:
                copy.wait()
        scores[slot, :, start : start + tile] = lax.dot_general(
            asked[part, :, h * HD : (h + 1) * HD],
            ordered[start : start + tile, h * HD : (h + 1) * HD],
            (((1,), (1,)), ((), ())),
            preferred_element_type=jnp.float32,
        )
        top = None if start == 0 else highest[slot]
        for column in range(start, start + tile, 128):
            piece = visible(unit, slot, column)
            top = piece if top is None else jnp.maximum(top, piece)
        highest[slot] = top

    def value_tile(unit, slot, start):
        part, h = unit
        top = highest[slot]
        added = None if start == 0 else sums[slot]
        weights = []
        for column in range(start, start + tile, 128):
            piece = jnp.exp2((visible(unit, slot, column) - top) * slope)
            added = piece if added is None else added + piece
            weights.append(piece.astype(jnp.bfloat16))
        sums[slot] = added
        product = jnp.dot(
            jnp.concatenate(weights, axis=1),
            ordered[start : start + tile, width + h * HD : width + (h + 1) * HD],
            preferred_element_type=jnp.float32,
        )
        if start == 0:
            total[slot] = product
        else:
            total[slot] += product

    units = [(0, 0)] + [(1, h) for h in range(heads)] + [(0, h) for h in range(1, heads)]
    for n in range(len(units) + 1):
        todo = []
        if n < len(units):
            todo.append([functools.partial(score_tile, units[n], n % 2, start) for start in starts(units[n][0])])
        if n > 0:
            slot = (n - 1) % 2
            highest[slot] = jnp.broadcast_to(jnp.max(highest[slot], axis=1, keepdims=True), highest.shape[1:])
            todo.append([functools.partial(value_tile, units[n - 1], slot, start) for start in starts(units[n - 1][0])])
        for index in range(max(len(steps) for steps in todo)):
            for steps in todo:
                if index < len(steps):
                    steps[index]()
        if n > 0:
            part, h = units[n - 1]
            result = total[slot] / jnp.sum(sums[slot], axis=1, keepdims=True)
            for a in range(ways):
                out_refs[a][part * half : (part + 1) * half, h * HD : (h + 1) * HD] = result[
                    a * half : (a + 1) * half
                ].astype(jnp.bfloat16)


def attend(block, queries, blocks, table):
    rows, width = queries[0].shape
    ways, count = len(queries), len(blocks)
    arrays = []
    slots = []
    for offset in sorted(blocks):
        array, row = blocks[offset]
        if not any(array is other for other in arrays):
            arrays.append(array)
        slots.append((offset, [array is other for other in arrays].index(True), row))
    spans = 2 * count
    half = rows // 2
    length = count * rows
    tile = 8 * half
    heads = width // HD
    many = ways * half
    smem = pl.BlockSpec(memory_space=pltpu.SMEM)
    flops = 6 * many * heads * length * HD
    return pl.pallas_call(
        functools.partial(attend_body, block, ways, slots, len(arrays), spans, tile),
        out_shape=[jax.ShapeDtypeStruct((rows, width), jnp.bfloat16)] * ways,
        grid=(1,),
        in_specs=[smem]
        + [pl.BlockSpec((rows, width), lambda i: (0, 0))] * ways
        + [pl.BlockSpec(memory_space=pl.ANY)] * len(arrays),
        out_specs=[pl.BlockSpec((rows, width), lambda i: (0, 0))] * ways,
        scratch_shapes=[
            pltpu.VMEM((length, 2 * width), jnp.bfloat16),
            pltpu.VMEM((2, many, width), jnp.bfloat16),
            pltpu.VMEM((2, many, length), jnp.float32),
            pltpu.VMEM((2, many, 128), jnp.float32),
            pltpu.VMEM((2, many, 128), jnp.float32),
            pltpu.VMEM((2, many, HD), jnp.float32),
            pltpu.VMEM((2, many, 128), jnp.int32),
            pltpu.SemaphoreType.DMA((2 * count,)),
        ],
        compiler_params=pltpu.CompilerParams(vmem_limit_bytes=ATTEND_LIMIT),
        cost_estimate=pl.CostEstimate(
            flops=flops,
            bytes_accessed=4 * length * width + 4 * ways * rows * width,
            transcendentals=flops // (4 * HD),
        ),
    )(table, *queries, *arrays)


def table_body(offsets, *refs):
    table = refs[-1]
    for offset, ref in zip(offsets, refs):
        found = ref[...].astype(jnp.float32)
        for part in range(2):
            table[offset + part] = jnp.max(found[part * EXTRA // 2 : (part + 1) * EXTRA // 2]).astype(jnp.int32)


def span_table(blocks, rows):
    offsets = sorted(blocks)
    return pl.pallas_call(
        functools.partial(table_body, offsets),
        out_shape=jax.ShapeDtypeStruct((2 * len(offsets),), jnp.int32),
        grid=(1,),
        in_specs=[
            pl.BlockSpec((EXTRA, 128), functools.partial(lambda row, i: (row, 0), (blocks[i][1] + rows) // EXTRA))
            for i in offsets
        ],
        out_specs=pl.BlockSpec(memory_space=pltpu.SMEM),
        compiler_params=pltpu.CompilerParams(vmem_limit_bytes=VMEM_LIMIT),
    )(*[blocks[i][0] for i in offsets])


def assemble_body(ways, place, *refs):
    for a in range(ways):

        @pl.when(pl.program_id(0) == a)
        def _():
            refs[-1][0] = refs[ways - 1 - a][...]


def assemble(pieces, b, before, place):
    ways = len(pieces)
    rows, width = pieces[0].shape
    in_specs = [pl.BlockSpec((rows, width), lambda a, place: (0, 0))] * ways
    operands = list(pieces[::-1])
    aliases = {}
    if before is not None:
        in_specs.append(pl.BlockSpec(memory_space=pl.ANY))
        operands.append(before)
        aliases = {1 + ways: 0}
    return pl.pallas_call(
        functools.partial(assemble_body, ways),
        out_shape=jax.ShapeDtypeStruct((2, rows, ways * width), jnp.bfloat16),
        grid_spec=pltpu.PrefetchScalarGridSpec(
            num_scalar_prefetch=1,
            grid=(ways,),
            in_specs=in_specs,
            out_specs=pl.BlockSpec((1, rows, width), lambda a, place: (place[2] ^ b, 0, place[1] ^ a)),
        ),
        input_output_aliases=aliases,
        compiler_params=pltpu.CompilerParams(vmem_limit_bytes=VMEM_LIMIT),
    )(place, *operands)


def on_device(ctx_size, tp_size, hidden_in, w_q, w_k, w_v, event_pos):
    _, rows, _ = hidden_in.shape
    features = w_q.shape[1]
    ways = math.gcd(features // HD, ctx_size // 2)
    rest = ctx_size // ways
    ctx_me = lax.axis_index("ctx").astype(jnp.int32)
    tp_me = lax.axis_index("tp").astype(jnp.int32)
    core = ctx_me % 2
    place = jnp.stack([tp_me, ctx_me // rest, core, ctx_me])
    away = list(range(ways))

    def over_ctx(value, offset):
        return exchange(value, "ctx", ctx_size, offset) if offset else value

    def other_shares(own):
        shares = [own]
        bit = 1
        while bit < tp_size:
            shares += [exchange(share, "tp", tp_size, bit) for share in shares]
            bit *= 2
        return shares[1:]

    mine = lax.dynamic_index_in_dim(hidden_in, core, 0, keepdims=False)
    other = over_ctx(lax.dynamic_index_in_dim(hidden_in, 1 - core, 0, keepdims=False), 1)
    received = [other_shares(mine), other_shares(other)]

    start_k, start_v, start_q = own_products(hidden_in, other, [w_k, w_v, w_q], place, ways)

    spans = event_pos[:, 0] // (rows // 2)
    span_other = over_ctx(lax.dynamic_index_in_dim(spans, 1 - core, 0), 1)
    later = jnp.concatenate([place, lax.dynamic_index_in_dim(spans, core, 0), span_other])
    made_0 = {}
    for part in (away[: ways // 2 - 1 : -1] or away, away[: ways // 2][::-1] if ways > 1 else []):
        if part:
            made_0.update(
                rest_products(received, [0], [w_k, w_v], [start_k, start_v], later, ways, part, EXTRA)[0]
            )
    first = {a: over_ctx(made_0[a], a * rest) for a in away}
    ahead = over_ctx(made_0[0], rest // 2)
    asked = rest_products(received, [0], [w_q], [start_q], place, ways, away)
    received, asked = lax.optimization_barrier((received, asked))
    (made_1,) = rest_products(received, [1], [w_k, w_v], [start_k, start_v], place, ways, away)
    ahead_1 = over_ctx(made_1[0], rest // 2)
    for a in away:
        first[a], made_1[a] = lax.optimization_barrier((first[a], made_1[a]))

    def over_y(blocks):
        bit = rest // 2
        while bit > 1:
            for i in list(blocks):
                if i ^ bit not in blocks:
                    blocks[i ^ bit] = over_ctx(blocks[i], bit)
            bit //= 2
        return blocks

    blocks = {a * rest: first[a] for a in away}
    blocks[rest // 2] = ahead
    before = []
    for a in range(1, ways - 1):
        before.append(over_ctx(first[a], rest // 2))
        blocks[a * rest + rest // 2] = before[-1]
    received, _ = lax.optimization_barrier((received, before[-1:]))
    asked += rest_products(received, [1], [w_q], [start_q], place, ways, away)
    if ways > 1:
        value, _ = lax.optimization_barrier((first[ways - 1], (before, asked[1])))
        blocks[(ways - 1) * rest + rest // 2] = over_ctx(value, rest // 2)
    blocks = over_y(blocks)
    second = {}
    for a in away:
        value, _ = lax.optimization_barrier((made_1[a], (first[a], ahead)))
        second[a * rest + 1] = over_ctx(value, a * rest)
    queries = [{}, {}]
    for a in away:
        wait = (second[a * rest + 1], ahead_1) if a else ()
        if a == ways - 1:
            wait = (wait, [blocks[i] for i in sorted(blocks)])
        value, _ = lax.optimization_barrier((asked[0][a], wait))
        queries[0][a] = over_ctx(value, a * rest)
    for a in away:
        value, _ = lax.optimization_barrier((asked[1][a], queries[0][a]))
        queries[1][a] = over_ctx(value, a * rest)
    table = span_table({i: (array, 0) for i, array in blocks.items()}, rows)
    second[rest // 2 + 1] = ahead_1
    blocks.update(over_y(second))
    blocks = {i: (array, 0) for i, array in blocks.items()}
    out = None
    for b in range(2):
        outs = attend(b, [queries[b][a] for a in range(ways)], blocks, table)
        pieces = {a: over_ctx(outs[a], a * rest + b) for a in away}
        out = assemble([pieces[a] for a in range(ways)], b, out, place)
    return out


def solution(mesh):
    sizes = dict(mesh.shape)
    placed = (P(None, "ctx", "tp"), P(None, "tp"), P(None, "tp"), P(None, "tp"), P(None, "ctx"))
    return jax.shard_map(
        functools.partial(on_device, sizes["ctx"], sizes["tp"]),
        mesh=mesh,
        in_specs=placed,
        out_specs=P(None, "ctx", "tp"),
        check_vma=False,
    )
```

```python
import functools
import math

import jax
import jax.numpy as jnp
from jax import lax
from jax.experimental import pallas as pl
from jax.experimental.pallas import tpu as pltpu
from jax.sharding import PartitionSpec as P

HD = 128
LOG2_E = 1.4426950408889634
HIDDEN = -1e30
VMEM_LIMIT = 44 * 2**20


def exchange(value, axis, size, bit):
    return lax.ppermute(value, axis, [(i, i ^ bit) for i in range(size)])


EXTRA = 16


def own_body(weights, place, mine_ref, other_ref, *refs):
    flat_ref = refs[-1]
    rows = other_ref.shape[0]

    @pl.when(pl.program_id(0) == 0)
    def _():
        flat_ref[:rows] = mine_ref[0]
        flat_ref[rows:] = other_ref[...]

    for weight_ref, out_ref in zip(refs[:weights], refs[weights:-1]):
        result = jnp.dot(flat_ref[...], weight_ref[...], preferred_element_type=jnp.float32)
        out_ref[...] = result.reshape(2, rows, -1)


def own_products(hidden_in, other, weights, place, ways):
    rows, feats = other.shape
    features = weights[0].shape[1]
    width = features // ways
    return pl.pallas_call(
        functools.partial(own_body, len(weights)),
        out_shape=[jax.ShapeDtypeStruct((2, rows, features), jnp.float32)] * len(weights),
        grid_spec=pltpu.PrefetchScalarGridSpec(
            num_scalar_prefetch=1,
            grid=(ways,),
            in_specs=[
                pl.BlockSpec((1, rows, feats), lambda g, place: (place[2], 0, 0)),
                pl.BlockSpec((rows, feats), lambda g, place: (0, 0)),
            ]
            + [pl.BlockSpec((feats, width), lambda g, place: (place[0], g))] * len(weights),
            out_specs=[pl.BlockSpec((2, rows, width), lambda g, place: (0, 0, g))] * len(weights),
            scratch_shapes=[pltpu.VMEM((2 * rows, feats), jnp.bfloat16)],
        ),
        compiler_params=pltpu.CompilerParams(vmem_limit_bytes=VMEM_LIMIT),
        cost_estimate=pl.CostEstimate(
            flops=4 * rows * feats * features * len(weights),
            bytes_accessed=2 * feats * features * len(weights),
            transcendentals=0,
        ),
    )(place, hidden_in, other, *weights)


def rest_body(shares, weights, chunks, away, extra, place, *refs):
    inputs = refs[: shares * chunks]
    refs = refs[shares * chunks :]
    weight_refs, refs = refs[: weights * shares], refs[weights * shares :]
    start_refs, refs = refs[:weights], refs[weights:]
    out_refs, flats = refs[: chunks * len(away)], refs[chunks * len(away) :]
    rows, width = out_refs[0].shape
    rows -= extra
    width //= weights
    step = pl.program_id(0)
    if chunks > 1:

        @pl.when(step == 0)
        def _():
            for share in range(shares):
                for c in range(chunks):
                    flats[share][c * rows : (c + 1) * rows] = inputs[c * shares + share][...]

    else:
        flats = inputs
    made = []
    for n in range(weights):
        total = start_refs[n][...].reshape(chunks * rows, width)
        for share in range(shares):
            total += jnp.dot(
                flats[share][...], weight_refs[n * shares + share][...], preferred_element_type=jnp.float32
            )
        made.append(total.astype(jnp.bfloat16))
    for index in range(len(away)):

        @pl.when(step == index)
        def _():
            for c in range(chunks):
                for n in range(weights):
                    out_refs[c * len(away) + index][:rows, n * width : (n + 1) * width] = made[n][
                        c * rows : (c + 1) * rows
                    ]
            if extra:
                line = lax.broadcasted_iota(jnp.int32, (extra, weights * width), 0)
                spans = jnp.where(line < extra // 2, place[4], place[5]).astype(jnp.float32)
                out_refs[index][rows:] = spans.astype(jnp.bfloat16)


def rest_products(received, chosen, weights, starts, place, ways, away, extra=0):
    shares = len(received[0])
    rows, feats = received[0][0].shape
    width = weights[0].shape[1] // ways
    chunks = len(chosen)
    top = away[0]
    stride = away[1] - top if len(away) > 1 else 0

    def weight_map(share, i, place):
        return (place[0] ^ (share + 1), place[1] ^ (top + stride * i))

    in_specs = [pl.BlockSpec((rows, feats), lambda i, place: (0, 0))] * (shares * chunks)
    for _ in weights:
        for share in range(shares):
            in_specs.append(pl.BlockSpec((feats, width), functools.partial(weight_map, share)))
    in_specs += [
        pl.BlockSpec((chunks, rows, width), lambda i, place: (chosen[0] // chunks, 0, place[1] ^ (top + stride * i)))
    ] * len(weights)
    columns = width * len(weights)
    scratch = [pltpu.VMEM((chunks * rows, feats), jnp.bfloat16)] * (shares if chunks > 1 else 0)
    outs = pl.pallas_call(
        functools.partial(rest_body, shares, len(weights), chunks, away, extra),
        out_shape=[jax.ShapeDtypeStruct((rows + extra, columns), jnp.bfloat16)] * (chunks * len(away)),
        grid_spec=pltpu.PrefetchScalarGridSpec(
            num_scalar_prefetch=1,
            grid=(len(away),),
            in_specs=in_specs,
            out_specs=[pl.BlockSpec((rows + extra, columns), lambda i, place: (0, 0))] * (chunks * len(away)),
            scratch_shapes=scratch,
        ),
        compiler_params=pltpu.CompilerParams(vmem_limit_bytes=VMEM_LIMIT),
        cost_estimate=pl.CostEstimate(
            flops=2 * chunks * rows * feats * shares * columns * len(away),
            bytes_accessed=2 * feats * shares * columns * len(away),
            transcendentals=0,
        ),
    )(
        place,
        *[share for c in chosen for share in received[c]],
        *[weight for weight in weights for _ in range(shares)],
        *starts,
    )
    return [dict(zip(away, outs[c * len(away) : (c + 1) * len(away)])) for c in range(chunks)]


def attend_body(block, ways, slots, arrays, spans, tile, table, *refs):
    count = len(slots)
    query_refs = refs[:ways]
    block_refs = refs[ways : ways + arrays]
    out_refs = refs[ways + arrays : 2 * ways + arrays]
    ordered, asked, scores, highest, sums, total, position = refs[2 * ways + arrays :]
    rows, width = out_refs[0].shape
    half = rows // 2
    heads = width // HD
    rest = count // ways

    for slot, (offset, array, row) in enumerate(slots):
        low = table[offset]
        for part, span in ((0, low), (1, spans - 1 - low)):
            ordered[pl.ds(pl.multiple_of(span * half, 16), half)] = block_refs[array][
                row + part * half : row + (part + 1) * half
            ]

    from_lane = lax.broadcasted_iota(jnp.int32, (half, 128), 0) - lax.broadcasted_iota(
        jnp.int32, (half, 128), 1
    )
    for a in range(ways):
        low = table[a * rest + block]
        here = slice(a * half, (a + 1) * half)
        for part, span in ((0, low), (1, spans - 1 - low)):
            asked[part, here] = query_refs[a][part * half : (part + 1) * half]
            position[part, here] = from_lane + span * half

    slope = LOG2_E / math.sqrt(HD)
    middle = spans * half // 2

    def starts(part):
        return range(0, middle * (part + 1), tile)

    def visible(unit, slot, column):
        piece = scores[slot, :, column : column + 128]
        if column < middle * unit[0]:
            return piece
        return jnp.where(position[unit[0]] >= column, piece, HIDDEN)

    def score_tile(unit, slot, start):
        part, h = unit
        scores[slot, :, start : start + tile] = lax.dot_general(
            asked[part, :, h * HD : (h + 1) * HD],
            ordered[start : start + tile, h * HD : (h + 1) * HD],
            (((1,), (1,)), ((), ())),
            preferred_element_type=jnp.float32,
        )
        top = None if start == 0 else highest[slot]
        for column in range(start, start + tile, 128):
            piece = visible(unit, slot, column)
            top = piece if top is None else jnp.maximum(top, piece)
        highest[slot] = top

    def value_tile(unit, slot, start):
        part, h = unit
        top = highest[slot]
        added = None if start == 0 else sums[slot]
        weights = []
        for column in range(start, start + tile, 128):
            piece = jnp.exp2((visible(unit, slot, column) - top) * slope)
            added = piece if added is None else added + piece
            weights.append(piece.astype(jnp.bfloat16))
        sums[slot] = added
        product = jnp.dot(
            jnp.concatenate(weights, axis=1),
            ordered[start : start + tile, width + h * HD : width + (h + 1) * HD],
            preferred_element_type=jnp.float32,
        )
        if start == 0:
            total[slot] = product
        else:
            total[slot] += product

    units = [(0, 0)] + [(1, h) for h in range(heads)] + [(0, h) for h in range(1, heads)]
    for n in range(len(units) + 1):
        todo = []
        if n < len(units):
            todo.append([functools.partial(score_tile, units[n], n % 2, start) for start in starts(units[n][0])])
        if n > 0:
            slot = (n - 1) % 2
            highest[slot] = jnp.broadcast_to(jnp.max(highest[slot], axis=1, keepdims=True), highest.shape[1:])
            todo.append([functools.partial(value_tile, units[n - 1], slot, start) for start in starts(units[n - 1][0])])
        for index in range(max(len(steps) for steps in todo)):
            for steps in todo:
                if index < len(steps):
                    steps[index]()
        if n > 0:
            part, h = units[n - 1]
            result = total[slot] / jnp.sum(sums[slot], axis=1, keepdims=True)
            for a in range(ways):
                out_refs[a][part * half : (part + 1) * half, h * HD : (h + 1) * HD] = result[
                    a * half : (a + 1) * half
                ].astype(jnp.bfloat16)


def attend(block, queries, blocks, table):
    rows, width = queries[0].shape
    ways, count = len(queries), len(blocks)
    arrays = []
    slots = []
    for offset in sorted(blocks):
        array, row = blocks[offset]
        if not any(array is other for other in arrays):
            arrays.append(array)
        slots.append((offset, [array is other for other in arrays].index(True), row))
    spans = 2 * count
    half = rows // 2
    length = count * rows
    tile = 8 * half
    heads = width // HD
    many = ways * half
    smem = pl.BlockSpec(memory_space=pltpu.SMEM)
    flops = 6 * many * heads * length * HD
    return pl.pallas_call(
        functools.partial(attend_body, block, ways, slots, len(arrays), spans, tile),
        out_shape=[jax.ShapeDtypeStruct((rows, width), jnp.bfloat16)] * ways,
        grid=(1,),
        in_specs=[smem]
        + [pl.BlockSpec((rows, width), lambda i: (0, 0))] * ways
        + [pl.BlockSpec(array.shape, lambda i: (0, 0)) for array in arrays],
        out_specs=[pl.BlockSpec((rows, width), lambda i: (0, 0))] * ways,
        scratch_shapes=[
            pltpu.VMEM((length, 2 * width), jnp.bfloat16),
            pltpu.VMEM((2, many, width), jnp.bfloat16),
            pltpu.VMEM((2, many, length), jnp.float32),
            pltpu.VMEM((2, many, 128), jnp.float32),
            pltpu.VMEM((2, many, 128), jnp.float32),
            pltpu.VMEM((2, many, HD), jnp.float32),
            pltpu.VMEM((2, many, 128), jnp.int32),
        ],
        compiler_params=pltpu.CompilerParams(vmem_limit_bytes=VMEM_LIMIT),
        cost_estimate=pl.CostEstimate(
            flops=flops,
            bytes_accessed=4 * length * width + 4 * ways * rows * width,
            transcendentals=flops // (4 * HD),
        ),
    )(table, *queries, *arrays)


def table_body(offsets, *refs):
    table = refs[-1]
    for offset, ref in zip(offsets, refs):
        found = ref[...].astype(jnp.float32)
        for part in range(2):
            table[offset + part] = jnp.max(found[part * EXTRA // 2 : (part + 1) * EXTRA // 2]).astype(jnp.int32)


def span_table(blocks, rows):
    offsets = sorted(blocks)
    return pl.pallas_call(
        functools.partial(table_body, offsets),
        out_shape=jax.ShapeDtypeStruct((2 * len(offsets),), jnp.int32),
        grid=(1,),
        in_specs=[
            pl.BlockSpec((EXTRA, 128), functools.partial(lambda row, i: (row, 0), (blocks[i][1] + rows) // EXTRA))
            for i in offsets
        ],
        out_specs=pl.BlockSpec(memory_space=pltpu.SMEM),
        compiler_params=pltpu.CompilerParams(vmem_limit_bytes=VMEM_LIMIT),
    )(*[blocks[i][0] for i in offsets])


def assemble_body(ways, place, *refs):
    for a in range(ways):

        @pl.when(pl.program_id(0) == a)
        def _():
            refs[-1][0] = refs[ways - 1 - a][...]


def assemble(pieces, b, before, place):
    ways = len(pieces)
    rows, width = pieces[0].shape
    in_specs = [pl.BlockSpec((rows, width), lambda a, place: (0, 0))] * ways
    operands = list(pieces[::-1])
    aliases = {}
    if before is not None:
        in_specs.append(pl.BlockSpec(memory_space=pl.ANY))
        operands.append(before)
        aliases = {1 + ways: 0}
    return pl.pallas_call(
        functools.partial(assemble_body, ways),
        out_shape=jax.ShapeDtypeStruct((2, rows, ways * width), jnp.bfloat16),
        grid_spec=pltpu.PrefetchScalarGridSpec(
            num_scalar_prefetch=1,
            grid=(ways,),
            in_specs=in_specs,
            out_specs=pl.BlockSpec((1, rows, width), lambda a, place: (place[2] ^ b, 0, place[1] ^ a)),
        ),
        input_output_aliases=aliases,
        compiler_params=pltpu.CompilerParams(vmem_limit_bytes=VMEM_LIMIT),
    )(place, *operands)


def on_device(ctx_size, tp_size, hidden_in, w_q, w_k, w_v, event_pos):
    _, rows, _ = hidden_in.shape
    features = w_q.shape[1]
    ways = math.gcd(features // HD, ctx_size // 2)
    rest = ctx_size // ways
    ctx_me = lax.axis_index("ctx").astype(jnp.int32)
    tp_me = lax.axis_index("tp").astype(jnp.int32)
    core = ctx_me % 2
    place = jnp.stack([tp_me, ctx_me // rest, core, ctx_me])
    away = list(range(ways))

    def over_ctx(value, offset):
        return exchange(value, "ctx", ctx_size, offset) if offset else value

    def other_shares(own):
        shares = [own]
        bit = 1
        while bit < tp_size:
            shares += [exchange(share, "tp", tp_size, bit) for share in shares]
            bit *= 2
        return shares[1:]

    mine = lax.dynamic_index_in_dim(hidden_in, core, 0, keepdims=False)
    other = over_ctx(lax.dynamic_index_in_dim(hidden_in, 1 - core, 0, keepdims=False), 1)
    received = [other_shares(mine), other_shares(other)]

    start_k, start_v, start_q = own_products(hidden_in, other, [w_k, w_v, w_q], place, ways)

    spans = event_pos[:, 0] // (rows // 2)
    span_other = over_ctx(lax.dynamic_index_in_dim(spans, 1 - core, 0), 1)
    later = jnp.concatenate([place, lax.dynamic_index_in_dim(spans, core, 0), span_other])
    made_0 = {}
    for part in (away[: ways // 2 - 1 : -1] or away, away[: ways // 2][::-1] if ways > 1 else []):
        if part:
            made_0.update(
                rest_products(received, [0], [w_k, w_v], [start_k, start_v], later, ways, part, EXTRA)[0]
            )
    first = {a: over_ctx(made_0[a], a * rest) for a in away}
    ahead = over_ctx(made_0[0], rest // 2)
    asked = rest_products(received, [0], [w_q], [start_q], place, ways, away)
    received, asked = lax.optimization_barrier((received, asked))
    (made_1,) = rest_products(received, [1], [w_k, w_v], [start_k, start_v], place, ways, away)
    ahead_1 = over_ctx(made_1[0], rest // 2)
    for a in away:
        first[a], made_1[a] = lax.optimization_barrier((first[a], made_1[a]))
    received, ahead_1 = lax.optimization_barrier((received, ahead_1))
    asked += rest_products(received, [1], [w_q], [start_q], place, ways, away)

    def over_y(blocks):
        bit = rest // 2
        while bit > 1:
            for i in list(blocks):
                if i ^ bit not in blocks:
                    blocks[i ^ bit] = over_ctx(blocks[i], bit)
            bit //= 2
        return blocks

    blocks = {a * rest: first[a] for a in away}
    blocks[rest // 2] = ahead
    before = []
    for a in range(1, ways):
        value = lax.optimization_barrier((first[a], before))[0] if a == ways - 1 else first[a]
        before.append(over_ctx(value, rest // 2))
        blocks[a * rest + rest // 2] = before[-1]
    blocks = over_y(blocks)
    second = {}
    for a in away:
        value, _ = lax.optimization_barrier((made_1[a], (first[a], ahead)))
        second[a * rest + 1] = over_ctx(value, a * rest)
    queries = [{}, {}]
    for a in away:
        wait = (second[a * rest + 1], ahead_1) if a else ()
        if a == ways - 1:
            wait = (wait, [blocks[i] for i in sorted(blocks)])
        value, _ = lax.optimization_barrier((asked[0][a], wait))
        queries[0][a] = over_ctx(value, a * rest)
    for a in away:
        value, _ = lax.optimization_barrier((asked[1][a], queries[0][a]))
        queries[1][a] = over_ctx(value, a * rest)
    table = span_table({i: (array, 0) for i, array in blocks.items()}, rows)
    second[rest // 2 + 1] = ahead_1
    blocks.update(over_y(second))
    blocks = {i: (array, 0) for i, array in blocks.items()}
    out = None
    for b in range(2):
        outs = attend(b, [queries[b][a] for a in range(ways)], blocks, table)
        pieces = {a: over_ctx(outs[a], a * rest + b) for a in away}
        out = assemble([pieces[a] for a in range(ways)], b, out, place)
    return out


def solution(mesh):
    sizes = dict(mesh.shape)
    placed = (P(None, "ctx", "tp"), P(None, "tp"), P(None, "tp"), P(None, "tp"), P(None, "ctx"))
    return jax.shard_map(
        functools.partial(on_device, sizes["ctx"], sizes["tp"]),
        mesh=mesh,
        in_specs=placed,
        out_specs=P(None, "ctx", "tp"),
        check_vma=False,
    )
```
